256 devices in a mesh: dp: 8 (over z), seq: 32 (over y, x, core).
Axes of the slice: x: 4, y: 4, z: 8, core: 2. Of those that a mesh axis runs over, the one named last changes fastest.
Arguments:
- projected: bfloat16 [8, 4096, 6144], P('dp', 'seq'), may hold values from -6 to 6
- conv_weight: float32 [4, 6144], replicated, may hold values from -3 to 3
- initial_memory: float32 [16, 128, 128], replicated, may hold values from -3 to 3
- log_forget: float32 [8, 16, 4096], P('dp', None, 'seq'), as said below
- log_momentum: float32 [8, 16, 4096], P('dp', None, 'seq'), as said below
- learn_rate: float32 [8, 16, 4096], P('dp', None, 'seq'), as said below
- cotangent: bfloat16 [8, 4096, 2048], P('dp', 'seq'), may hold values from -6 to 6
Outputs:
- output: bfloat16 [8, 4096, 2048], P('dp', 'seq')
- projected_grad: bfloat16 [8, 4096, 6144], P('dp', 'seq')
- conv_grad: float32 [4, 6144], replicated
- memory_grad: float32 [16, 128, 128], P(None, 'seq')
The draws below stay inside these ranges and needn't reach their ends.
Inputs may be any that keep to these rules, and one draw needn't show every extreme that they name: `log_forget`: never positive. `log_momentum`: never positive. `learn_rate`: positive.
All inputs are finite; a program needn't handle non-finite values.
Results may differ from the reference program's by a relative error of at most 0.0056.
Values may be sent and summed in bfloat16 or wider, within the bound.
No kernel may reach another device: no remote copies, remote signals or barrier semaphores. Data moves between devices by JAX's collectives and lax.ppermute only.
A program may use at most 256 MiB of HBM per device.

```python
import jax
import jax.numpy as jnp
from jax import lax

H = 16
DK = 128
KW = 4
TOK_DEV = 128
HD = 2048
TOKENS = 4096
BATCH = 8


def decay_spans(key, exponent):
    first_key, second_key = jax.random.split(key)
    reach = 2.0 * TOKENS / 32.0
    forget_draw = jax.random.uniform(first_key, (BATCH, H, 1), dtype=jnp.float32)
    moment_draw = jax.random.uniform(second_key, (BATCH, H, 1), dtype=jnp.float32)
    forget_span = 32.0 * reach ** forget_draw ** exponent
    moment_span = 32.0 * reach ** moment_draw ** exponent
    return (forget_span, moment_span)


def device_factor(key):
    block_count = TOKENS // TOK_DEV
    factor = jnp.exp(jax.random.uniform(key, (BATCH, H, block_count), dtype=jnp.float32, minval=-0.7, maxval=0.7))
    return jnp.repeat(factor, TOK_DEV, axis=2)


def token_factor(key):
    return jnp.exp(jax.random.uniform(key, (BATCH, H, TOKENS), dtype=jnp.float32, minval=-0.7, maxval=0.7))


def draw_log_forget(key, part):
    exponent = 1.0 / 3.0
    forget_span, moment_span = decay_spans(key, exponent)
    key = jax.random.fold_in(key, 11)
    token_key, block_key, place_key, loss_key = jax.random.split(key, 4)
    update_speed = token_factor(token_key) * device_factor(block_key) / forget_span
    places = jax.random.randint(place_key, (BATCH, H, 4), 0, TOKENS)
    objective_scores = jnp.log(jax.random.uniform(loss_key, (BATCH, H, 4), dtype=jnp.float32, minval=0.5, maxval=0.8))
    positions = jnp.arange(TOKENS)
    agreement_tally = positions[None, None, None, :] == places[:, :, :, None]
    shard_bunches = jnp.sum(jnp.where(agreement_tally, objective_scores[:, :, :, None], 0.0), axis=2)
    return -update_speed + shard_bunches


def draw_log_momentum(key, part):
    exponent = 1.0 / 3.0
    forget_span, moment_span = decay_spans(key, exponent)
    key = jax.random.fold_in(key, 12)
    token_key, block_key = jax.random.split(key)
    return -(token_factor(token_key) * device_factor(block_key) / moment_span)


def draw_learn_rate(key, part):
    exponent = 1.0 / 3.0
    forget_span, moment_span = decay_spans(key, exponent)
    key = jax.random.fold_in(key, 13)
    return 16.0 / (moment_span * jnp.sqrt(forget_span)) * token_factor(key)


def steps_of(own_key, shape, cuts, low, high):
    def one(axis_at, blocks):
        draws = jax.random.uniform(jax.random.fold_in(jax.random.fold_in(own_key, 6), axis_at), (blocks,), jnp.float32, low / len(cuts), high / len(cuts))
        return jnp.repeat(jnp.exp(draws), shape[axis_at] // blocks).reshape((-1,) + (1,) * (len(shape) - axis_at - 1))

    loudness = one(*cuts[0])
    for cut in cuts[1:]:
        loudness = loudness * one(*cut)
    return loudness


def noise(stream_key, extent, deviation, limit, cuts=(), held_as=jnp.bfloat16):
    factor_of = steps_of(stream_key, extent, cuts, -0.22, 0.18) if cuts else 1.0
    entries = jax.random.normal(stream_key, extent, jnp.float32) * deviation * factor_of
    return jnp.minimum(jnp.maximum(entries, -limit), limit).astype(held_as)


def setup_inputs(seed: int = 0) -> dict:
    key_of = jax.random.split(jax.random.key(seed), 8)
    projected = noise(key_of[0], (BATCH, TOKENS, 3 * HD), 1.0, 6.0, ((0, 8), (1, 32)))
    conv_weight = noise(key_of[1], (KW, 3 * HD), KW ** -0.5, 3.0, (), jnp.float32)
    initial_memory = noise(key_of[2], (H, DK, DK), 0.5, 3.0, (), jnp.float32)
    log_forget = draw_log_forget(jax.random.fold_in(key_of[7], 71), 0)
    log_momentum = draw_log_momentum(jax.random.fold_in(key_of[7], 71), 0)
    learn_rate = draw_learn_rate(jax.random.fold_in(key_of[7], 71), 0)
    cotangent = noise(key_of[6], (BATCH, TOKENS, HD), 1.0, 6.0, ((0, 8), (1, 32)))
    return {"projected": projected, "conv_weight": conv_weight, "initial_memory": initial_memory, "log_forget": log_forget, "log_momentum": log_momentum, "learn_rate": learn_rate, "cotangent": cotangent}


def features(extended, weights):
    kernel_width = weights.shape[0]
    length = extended.shape[0] - kernel_width + 1
    convolved = weights[0] * extended[0:length]
    for offset in range(1, kernel_width):
        convolved = convolved + weights[offset] * extended[offset:offset + length]
    active = jax.nn.silu(convolved)
    group_width = active.shape[1] // 3
    head_count = group_width // DK

    def normalize(section):
        shaped = section.reshape(length, head_count, DK)
        return shaped * lax.rsqrt(lax.optimization_barrier(jnp.sum(shaped * shaped, axis=2, keepdims=True)) + 1e-06)
    probe_vectors = normalize(active[:, :group_width]).astype(jnp.bfloat16)
    memory_keys = normalize(active[:, group_width:2 * group_width]).astype(jnp.bfloat16)
    values = active[:, 2 * group_width:].reshape(length, head_count, DK).astype(jnp.bfloat16)
    return (probe_vectors, memory_keys, values)

def tables(forget, momentum):
    cum_forget = jnp.cumsum(forget, axis=1)
    cum_moment = jnp.cumsum(momentum, axis=1)
    positions = jnp.arange(forget.shape[1])
    causal = (positions[:, None] >= positions[None, :]).astype(jnp.float32)

    def decay_map(running):
        differences = running[:, :, None] - running[:, None, :]
        return jnp.exp(jnp.minimum(differences, 0.0)) * causal
    forget_map = decay_map(cum_forget)
    moment_map = decay_map(cum_moment)
    coupling = jnp.einsum('htr,hrs->hts', forget_map, moment_map, precision=lax.Precision.HIGHEST)
    start_forget = jnp.exp(cum_forget)
    start_moment = jnp.exp(cum_moment)
    carry_moment = jnp.einsum('htr,hr->ht', forget_map, start_moment, precision=lax.Precision.HIGHEST)
    return (coupling, moment_map[:, -1, :], start_forget, start_moment, carry_moment)

def memory_core(probe_vectors, memory_keys, values, memory_in, moment_in, decay_tables, rates):
    coupling, moment_tail, start_forget, start_moment, carry_moment = decay_tables
    highest = lax.Precision.HIGHEST
    query_f = probe_vectors.astype(jnp.float32)
    weighted = memory_keys.astype(jnp.float32) * jnp.transpose(rates)[:, :, None]
    value_f = values.astype(jnp.float32)
    scores = jnp.einsum('thd,shd->hts', query_f, weighted, precision=highest)
    inside = jnp.einsum('hts,she->the', scores * coupling, value_f, precision=highest)
    from_memory = jnp.einsum('thd,hde->the', query_f, memory_in, precision=highest)
    from_moment = jnp.einsum('thd,hde->the', query_f, moment_in, precision=highest)
    readout = inside + jnp.transpose(start_forget)[:, :, None] * from_memory + jnp.transpose(carry_moment)[:, :, None] * from_moment
    memory_local = jnp.einsum('shd,she->hde', weighted * jnp.transpose(coupling[:, -1, :])[:, :, None], value_f, precision=highest)
    moment_local = jnp.einsum('shd,she->hde', weighted * jnp.transpose(moment_tail)[:, :, None], value_f, precision=highest)
    memory_out = start_forget[:, -1][:, None, None] * memory_in + carry_moment[:, -1][:, None, None] * moment_in + memory_local
    moment_out = start_moment[:, -1][:, None, None] * moment_in + moment_local
    return (readout, memory_out, moment_out)

def one_sequence(projected_f, weights, memory_start, forget, momentum, rates):
    padded = jnp.concatenate([jnp.zeros((KW - 1, projected_f.shape[1]), jnp.float32), projected_f], axis=0)
    block_count = TOKENS // TOK_DEV

    def advance(carry, index):
        memory_in, moment_in = carry
        start = (index * TOK_DEV).astype(jnp.int32)
        extended = lax.dynamic_slice_in_dim(padded, start, TOK_DEV + KW - 1, 0)
        forget_part = lax.dynamic_slice_in_dim(forget, start, TOK_DEV, 1)
        moment_part = lax.dynamic_slice_in_dim(momentum, start, TOK_DEV, 1)
        rate_part = lax.dynamic_slice_in_dim(rates, start, TOK_DEV, 1)
        probe_vectors, memory_keys, values = features(extended, weights)
        decay_tables = tables(forget_part, moment_part)
        readout, memory_out, moment_out = memory_core(probe_vectors, memory_keys, values, memory_in, moment_in, decay_tables, rate_part)
        return ((memory_out, moment_out), readout.reshape(TOK_DEV, -1))
    entering_carry = (memory_start, jnp.zeros_like(memory_start))
    finals, readouts = lax.scan(advance, entering_carry, jnp.arange(block_count, dtype=jnp.int32))
    return readouts.reshape(TOKENS, -1)

def reference(projected, conv_weight, initial_memory, log_forget, log_momentum, learn_rate, cotangent):

    def per_sequence(items):
        rows_in, forget, momentum, rates, upstream = items

        def forward(projected_f, weights, memory_start):
            return one_sequence(projected_f, weights, memory_start, forget, momentum, rates)
        readout, pullback = jax.vjp(forward, rows_in.astype(jnp.float32), conv_weight, initial_memory)
        rows_grad, weight_grad, initial_gradient = pullback(upstream.astype(jnp.float32))
        return (readout.astype(jnp.bfloat16), rows_grad.astype(jnp.bfloat16), weight_grad, initial_gradient)
    results = lax.map(per_sequence, (projected, log_forget, log_momentum, learn_rate, cotangent))
    return (results[0], results[1], lax.optimization_barrier(jnp.sum(results[2], axis=0)), lax.optimization_barrier(jnp.sum(results[3], axis=0)))
```

```python
import functools

import jax
import jax.numpy as jnp
from jax import lax
from jax.experimental import pallas as pl
from jax.experimental.pallas import tpu as pltpu
from jax.sharding import PartitionSpec as P

DK = 128
BF = jnp.bfloat16
F32 = jnp.float32
PARAMS = pltpu.CompilerParams(vmem_limit_bytes=60 * 1024 * 1024)
SHARED = pltpu.CompilerParams(vmem_limit_bytes=32 * 1024 * 1024)
CHIPS = 16
HALF = 8
EXTRA = 16
PIECE = 4 * 64 + EXTRA


def dot(a, b, contract):
    return lax.dot_general(a, b, ((contract[:1], contract[1:]), ((), ())), preferred_element_type=F32)


def to_column(row, eye):
    return jnp.sum(jnp.where(eye, row, 0.0), axis=1, keepdims=True)


def tables_kernel(forget_ref, momentum_ref, rate_ref, coupling_ref, column_ref, coef_ref):
    heads, tokens = forget_ref.shape
    rows = lax.broadcasted_iota(jnp.int32, (tokens, tokens), 0)
    lanes = lax.broadcasted_iota(jnp.int32, (tokens, tokens), 1)
    eye = rows == lanes
    causal = rows >= lanes
    upper = (rows <= lanes).astype(F32)
    exact = functools.partial(
        lax.dot_general,
        dimension_numbers=(((1,), (0,)), ((), ())),
        precision=lax.Precision.HIGHEST,
        preferred_element_type=F32,
    )
    cum_forget = exact(forget_ref[...], upper)
    cum_moment = exact(momentum_ref[...], upper)
    narrow = lax.broadcasted_iota(jnp.int32, (tokens, 8), 1)
    last = tokens - 1
    for h in range(heads):
        forget_row = cum_forget[h : h + 1, :]
        moment_row = cum_moment[h : h + 1, :]
        rate_row = rate_ref[h : h + 1, :]
        forget_col = to_column(forget_row, eye)
        moment_col = to_column(moment_row, eye)
        rate_col = to_column(rate_row, eye)
        forget_map = jnp.where(causal, jnp.exp(jnp.minimum(forget_col - forget_row, 0.0)), 0.0)
        moment_map = jnp.where(causal, jnp.exp(jnp.minimum(moment_col - moment_row, 0.0)), 0.0)
        coupling = dot(forget_map.astype(BF), moment_map.astype(BF), (1, 0))
        carry = coupling[:, 0:1] * jnp.exp(moment_row[:, 0:1])
        rated = coupling * rate_row
        coupling_ref[h] = rated
        memory_col = to_column(rated[last : last + 1, :], eye)
        tail_col = rate_col * jnp.exp(jnp.minimum(moment_row[:, last:] - moment_col, 0.0))
        quad = jnp.where(
            narrow % 4 == 0,
            memory_col,
            jnp.where(narrow % 4 == 1, tail_col, jnp.where(narrow % 4 == 2, jnp.exp(forget_col), carry)),
        )
        if h % 2 == 0:
            first_quad = quad
        else:
            column_ref[h // 2] = jnp.where(narrow < 4, first_quad, quad)
        spread = functools.partial(jnp.broadcast_to, shape=(1, tokens))
        coef_ref[h : h + 1, :] = spread(jnp.exp(forget_row[:, last:]))
        coef_ref[heads + h : heads + h + 1, :] = spread(carry[last : last + 1, :])
        coef_ref[2 * heads + h : 2 * heads + h + 1, :] = spread(jnp.exp(moment_row[:, last:]))


def extend(ext_ref, slot, halo, own):
    cols = slice(slot * DK, (slot + 1) * DK)
    ext_ref[0:8, cols] = halo
    ext_ref[8 : 8 + own.shape[0], cols] = own.astype(F32)


def convolve(ext_ref, slot, weights, tokens):
    cols = slice(slot * DK, (slot + 1) * DK)
    total = weights[0:1] * ext_ref[5 : 5 + tokens, cols]
    for tap in range(1, 4):
        total = total + weights[tap : tap + 1] * ext_ref[5 + tap : 5 + tap + tokens, cols]
    return total


def element_kernel(
    base_ref, q_ref, k_ref, v_ref, u_ref, halo_ref, weight_ref, column_ref, element_ref, ext_ref
):
    tokens, width = q_ref.shape
    section = halo_ref.shape[1] // 3
    block = base_ref[0] + pl.program_id(0)
    for side in range(width // DK):
        cols = slice(side * DK, (side + 1) * DK)
        made = []
        for part, ref in enumerate((q_ref, k_ref, v_ref)):
            at = pl.ds(pl.multiple_of(part * section + block * width + side * DK, DK), DK)
            slot = side * 3 + part
            extend(ext_ref, slot, halo_ref[:, at], ref[:, cols])
            conv = convolve(ext_ref, slot, weight_ref[:, at], tokens)
            active = conv * (0.5 + 0.5 * jnp.tanh(0.5 * conv))
            if part < 2:
                active = active * lax.rsqrt(
                    jnp.sum(active * active, axis=1, keepdims=True) + 1e-06
                )
            made.append(active.astype(BF))
        query, key, value = made
        column = column_ref[0, :, 4 * side : 4 * side + 4]
        query = query.astype(F32)
        key = key.astype(F32)
        left = jnp.concatenate(
            [(key * column[:, 0:1]).astype(BF), (key * column[:, 1:2]).astype(BF)], axis=1
        )
        element_ref[side, 0 : 2 * DK] = dot(left, value, (0, 0)).astype(BF)
        left = jnp.concatenate(
            [(query * column[:, 2:3]).astype(BF), (query * column[:, 3:4]).astype(BF)], axis=1
        )
        element_ref[side, 2 * DK : 4 * DK] = dot(left, u_ref[:, cols], (0, 0)).astype(BF)


def compose_kernel(place_ref, own_ref, other_ref, own_coef_ref, other_coef_ref, out_ref):
    core = place_ref[0]
    first_core = core == 0
    heads = own_coef_ref.shape[0] // 3
    for j in range(own_ref.shape[0]):
        head = core * HALF + pl.program_id(0) * own_ref.shape[0] + j

        def coef(which):
            mine = own_coef_ref[pl.ds(which * heads + head, 1), :]
            theirs = other_coef_ref[pl.ds(which * heads + head, 1), :]
            return jnp.where(first_core, mine, theirs), jnp.where(first_core, theirs, mine)

        def matrix(which):
            at = slice(which * DK, (which + 1) * DK)
            mine = own_ref[j, at].astype(F32)
            theirs = other_ref[j, at].astype(F32)
            return jnp.where(first_core, mine, theirs), jnp.where(first_core, theirs, mine)

        forget_a, forget_b = coef(0)
        carry_a, carry_b = coef(1)
        moment_a, moment_b = coef(2)
        memory_a, memory_b = matrix(0)
        state_a, state_b = matrix(1)
        recall_a, recall_b = matrix(2)
        direct_a, direct_b = matrix(3)
        joined = (
            forget_b * memory_a + carry_b * state_a + memory_b,
            moment_b * state_a + state_b,
            forget_a * recall_b + recall_a,
            carry_a * recall_b + moment_a * direct_b + direct_a,
        )
        scalars = []
        for value in (
            forget_a * forget_b,
            forget_b * carry_a + carry_b * moment_a,
            moment_a * moment_b,
        ):
            for term in range(3):
                kept = value.astype(BF).astype(F32)
                scalars.append(kept)
                value = value - kept
        scalars.append(jnp.zeros((EXTRA - len(scalars), DK), F32))
        tail = jnp.concatenate(scalars, axis=0).astype(BF)
        for half in range(2):
            for which, full in enumerate(joined):
                out_ref[2 * j + half, which * 64 : (which + 1) * 64] = full[
                    half * 64 : (half + 1) * 64
                ].astype(BF)
            out_ref[2 * j + half, 256:PIECE] = tail


def scan_kernel(got_ref, start_ref, out_ref):
    count = got_ref.shape[0]

    def coefs(c):
        rows = got_ref[c, 256:PIECE].astype(F32)
        return tuple(
            (rows[3 * i : 3 * i + 1] + rows[3 * i + 1 : 3 * i + 2]) + rows[3 * i + 2 : 3 * i + 3]
            for i in range(3)
        )

    scalars = [coefs(c) for c in range(count)]
    memory = start_ref[...]
    state = jnp.zeros_like(memory)
    for c in range(count):
        out_ref[c, 0:64] = memory.astype(BF)
        out_ref[c, 64:128] = state.astype(BF)
        forget, carry, moment = scalars[c]
        memory = forget * memory + carry * state + got_ref[c, 0:64].astype(F32)
        state = moment * state + got_ref[c, 64:128].astype(F32)
    memory = jnp.zeros_like(state)
    state = jnp.zeros_like(state)
    for c in reversed(range(count)):
        out_ref[c, 128:192] = memory.astype(BF)
        out_ref[c, 192:256] = state.astype(BF)
        forget, carry, moment = scalars[c]
        state = carry * memory + moment * state + got_ref[c, 192:256].astype(F32)
        memory = forget * memory + got_ref[c, 128:192].astype(F32)
    for c in range(count):
        rows = memory[8 * (c % 8) : 8 * (c % 8) + 8]
        high = rows.astype(BF).astype(F32)
        out_ref[c, 256:PIECE] = jnp.concatenate([high, rows - high], axis=0).astype(BF)


def spread_kernel(
    place_ref, got_ref, own_ref, other_ref, own_coef_ref, other_coef_ref, keep_ref, send_ref, start_ref
):
    core = place_ref[0]
    side = place_ref[1]
    first_core = core == 0
    heads = own_coef_ref.shape[0] // 3
    for j in range(own_ref.shape[0]):
        head = core * HALF + pl.program_id(0) * own_ref.shape[0] + j

        def coef(which):
            mine = own_coef_ref[pl.ds(which * heads + head, 1), :]
            theirs = other_coef_ref[pl.ds(which * heads + head, 1), :]
            return jnp.where(first_core, mine, theirs), jnp.where(first_core, theirs, mine)

        def local(which):
            at = slice(which * DK, (which + 1) * DK)
            mine = own_ref[j, at].astype(F32)
            theirs = other_ref[j, at].astype(F32)
            return jnp.where(first_core, mine, theirs), jnp.where(first_core, theirs, mine)

        def entering(which):
            at = slice(which * 64, (which + 1) * 64)
            return jnp.concatenate([got_ref[2 * j, at], got_ref[2 * j + 1, at]], axis=0).astype(F32)

        forget_a, forget_b = coef(0)
        carry_a, carry_b = coef(1)
        moment_a, moment_b = coef(2)
        memory, state = entering(0), entering(1)
        memory_end, state_end = entering(2), entering(3)
        one = (
            memory,
            state,
            forget_b * memory_end + local(2)[1],
            carry_b * memory_end + moment_b * state_end + local(3)[1],
        )
        two = (
            forget_a * memory + carry_a * state + local(0)[0],
            moment_a * state + local(1)[0],
            memory_end,
            state_end,
        )
        for which in range(4):
            at = slice(which * DK, (which + 1) * DK)
            keep_ref[j, at] = jnp.where(first_core, one[which], two[which]).astype(BF)
            send_ref[j, at] = jnp.where(first_core, two[which], one[which]).astype(BF)
        rows = got_ref[2 * j + side, 256:PIECE].astype(F32)
        start_ref[j] = rows[0:8] + rows[8:16]


def inner_kernel(
    q_ref, k_ref, v_ref, u_ref, halo_ref, weight_ref, coupling_ref, out_ref, read_ref, ext_ref
):
    tokens, width = q_ref.shape
    section = halo_ref.shape[1] // 3
    block = pl.program_id(0)
    for side in range(width // DK):
        cols = slice(side * DK, (side + 1) * DK)
        made, slopes, units = [], [], []
        for part, ref in enumerate((q_ref, k_ref, v_ref)):
            at = pl.ds(pl.multiple_of(part * section + block * width + side * DK, DK), DK)
            slot = side * 3 + part
            extend(ext_ref, slot, halo_ref[:, at], ref[:, cols])
            conv = convolve(ext_ref, slot, weight_ref[:, at], tokens)
            gate = 0.5 + 0.5 * jnp.tanh(0.5 * conv)
            active = conv * gate
            slope = gate * (1.0 + conv * (1.0 - gate))
            slopes.append(slope)
            if part < 2:
                scale = lax.rsqrt(jnp.sum(active * active, axis=1, keepdims=True) + 1e-06)
                active = active * scale
                slope = slope * scale
                slopes[part] = slope
                units.append(active)
            active = active.astype(BF)
            made.append(active)
            out_ref[0, part, :, cols] = active
            out_ref[0, 4 + part, :, cols] = slope.astype(BF)
            out_ref[0, 10 + part, :, cols] = ref[:, cols]
        query, key, value = made
        upstream = u_ref[:, cols]
        out_ref[0, 3, :, cols] = upstream
        coupling = coupling_ref[side]
        scores = (dot(query, key, (1, 1)) * coupling).astype(BF)
        sense = (dot(upstream, value, (1, 1)) * coupling).astype(BF)
        grads = (
            dot(sense, key, (1, 0)),
            dot(sense, query, (0, 0)),
            dot(scores, upstream, (0, 0)),
        )
        for part, grad in enumerate(grads):
            if part < 2:
                unit = units[part]
                grad = grad - unit * jnp.sum(unit * grad, axis=1, keepdims=True)
            out_ref[0, 7 + part, :, cols] = (grad * slopes[part]).astype(BF)
        read_ref[0, 0, :, cols] = query
        read_ref[0, 1, :, cols] = dot(scores, value, (1, 0)).astype(BF)


def along_rows(left, pair):
    return dot(left, pair[:DK], (1, 0)), dot(left, pair[DK:], (1, 0))


def along_lanes(left, pair):
    both = dot(left, pair, (1, 1))
    return both[:, :DK], both[:, DK:]


def sense_kernel(
    base_ref, in_ref, halo_ref, weight_ref, column_ref, state_ref, before_ref,
    conv_ref, rim_ref, tap_ref, pad_ref, ext_ref,
):
    tokens = in_ref.shape[2]
    width = in_ref.shape[3]
    section = halo_ref.shape[1] // 3
    block = base_ref[0] + pl.program_id(0)

    @pl.when(pl.program_id(0) == 0)
    def _():
        pad_ref[0:8] = jnp.zeros((8, pad_ref.shape[1]), F32)
        pad_ref[8 + tokens :] = jnp.zeros((8, pad_ref.shape[1]), F32)

    rim_ref[0] = before_ref[1]
    for side in range(width // DK):
        cols = slice(side * DK, (side + 1) * DK)
        query, key, value, upstream = (in_ref[0, i, :, cols] for i in range(4))
        column = column_ref[0, :, 4 * side : 4 * side + 4]
        memory_col, tail_col, forget_col, carry_col = (column[:, i : i + 1] for i in range(4))
        forward, adjoint = state_ref[side, : 2 * DK], state_ref[side, 2 * DK :]
        grads = []
        a, b = along_lanes(upstream, forward)
        grads.append(forget_col * a + carry_col * b)
        a, b = along_lanes(value, adjoint)
        grads.append(memory_col * a + tail_col * b)
        a, b = along_rows(key, adjoint)
        grads.append(memory_col * a + tail_col * b)
        for part in range(3):
            grad = grads[part]
            if part < 2:
                unit = (query, key)[part].astype(F32)
                grad = grad - unit * jnp.sum(unit * grad, axis=1, keepdims=True)
            grad = grad * in_ref[0, 4 + part, :, cols].astype(F32)
            grad = grad + in_ref[0, 7 + part, :, cols].astype(F32)
            conv_ref[0, part, :, cols] = grad
            slot = side * 3 + part
            there = slice(slot * DK, (slot + 1) * DK)
            pad_ref[8 : 8 + tokens, there] = grad
            at = pl.ds(pl.multiple_of(part * section + block * width + side * DK, DK), DK)
            extend(ext_ref, slot, halo_ref[:, at], in_ref[0, 10 + part, :, cols])
            rows = ext_ref[:, there]
            weights = weight_ref[:, at]
            rim = None
            for tap in range(4):
                moved = pad_ref[3 - tap : 3 - tap + 8 + tokens, there]
                slot_row = 12 * (2 * pl.program_id(0) + side) + 4 * part + tap
                tap_ref[pl.ds(slot_row, 1), :] = jnp.sum(moved * rows, axis=0, keepdims=True)
                lead = moved[0:8] * weights[tap : tap + 1]
                rim = lead if rim is None else rim + lead
            rim_ref[1, :, part * width + side * DK : part * width + (side + 1) * DK] = jnp.concatenate(
                [jnp.zeros_like(rim), rim], axis=0
            ).astype(BF)


def readout_kernel(place_ref, read_ref, column_ref, own_ref, other_ref, output_ref):
    width = read_ref.shape[3]
    owned = (pl.program_id(0) // (pl.num_programs(0) // 2)) == place_ref[0]
    for side in range(width // DK):
        cols = slice(side * DK, (side + 1) * DK)
        column = column_ref[0, :, 4 * side : 4 * side + 4]
        states = jnp.where(owned, own_ref[side], other_ref[side])
        from_memory, from_moment = along_rows(read_ref[0, 0, :, cols], states)
        readout = read_ref[0, 1, :, cols].astype(F32) + column[:, 2:3] * from_memory + column[:, 3:4] * from_moment
        output_ref[:, cols] = readout.astype(BF)


def unroll_kernel(
    place_ref, conv_own_ref, conv_other_ref, weight_ref, rim_own_ref, rim_other_ref, grad_ref, pad_ref
):
    tokens, width = conv_own_ref.shape[2:]
    section = weight_ref.shape[1] // 3
    block = pl.program_id(0)
    owned = (block // (pl.num_programs(0) // 2)) == place_ref[0]

    @pl.when(block == 0)
    def _():
        pad_ref[tokens:] = jnp.zeros((8, pad_ref.shape[1]), F32)

    for side in range(width // DK):
        cols = slice(side * DK, (side + 1) * DK)
        for part in range(3):
            at = pl.ds(pl.multiple_of(part * section + block * width + side * DK, DK), DK)
            slot = side * 3 + part
            there = slice(slot * DK, (slot + 1) * DK)
            grad = jnp.where(owned, conv_own_ref[0, part, :, cols], conv_other_ref[0, part, :, cols])
            weights = weight_ref[:, at]
            pad_ref[0:tokens, there] = grad
            total = grad * weights[3:4]
            for tap in range(3):
                total = total + pad_ref[3 - tap : 3 - tap + tokens, there] * weights[tap : tap + 1]
            near = slice(part * width + side * DK, part * width + (side + 1) * DK)
            rim = jnp.where(owned, rim_own_ref[0, :, near], rim_other_ref[0, :, near]).astype(F32)
            total = jnp.concatenate([total[: tokens - 16], total[tokens - 16 :] + rim], axis=0)
            grad_ref[:, at] = total.astype(BF)


def assemble_kernel(place_ref, own_ref, other_ref, out_ref):
    section = out_ref.shape[1] // 3
    for h in range(section // DK):
        for part in range(3):
            first = 12 * (h % HALF) + 4 * part
            rows = slice(first, first + 4)
            at = part * section + h * DK
            out_ref[:, at : at + DK] = jnp.where(
                place_ref[0] == h // HALF, own_ref[rows], other_ref[rows]
            )


def whole(*shape):
    return pl.BlockSpec(shape, lambda *_: (0,) * len(shape))


def local(projected, conv_weight, initial_memory, log_forget, log_momentum, learn_rate, cotangent):
    rows = projected[0]
    upstream = cotangent[0]
    tokens, channels = rows.shape
    heads = initial_memory.shape[0]
    width = 2 * DK
    blocks = heads * DK // width
    count = lax.axis_size("seq")
    mine = lax.axis_index("seq")
    core = mine % 2
    chip = mine // 2
    place = jnp.stack([core, chip // 8]).astype(jnp.int32)
    pairs = [(i, i ^ 1) for i in range(count)]
    groups = [[2 * c + k for c in range(count // 2)] for k in range(2)]

    rim = lax.ppermute(rows[tokens - 3 :], "seq", [(i, i + 1) for i in range(count - 1)])
    shape = jax.ShapeDtypeStruct
    coupling, columns, coefs = pl.pallas_call(
        tables_kernel,
        out_shape=(
            shape((heads, tokens, tokens), F32),
            shape((heads // 2, tokens, 8), F32),
            shape((3 * heads, DK), F32),
        ),
        compiler_params=PARAMS,
        name="tables",
    )(log_forget[0], log_momentum[0], learn_rate[0])
    halo = jnp.pad(rim.astype(F32), ((5, 0), (0, 0)))
    other_coefs = lax.ppermute(coefs, "seq", pairs)

    def elements(base):
        def block_of(part):
            return pl.BlockSpec((tokens, width), lambda i, b: (0, part * blocks + b[0] + i))

        return pl.pallas_call(
            element_kernel,
            out_shape=shape((heads // 2, 4 * DK, DK), BF),
            grid_spec=pltpu.PrefetchScalarGridSpec(
                num_scalar_prefetch=1,
                grid=(blocks // 2,),
                in_specs=[
                    block_of(0),
                    block_of(1),
                    block_of(2),
                    block_of(0),
                    whole(8, channels),
                    whole(4, channels),
                    pl.BlockSpec((1, tokens, 8), lambda i, b: (b[0] + i, 0, 0)),
                ],
                out_specs=pl.BlockSpec((2, 4 * DK, DK), lambda i, b: (i, 0, 0)),
                scratch_shapes=[pltpu.VMEM((tokens + 8, 6 * DK), F32)],
            ),
            compiler_params=PARAMS,
            name="elements",
        )(base.astype(jnp.int32).reshape(1), rows, rows, rows, upstream, halo, conv_weight, columns)

    sent = elements((1 - core) * (blocks // 2))
    other = lax.ppermute(sent, "seq", pairs)
    own = elements(core * (blocks // 2))

    by_two = pl.BlockSpec((2, 4 * DK, DK), lambda i, b: (i, 0, 0))
    pieces = pl.BlockSpec((4, PIECE, DK), lambda i, b: (i, 0, 0))
    payload = pl.pallas_call(
        compose_kernel,
        out_shape=shape((CHIPS, PIECE, DK), BF),
        grid_spec=pltpu.PrefetchScalarGridSpec(
            num_scalar_prefetch=1,
            grid=(HALF // 2,),
            in_specs=[by_two, by_two, whole(3 * heads, DK), whole(3 * heads, DK)],
            out_specs=pieces,
        ),
        compiler_params=SHARED,
        name="compose",
    )(place, own, other, coefs, other_coefs)
    payload, coupling = lax.optimization_barrier((payload, coupling))
    got = lax.all_to_all(payload, "seq", 0, 0, axis_index_groups=groups)

    def block_at(part):
        return pl.BlockSpec((tokens, width), lambda i: (0, part * blocks + i))

    inner, inside = pl.pallas_call(
        inner_kernel,
        out_shape=(
            shape((blocks, 13, tokens, width), BF),
            shape((blocks, 2, tokens, width), BF),
        ),
        grid=(blocks,),
        in_specs=[
            block_at(0),
            block_at(1),
            block_at(2),
            block_at(0),
            whole(8, channels),
            whole(4, channels),
            pl.BlockSpec((2, tokens, tokens), lambda i: (i, 0, 0)),
        ],
        out_specs=(
            pl.BlockSpec((1, 13, tokens, width), lambda i: (i, 0, 0, 0)),
            pl.BlockSpec((1, 2, tokens, width), lambda i: (i, 0, 0, 0)),
        ),
        scratch_shapes=[pltpu.VMEM((tokens + 8, 6 * DK), F32)],
        compiler_params=PARAMS,
        name="inner",
    )(rows, rows, rows, upstream, halo, conv_weight, coupling)

    start = lax.dynamic_slice_in_dim(
        initial_memory.reshape(heads * DK, DK), core * (HALF * DK) + chip * 64, 64, 0
    )
    got, inner = lax.optimization_barrier((got, inner))
    back = pl.pallas_call(
        scan_kernel,
        out_shape=shape((CHIPS, PIECE, DK), BF),
        compiler_params=SHARED,
        name="scan",
    )(got, start)
    states = lax.all_to_all(back, "seq", 0, 0, axis_index_groups=groups)

    kept, passed, start_grad = pl.pallas_call(
        spread_kernel,
        out_shape=(
            shape((HALF, 4 * DK, DK), BF),
            shape((HALF, 4 * DK, DK), BF),
            shape((HALF, 8, DK), F32),
        ),
        grid_spec=pltpu.PrefetchScalarGridSpec(
            num_scalar_prefetch=1,
            grid=(HALF // 2,),
            in_specs=[pieces, by_two, by_two, whole(3 * heads, DK), whole(3 * heads, DK)],
            out_specs=(by_two, by_two, pl.BlockSpec((2, 8, DK), lambda i, b: (i, 0, 0))),
        ),
        compiler_params=SHARED,
        name="spread",
    )(place, states, own, other, coefs, other_coefs)
    received = lax.ppermute(passed, "seq", pairs)
    other_start = lax.ppermute(start_grad, "seq", pairs)

    half_blocks = blocks // 2

    def sense(base, state, before):
        return pl.pallas_call(
            sense_kernel,
            out_shape=(
                shape((half_blocks, 3, tokens, width), F32),
                shape((2, 16, channels // 2), BF),
                shape((12 * HALF, DK), F32),
            ),
            grid_spec=pltpu.PrefetchScalarGridSpec(
                num_scalar_prefetch=1,
                grid=(half_blocks,),
                in_specs=[
                    pl.BlockSpec((1, 13, tokens, width), lambda i, b: (b[0] + i, 0, 0, 0)),
                    whole(8, channels),
                    whole(4, channels),
                    pl.BlockSpec((1, tokens, 8), lambda i, b: (b[0] + i, 0, 0)),
                    by_two,
                    pl.BlockSpec((2, 16, 3 * width), lambda i, b: (0, 0, i)),
                ],
                out_specs=(
                    pl.BlockSpec((1, 3, tokens, width), lambda i, b: (i, 0, 0, 0)),
                    pl.BlockSpec((2, 16, 3 * width), lambda i, b: (0, 0, i)),
                    whole(12 * HALF, DK),
                ),
                scratch_shapes=[
                    pltpu.VMEM((tokens + 16, 6 * DK), F32),
                    pltpu.VMEM((tokens + 8, 6 * DK), F32),
                ],
            ),
            compiler_params=PARAMS,
            name="sense",
        )(base.astype(jnp.int32).reshape(1), inner, halo, conv_weight, columns, state, before)

    rim = jnp.zeros((2, 16, channels // 2), BF)
    conv_own, rim, tap_own = sense(core * half_blocks, kept, rim)
    conv_other, rim, tap_other = sense((1 - core) * half_blocks, received, rim)

    tap_far = lax.ppermute(tap_other, "seq", pairs)

    def ordered(one, two):
        return jnp.where(core == 0, one, two), jnp.where(core == 0, two, one)

    back_one = [(i + 1, i) for i in range(count - 1)]
    rim = lax.ppermute(rim, "seq", back_one)

    def own_at(i, b):
        return jnp.clip(i - b[0] * half_blocks, 0, half_blocks - 1)

    def other_at(i, b):
        return jnp.clip(i - (1 - b[0]) * half_blocks, 0, half_blocks - 1)

    def readouts(inside):
        return pl.pallas_call(
            readout_kernel,
            out_shape=shape((tokens, heads * DK), BF),
            grid_spec=pltpu.PrefetchScalarGridSpec(
                num_scalar_prefetch=1,
                grid=(blocks,),
                in_specs=[
                    pl.BlockSpec((1, 2, tokens, width), lambda i, b: (i, 0, 0, 0)),
                    pl.BlockSpec((1, tokens, 8), lambda i, b: (i, 0, 0)),
                    pl.BlockSpec((2, 2 * DK, DK), lambda i, b: (own_at(i, b), 0, 0)),
                    pl.BlockSpec((2, 2 * DK, DK), lambda i, b: (other_at(i, b), 0, 0)),
                ],
                out_specs=pl.BlockSpec((tokens, width), lambda i, b: (0, i)),
            ),
            compiler_params=PARAMS,
            name="readout",
        )(place, inside, columns, kept, received)

    def unrolled(rim):
        return pl.pallas_call(
            unroll_kernel,
            out_shape=shape((tokens, channels), BF),
            grid_spec=pltpu.PrefetchScalarGridSpec(
                num_scalar_prefetch=1,
                grid=(blocks,),
                in_specs=[
                    pl.BlockSpec((1, 3, tokens, width), lambda i, b: (own_at(i, b), 0, 0, 0)),
                    pl.BlockSpec((1, 3, tokens, width), lambda i, b: (other_at(i, b), 0, 0, 0)),
                    whole(4, channels),
                    pl.BlockSpec((1, 16, 3 * width), lambda i, b: (1, 0, own_at(i, b))),
                    pl.BlockSpec((1, 16, 3 * width), lambda i, b: (0, 0, other_at(i, b))),
                ],
                out_specs=whole(tokens, channels),
                scratch_shapes=[pltpu.VMEM((tokens + 8, 6 * DK), F32)],
            ),
            compiler_params=PARAMS,
            name="unroll",
        )(place, conv_own, conv_other, conv_weight, rim, rim)

    start_own = lax.dynamic_slice_in_dim(start_grad, 4 * core, 4, 1)
    start_other = lax.dynamic_slice_in_dim(other_start, 4 * core, 4, 1)
    start_all = jnp.concatenate(ordered(start_own, start_other), axis=0)
    start_all = start_all.reshape(4 * heads, DK)

    def gathered_sum(value, axis, size, axis_groups, ready, beside):
        value = value.astype(BF)
        value, ready = lax.optimization_barrier((value, ready))
        spread = jnp.broadcast_to(value[None], (size, *value.shape))
        pieces = lax.all_to_all(spread, axis, 0, 0, axis_index_groups=axis_groups)
        pieces, made = lax.optimization_barrier((pieces, beside(ready)))
        return jnp.sum(pieces.astype(F32), axis=0), made

    total, output = gathered_sum(tap_own + tap_far, "seq", CHIPS, groups, inside, readouts)
    total = jnp.concatenate([total, start_all], axis=0)
    total, grad = gathered_sum(total, "dp", lax.axis_size("dp"), None, rim, unrolled)
    tap_far = lax.ppermute(total[: 12 * HALF], "seq", pairs)
    start_all = total[12 * HALF :].reshape(heads, 4, DK)

    taps = pl.pallas_call(
        assemble_kernel,
        out_shape=shape((4, channels), F32),
        grid_spec=pltpu.PrefetchScalarGridSpec(
            num_scalar_prefetch=1,
            grid=(1,),
            in_specs=[whole(12 * HALF + 4 * heads, DK), whole(12 * HALF, DK)],
            out_specs=whole(4, channels),
        ),
        compiler_params=SHARED,
        name="assemble",
    )(place, total, tap_far)

    return (output[None], grad[None], taps, start_all)


def solution(mesh):
    in_specs = (
        P("dp", "seq", None),
        P(),
        P(),
        P("dp", None, "seq"),
        P("dp", None, "seq"),
        P("dp", None, "seq"),
        P("dp", "seq", None),
    )
    out_specs = (P("dp", "seq", None), P("dp", "seq", None), P(), P(None, "seq", None))
    return jax.shard_map(local, mesh=mesh, in_specs=in_specs, out_specs=out_specs, check_vma=False)
```

```python
import functools

import jax
import jax.numpy as jnp
from jax import lax
from jax.experimental import pallas as pl
from jax.experimental.pallas import tpu as pltpu
from jax.sharding import PartitionSpec as P

DK = 128
SIDES = 8
BF = jnp.bfloat16
F32 = jnp.float32
PARAMS = pltpu.CompilerParams(vmem_limit_bytes=32 * 1024 * 1024)
SHARED = pltpu.CompilerParams(vmem_limit_bytes=32 * 1024 * 1024)
CHIPS = 16
HALF = 8
EXTRA = 16
PIECE = 4 * 64 + EXTRA


def dot(a, b, contract):
    return lax.dot_general(a, b, ((contract[:1], contract[1:]), ((), ())), preferred_element_type=F32)


def to_column(row, eye):
    return jnp.sum(jnp.where(eye, row, 0.0), axis=1, keepdims=True)


def tables_kernel(gate_ref, coupling_ref, column_ref, coef_ref):
    heads, tokens = gate_ref.shape[0] // 3, gate_ref.shape[1]
    rows = lax.broadcasted_iota(jnp.int32, (tokens, tokens), 0)
    lanes = lax.broadcasted_iota(jnp.int32, (tokens, tokens), 1)
    eye = rows == lanes
    causal = rows >= lanes
    upper = (rows <= lanes).astype(F32)
    exact = functools.partial(
        lax.dot_general,
        dimension_numbers=(((1,), (0,)), ((), ())),
        precision=lax.Precision.HIGHEST,
        preferred_element_type=F32,
    )
    cum_forget = exact(gate_ref[0:heads], upper)
    cum_moment = exact(gate_ref[heads : 2 * heads], upper)
    narrow = lax.broadcasted_iota(jnp.int32, (tokens, 4 * SIDES), 1)
    last = tokens - 1
    for h in range(heads):
        forget_row = cum_forget[h : h + 1, :]
        moment_row = cum_moment[h : h + 1, :]
        rate_row = gate_ref[2 * heads + h : 2 * heads + h + 1, :]
        forget_col = to_column(forget_row, eye)
        moment_col = to_column(moment_row, eye)
        rate_col = to_column(rate_row, eye)
        forget_map = jnp.where(causal, jnp.exp(jnp.minimum(forget_col - forget_row, 0.0)), 0.0)
        moment_map = jnp.where(causal, jnp.exp(jnp.minimum(moment_col - moment_row, 0.0)), 0.0)
        coupling = dot(forget_map.astype(BF), moment_map.astype(BF), (1, 0))
        carry = coupling[:, 0:1] * jnp.exp(moment_row[:, 0:1])
        rated = coupling * rate_row
        coupling_ref[h] = rated.astype(BF)
        memory_col = to_column(rated[last : last + 1, :], eye)
        tail_col = rate_col * jnp.exp(jnp.minimum(moment_row[:, last:] - moment_col, 0.0))
        quad = jnp.where(
            narrow % 4 == 0,
            memory_col,
            jnp.where(narrow % 4 == 1, tail_col, jnp.where(narrow % 4 == 2, jnp.exp(forget_col), carry)),
        )
        packed = quad if h % SIDES == 0 else jnp.where(narrow // 4 == h % SIDES, quad, packed)
        if h % SIDES == SIDES - 1:
            column_ref[h // SIDES] = packed
        spread = functools.partial(jnp.broadcast_to, shape=(1, tokens))
        coef_ref[h : h + 1, :] = spread(jnp.exp(forget_row[:, last:]))
        coef_ref[heads + h : heads + h + 1, :] = spread(carry[last : last + 1, :])
        coef_ref[2 * heads + h : 2 * heads + h + 1, :] = spread(jnp.exp(moment_row[:, last:]))


def extend(ext_ref, slot, halo, own):
    cols = slice(slot * DK, (slot + 1) * DK)
    ext_ref[5:8, cols] = halo.astype(F32)
    ext_ref[8 : 8 + own.shape[0], cols] = own.astype(F32)


def convolve(ext_ref, slot, weights, tokens):
    cols = slice(slot * DK, (slot + 1) * DK)
    total = weights[0:1] * ext_ref[5 : 5 + tokens, cols]
    for tap in range(1, 4):
        total = total + weights[tap : tap + 1] * ext_ref[5 + tap : 5 + tap + tokens, cols]
    return total


def first_block(mine, place_ref, blocks):
    return (place_ref[0] if mine else 1 - place_ref[0]) * (blocks // 2)


def element_kernel(
    mine, place_ref, q_ref, k_ref, v_ref, u_ref, halo_ref, weight_ref, column_ref, element_ref, ext_ref
):
    tokens, width = q_ref.shape
    section = halo_ref.shape[1] // 3
    block = first_block(mine, place_ref, section // width) + pl.program_id(0)
    for side in range(width // DK):
        cols = slice(side * DK, (side + 1) * DK)
        made = []
        for part, ref in enumerate((q_ref, k_ref, v_ref)):
            at = pl.ds(pl.multiple_of(part * section + block * width + side * DK, DK), DK)
            slot = side * 3 + part
            extend(ext_ref, slot, halo_ref[:, at], ref[:, cols])
            conv = convolve(ext_ref, slot, weight_ref[:, at], tokens)
            active = conv * (0.5 + 0.5 * jnp.tanh(0.5 * conv))
            if part < 2:
                active = active * lax.rsqrt(
                    jnp.sum(active * active, axis=1, keepdims=True) + 1e-06
                )
            made.append(active.astype(BF))
        query, key, value = made
        column = column_ref[0, :, 4 * side : 4 * side + 4]
        query = query.astype(F32)
        key = key.astype(F32)
        left = jnp.concatenate(
            [(key * column[:, 0:1]).astype(BF), (key * column[:, 1:2]).astype(BF)], axis=1
        )
        element_ref[side, 0 : 2 * DK] = dot(left, value, (0, 0)).astype(BF)
        left = jnp.concatenate(
            [(query * column[:, 2:3]).astype(BF), (query * column[:, 3:4]).astype(BF)], axis=1
        )
        element_ref[side, 2 * DK : 4 * DK] = dot(left, u_ref[:, cols], (0, 0)).astype(BF)


def compose_kernel(place_ref, own_ref, other_ref, own_coef_ref, other_coef_ref, out_ref):
    core = place_ref[0]
    first_core = core == 0
    heads = own_coef_ref.shape[0] // 3
    for j in range(own_ref.shape[0]):
        head = core * HALF + pl.program_id(0) * own_ref.shape[0] + j

        def coef(which):
            mine = own_coef_ref[pl.ds(which * heads + head, 1), :]
            theirs = other_coef_ref[pl.ds(which * heads + head, 1), :]
            return jnp.where(first_core, mine, theirs), jnp.where(first_core, theirs, mine)

        def matrix(which):
            at = slice(which * DK, (which + 1) * DK)
            mine = own_ref[j, at].astype(F32)
            theirs = other_ref[j, at].astype(F32)
            return jnp.where(first_core, mine, theirs), jnp.where(first_core, theirs, mine)

        forget_a, forget_b = coef(0)
        carry_a, carry_b = coef(1)
        moment_a, moment_b = coef(2)
        memory_a, memory_b = matrix(0)
        state_a, state_b = matrix(1)
        recall_a, recall_b = matrix(2)
        direct_a, direct_b = matrix(3)
        joined = (
            forget_b * memory_a + carry_b * state_a + memory_b,
            moment_b * state_a + state_b,
            forget_a * recall_b + recall_a,
            carry_a * recall_b + moment_a * direct_b + direct_a,
        )
        scalars = []
        for value in (
            forget_a * forget_b,
            forget_b * carry_a + carry_b * moment_a,
            moment_a * moment_b,
        ):
            for term in range(3):
                kept = value.astype(BF).astype(F32)
                scalars.append(kept)
                value = value - kept
        scalars.append(jnp.zeros((EXTRA - len(scalars), DK), F32))
        tail = jnp.concatenate(scalars, axis=0).astype(BF)
        for half in range(2):
            for which, full in enumerate(joined):
                out_ref[2 * j + half, which * 64 : (which + 1) * 64] = full[
                    half * 64 : (half + 1) * 64
                ].astype(BF)
            out_ref[2 * j + half, 256:PIECE] = tail


def scan_kernel(place_ref, got_ref, start_ref, out_ref):
    count = got_ref.shape[0]

    def coefs(c):
        rows = got_ref[c, 256:PIECE].astype(F32)
        return tuple(
            (rows[3 * i : 3 * i + 1] + rows[3 * i + 1 : 3 * i + 2]) + rows[3 * i + 2 : 3 * i + 3]
            for i in range(3)
        )

    scalars = [coefs(c) for c in range(count)]
    memory = start_ref[...]
    state = jnp.zeros_like(memory)
    for c in range(count):
        out_ref[c, 0:64] = memory.astype(BF)
        out_ref[c, 64:128] = state.astype(BF)
        forget, carry, moment = scalars[c]
        memory = forget * memory + carry * state + got_ref[c, 0:64].astype(F32)
        state = moment * state + got_ref[c, 64:128].astype(F32)
    memory = jnp.zeros_like(state)
    state = jnp.zeros_like(state)
    for c in reversed(range(count)):
        out_ref[c, 128:192] = memory.astype(BF)
        out_ref[c, 192:256] = state.astype(BF)
        forget, carry, moment = scalars[c]
        state = carry * memory + moment * state + got_ref[c, 192:256].astype(F32)
        memory = forget * memory + got_ref[c, 128:192].astype(F32)
    for c in range(count):
        rows = memory[8 * (c % 8) : 8 * (c % 8) + 8]
        high = rows.astype(BF).astype(F32)
        out_ref[c, 256:PIECE] = jnp.concatenate([high, rows - high], axis=0).astype(BF)


def spread_kernel(
    place_ref, got_ref, own_ref, other_ref, own_coef_ref, other_coef_ref, keep_ref, send_ref
):
    core = place_ref[0]
    side = place_ref[1]
    first_core = core == 0
    heads = own_coef_ref.shape[0] // 3
    for j in range(own_ref.shape[0]):
        head = core * HALF + pl.program_id(0) * own_ref.shape[0] + j

        def coef(which):
            mine = own_coef_ref[pl.ds(which * heads + head, 1), :]
            theirs = other_coef_ref[pl.ds(which * heads + head, 1), :]
            return jnp.where(first_core, mine, theirs), jnp.where(first_core, theirs, mine)

        def local(which):
            at = slice(which * DK, (which + 1) * DK)
            mine = own_ref[j, at].astype(F32)
            theirs = other_ref[j, at].astype(F32)
            return jnp.where(first_core, mine, theirs), jnp.where(first_core, theirs, mine)

        def entering(which):
            at = slice(which * 64, (which + 1) * 64)
            return jnp.concatenate([got_ref[2 * j, at], got_ref[2 * j + 1, at]], axis=0).astype(F32)

        forget_a, forget_b = coef(0)
        carry_a, carry_b = coef(1)
        moment_a, moment_b = coef(2)
        memory, state = entering(0), entering(1)
        memory_end, state_end = entering(2), entering(3)
        one = (
            memory,
            state,
            forget_b * memory_end + local(2)[1],
            carry_b * memory_end + moment_b * state_end + local(3)[1],
        )
        two = (
            forget_a * memory + carry_a * state + local(0)[0],
            moment_a * state + local(1)[0],
            memory_end,
            state_end,
        )
        for which in range(4):
            at = slice(which * DK, (which + 1) * DK)
            keep_ref[j, at] = jnp.where(first_core, one[which], two[which]).astype(BF)
            send_ref[j, at] = jnp.where(first_core, two[which], one[which]).astype(BF)
        start = got_ref[2 * j + side, 256:PIECE]
        keep_ref[j, 4 * DK :] = start
        send_ref[j, 4 * DK :] = start


def inner_kernel(
    q_ref, k_ref, v_ref, u_ref, halo_ref, weight_ref, coupling_ref, out_ref, read_ref, ext_ref
):
    tokens, width = q_ref.shape
    section = halo_ref.shape[1] // 3
    block = pl.program_id(0)
    for side in range(width // DK):
        cols = slice(side * DK, (side + 1) * DK)
        made, slopes, units = [], [], []
        for part, ref in enumerate((q_ref, k_ref, v_ref)):
            at = pl.ds(pl.multiple_of(part * section + block * width + side * DK, DK), DK)
            slot = side * 3 + part
            extend(ext_ref, slot, halo_ref[:, at], ref[:, cols])
            conv = convolve(ext_ref, slot, weight_ref[:, at], tokens)
            gate = 0.5 + 0.5 * jnp.tanh(0.5 * conv)
            active = conv * gate
            slope = gate * (1.0 + conv * (1.0 - gate))
            slopes.append(slope)
            if part < 2:
                scale = lax.rsqrt(jnp.sum(active * active, axis=1, keepdims=True) + 1e-06)
                active = active * scale
                slope = slope * scale
                slopes[part] = slope
                units.append(active)
            active = active.astype(BF)
            made.append(active)
            out_ref[0, part, :, cols] = active
            out_ref[0, 4 + part, :, cols] = slope.astype(BF)
            out_ref[0, 10 + part, :, cols] = ref[:, cols]
        query, key, value = made
        upstream = u_ref[:, cols]
        out_ref[0, 3, :, cols] = upstream
        coupling = coupling_ref[side].astype(F32)
        scores = (dot(query, key, (1, 1)) * coupling).astype(BF)
        sense = (dot(upstream, value, (1, 1)) * coupling).astype(BF)
        grads = (
            dot(sense, key, (1, 0)),
            dot(sense, query, (0, 0)),
            dot(scores, upstream, (0, 0)),
        )
        for part, grad in enumerate(grads):
            if part < 2:
                unit = units[part]
                grad = grad - unit * jnp.sum(unit * grad, axis=1, keepdims=True)
            out_ref[0, 7 + part, :, cols] = (grad * slopes[part]).astype(BF)
        read_ref[0, 0, :, cols] = query
        read_ref[0, 1, :, cols] = dot(scores, value, (1, 0)).astype(BF)


def along_rows(left, pair):
    return dot(left, pair[:DK], (1, 0)), dot(left, pair[DK:], (1, 0))


def along_lanes(left, pair):
    both = dot(left, pair, (1, 1))
    return both[:, :DK], both[:, DK:]


def sense_kernel(
    mine, place_ref, in_ref, halo_ref, weight_ref, column_ref, state_ref, *refs
):
    conv_ref, rim_ref, tap_ref, pad_ref, ext_ref = refs[-5:]
    step = pl.program_id(0)
    tokens = in_ref.shape[2]
    width = in_ref.shape[3]
    section = halo_ref.shape[1] // 3
    block = first_block(mine, place_ref, section // width) + step
    if len(refs) > 5:
        rim_ref[0] = refs[0][1]
    else:
        rim_ref[0] = jnp.zeros(rim_ref.shape[1:], BF)

    @pl.when(pl.program_id(0) == 0)
    def _():
        pad_ref[0:8] = jnp.zeros((8, pad_ref.shape[1]), F32)
        pad_ref[8 + tokens :] = jnp.zeros((8, pad_ref.shape[1]), F32)
        ext_ref[0:8] = jnp.zeros((8, ext_ref.shape[1]), F32)

    for side in range(width // DK):
        cols = slice(side * DK, (side + 1) * DK)
        query, key, value, upstream = (in_ref[0, i, :, cols] for i in range(4))
        column = column_ref[0, :, 4 * side : 4 * side + 4]
        memory_col, tail_col, forget_col, carry_col = (column[:, i : i + 1] for i in range(4))
        forward, adjoint = state_ref[side, : 2 * DK], state_ref[side, 2 * DK :]
        grads = []
        a, b = along_lanes(upstream, forward)
        grads.append(forget_col * a + carry_col * b)
        a, b = along_lanes(value, adjoint)
        grads.append(memory_col * a + tail_col * b)
        a, b = along_rows(key, adjoint)
        grads.append(memory_col * a + tail_col * b)
        for part in range(3):
            grad = grads[part]
            if part < 2:
                unit = (query, key)[part].astype(F32)
                grad = grad - unit * jnp.sum(unit * grad, axis=1, keepdims=True)
            grad = grad * in_ref[0, 4 + part, :, cols].astype(F32)
            grad = grad + in_ref[0, 7 + part, :, cols].astype(F32)
            slot = side * 3 + part
            conv_ref[0, slot] = grad.astype(BF)
            there = slice(slot * DK, (slot + 1) * DK)
            pad_ref[8 : 8 + tokens, there] = grad
            at = pl.ds(pl.multiple_of(part * section + block * width + side * DK, DK), DK)
            extend(ext_ref, slot, halo_ref[:, at], in_ref[0, 10 + part, :, cols])
            rows = ext_ref[:, there]
            weights = weight_ref[:, at]
            rim = None
            for tap in range(4):
                moved = pad_ref[3 - tap : 3 - tap + 8 + tokens, there]
                slot_row = 12 * (SIDES * pl.program_id(0) + side) + 4 * part + tap
                tap_ref[pl.ds(slot_row, 1), :] = jnp.sum(moved * rows, axis=0, keepdims=True)
                lead = moved[0:8] * weights[tap : tap + 1]
                rim = lead if rim is None else rim + lead
            rim_ref[1, :, part * width + side * DK : part * width + (side + 1) * DK] = jnp.concatenate(
                [jnp.zeros_like(rim), rim], axis=0
            ).astype(BF)


def readout_kernel(
    place_ref, read_ref, column_ref, own_ref, other_ref, own_start_ref, other_start_ref,
    output_ref, start_ref,
):
    width = read_ref.shape[3]
    owned = (pl.program_id(0) // (pl.num_programs(0) // 2)) == place_ref[0]
    for side in range(width // DK):
        cols = slice(side * DK, (side + 1) * DK)
        column = column_ref[0, :, 4 * side : 4 * side + 4]
        states = jnp.where(owned, own_ref[side], other_ref[side])
        from_memory, from_moment = along_rows(read_ref[0, 0, :, cols], states)
        readout = read_ref[0, 1, :, cols].astype(F32) + column[:, 2:3] * from_memory + column[:, 3:4] * from_moment
        output_ref[:, cols] = readout.astype(BF)
        rows = jnp.where(owned, own_start_ref[side], other_start_ref[side]).astype(F32)
        rows = rows[0:8] + rows[8:16]
        start_ref[4 * side : 4 * side + 4] = jnp.where(place_ref[0] == 0, rows[0:4], rows[4:8])


def unroll_kernel(
    place_ref, conv_own_ref, conv_other_ref, weight_ref, rim_own_ref, rim_other_ref, grad_ref, pad_ref
):
    tokens = conv_own_ref.shape[2]
    width = conv_own_ref.shape[1] // 3 * DK
    section = weight_ref.shape[1] // 3
    block = pl.program_id(0)
    owned = (block // (pl.num_programs(0) // 2)) == place_ref[0]

    @pl.when(block == 0)
    def _():
        pad_ref[tokens:] = jnp.zeros((8, pad_ref.shape[1]), F32)

    for side in range(width // DK):
        cols = slice(side * DK, (side + 1) * DK)
        for part in range(3):
            at = pl.ds(pl.multiple_of(part * section + block * width + side * DK, DK), DK)
            slot = side * 3 + part
            there = slice(slot * DK, (slot + 1) * DK)
            grad = jnp.where(owned, conv_own_ref[0, slot], conv_other_ref[0, slot]).astype(F32)
            weights = weight_ref[:, at]
            pad_ref[0:tokens, there] = grad
            total = grad * weights[3:4]
            for tap in range(3):
                total = total + pad_ref[3 - tap : 3 - tap + tokens, there] * weights[tap : tap + 1]
            near = slice(part * width + side * DK, part * width + (side + 1) * DK)
            rim = jnp.where(owned, rim_own_ref[0, :, near], rim_other_ref[0, :, near]).astype(F32)
            total = jnp.concatenate([total[: tokens - 16], total[tokens - 16 :] + rim], axis=0)
            grad_ref[:, at] = total.astype(BF)


def pack_kernel(own_ref, far_ref, out_ref):
    value = (own_ref[...] + far_ref[...]).astype(BF)
    for i in range(out_ref.shape[0]):
        out_ref[i] = value


def fold_kernel(pieces_ref, start_ref, out_ref):
    total = pieces_ref[0].astype(F32)
    for i in range(1, pieces_ref.shape[0]):
        total = total + pieces_ref[i].astype(F32)
    value = jnp.concatenate([total, start_ref[...]], axis=0).astype(BF)
    for i in range(out_ref.shape[0]):
        out_ref[i] = value


def sum_kernel(pieces_ref, out_ref):
    total = pieces_ref[0].astype(F32)
    for i in range(1, pieces_ref.shape[0]):
        total = total + pieces_ref[i].astype(F32)
    out_ref[...] = total


def assemble_kernel(place_ref, own_ref, other_ref, out_ref, start_ref):
    section = out_ref.shape[1] // 3
    for h in range(section // DK):
        first = 12 * HALF + 4 * h
        start_ref[h] = own_ref[first : first + 4]
    for h in range(section // DK):
        for part in range(3):
            first = 12 * (h % HALF) + 4 * part
            rows = slice(first, first + 4)
            at = part * section + h * DK
            out_ref[:, at : at + DK] = jnp.where(
                place_ref[0] == h // HALF, own_ref[rows], other_ref[rows]
            )


def whole(*shape):
    return pl.BlockSpec(shape, lambda *_: (0,) * len(shape))


def local(projected, conv_weight, initial_memory, log_forget, log_momentum, learn_rate, cotangent):
    rows = projected[0]
    upstream = cotangent[0]
    tokens, channels = rows.shape
    heads = initial_memory.shape[0]
    width = SIDES * DK
    blocks = heads * DK // width
    count = lax.axis_size("seq")
    mine = lax.axis_index("seq")
    core = mine % 2
    chip = mine // 2
    place = jnp.stack([core, chip // 8, core * (HALF * DK // 64) + chip]).astype(jnp.int32)
    gates = jnp.concatenate([log_forget[0], log_momentum[0], learn_rate[0]], axis=0)
    gates, place = lax.optimization_barrier((gates, place))
    pairs = [(i, i ^ 1) for i in range(count)]
    groups = [[2 * c + k for c in range(count // 2)] for k in range(2)]

    rim = lax.ppermute(rows[tokens - 3 :], "seq", [(i, i + 1) for i in range(count - 1)])
    shape = jax.ShapeDtypeStruct
    coupling, columns, coefs = pl.pallas_call(
        tables_kernel,
        out_shape=(
            shape((heads, tokens, tokens), BF),
            shape((heads // SIDES, tokens, 4 * SIDES), F32),
            shape((3 * heads, DK), F32),
        ),
        compiler_params=PARAMS,
        name="tables",
        cost_estimate=pl.CostEstimate(flops=4000000000, transcendentals=0, bytes_accessed=14400000),
    )(gates)
    other_coefs = lax.ppermute(coefs, "seq", pairs)

    def elements(mine):
        def first(b):
            return first_block(mine, b, blocks)

        def block_of(part):
            return pl.BlockSpec((tokens, width), lambda i, b: (0, part * blocks + first(b) + i))

        return pl.pallas_call(
            functools.partial(element_kernel, mine),
            out_shape=shape((heads // 2, 4 * DK, DK), BF),
            grid_spec=pltpu.PrefetchScalarGridSpec(
                num_scalar_prefetch=1,
                grid=(blocks // 2,),
                in_specs=[
                    block_of(0),
                    block_of(1),
                    block_of(2),
                    block_of(0),
                    whole(3, channels),
                    whole(4, channels),
                    pl.BlockSpec((1, tokens, 4 * SIDES), lambda i, b: (first(b) + i, 0, 0)),
                ],
                out_specs=pl.BlockSpec((SIDES, 4 * DK, DK), lambda i, b: (i, 0, 0)),
                scratch_shapes=[pltpu.VMEM((tokens + 8, 3 * SIDES * DK), F32)],
            ),
            compiler_params=PARAMS,
            name="elements",
            cost_estimate=pl.CostEstimate(flops=3400000000, transcendentals=0, bytes_accessed=12240000),
        )(place, rows, rows, rows, upstream, rim, conv_weight, columns)

    sent = elements(False)
    other = lax.ppermute(sent, "seq", pairs)
    own = elements(True)

    by_two = pl.BlockSpec((2, 4 * DK, DK), lambda i, b: (i, 0, 0))
    pieces = pl.BlockSpec((4, PIECE, DK), lambda i, b: (i, 0, 0))
    payload = pl.pallas_call(
        compose_kernel,
        out_shape=shape((CHIPS, PIECE, DK), BF),
        grid_spec=pltpu.PrefetchScalarGridSpec(
            num_scalar_prefetch=1,
            grid=(HALF // 2,),
            in_specs=[by_two, by_two, whole(3 * heads, DK), whole(3 * heads, DK)],
            out_specs=pieces,
        ),
        compiler_params=SHARED,
        name="compose",
        cost_estimate=pl.CostEstimate(flops=1200000000, transcendentals=0, bytes_accessed=4320000),
    )(place, own, other, coefs, other_coefs)
    payload, coupling = lax.optimization_barrier((payload, coupling))
    got = lax.all_to_all(payload, "seq", 0, 0, axis_index_groups=groups)

    def block_at(part):
        return pl.BlockSpec((tokens, width), lambda i: (0, part * blocks + i))

    inner, inside = pl.pallas_call(
        inner_kernel,
        out_shape=(
            shape((blocks, 13, tokens, width), BF),
            shape((blocks, 2, tokens, width), BF),
        ),
        grid=(blocks,),
        in_specs=[
            block_at(0),
            block_at(1),
            block_at(2),
            block_at(0),
            whole(3, channels),
            whole(4, channels),
            pl.BlockSpec((SIDES, tokens, tokens), lambda i: (i, 0, 0)),
        ],
        out_specs=(
            pl.BlockSpec((1, 13, tokens, width), lambda i: (i, 0, 0, 0)),
            pl.BlockSpec((1, 2, tokens, width), lambda i: (i, 0, 0, 0)),
        ),
        scratch_shapes=[pltpu.VMEM((tokens + 8, 3 * SIDES * DK), F32)],
        compiler_params=PARAMS,
        name="inner",
        cost_estimate=pl.CostEstimate(flops=8000000000, transcendentals=0, bytes_accessed=28800000),
    )(rows, rows, rows, upstream, rim, conv_weight, coupling)

    got, inner, inside = lax.optimization_barrier((got, inner, inside))
    back = pl.pallas_call(
        scan_kernel,
        out_shape=shape((CHIPS, PIECE, DK), BF),
        grid_spec=pltpu.PrefetchScalarGridSpec(
            num_scalar_prefetch=1,
            grid=(1,),
            in_specs=[whole(CHIPS, PIECE, DK), pl.BlockSpec((64, DK), lambda i, b: (b[2], 0))],
            out_specs=whole(CHIPS, PIECE, DK),
        ),
        compiler_params=SHARED,
        name="scan",
        cost_estimate=pl.CostEstimate(flops=400000000, transcendentals=0, bytes_accessed=1440000),
    )(place, got, initial_memory.reshape(heads * DK, DK))
    states = lax.all_to_all(back, "seq", 0, 0, axis_index_groups=groups)

    kept, passed = pl.pallas_call(
        spread_kernel,
        out_shape=(
            shape((HALF, 4 * DK + EXTRA, DK), BF),
            shape((HALF, 4 * DK + EXTRA, DK), BF),
        ),
        grid_spec=pltpu.PrefetchScalarGridSpec(
            num_scalar_prefetch=1,
            grid=(HALF // 2,),
            in_specs=[pieces, by_two, by_two, whole(3 * heads, DK), whole(3 * heads, DK)],
            out_specs=(pl.BlockSpec((2, 4 * DK + EXTRA, DK), lambda i, b: (i, 0, 0)),) * 2,
        ),
        compiler_params=SHARED,
        name="spread",
        cost_estimate=pl.CostEstimate(flops=1300000000, transcendentals=0, bytes_accessed=4680000),
    )(place, states, own, other, coefs, other_coefs)
    received = lax.ppermute(passed, "seq", pairs)

    half_blocks = blocks // 2

    def sense(mine, state, *before):
        def first(b):
            return first_block(mine, b, blocks)

        return pl.pallas_call(
            functools.partial(sense_kernel, mine),
            out_shape=(
                shape((half_blocks, 3 * SIDES, tokens, DK), BF),
                shape((2, 16, channels // 2), BF),
                shape((12 * HALF, DK), F32),
            ),
            grid_spec=pltpu.PrefetchScalarGridSpec(
                num_scalar_prefetch=1,
                grid=(half_blocks,),
                in_specs=[
                    pl.BlockSpec((1, 13, tokens, width), lambda i, b: (first(b) + i, 0, 0, 0)),
                    whole(3, channels),
                    whole(4, channels),
                    pl.BlockSpec((1, tokens, 4 * SIDES), lambda i, b: (first(b) + i, 0, 0)),
                    pl.BlockSpec((SIDES, 4 * DK, DK), lambda i, b: (i, 0, 0)),
                    *[pl.BlockSpec((2, 16, 3 * width), lambda i, b: (0, 0, i)) for _ in before],
                ],
                out_specs=(
                    pl.BlockSpec((1, 3 * SIDES, tokens, DK), lambda i, b: (i, 0, 0, 0)),
                    pl.BlockSpec((2, 16, 3 * width), lambda i, b: (0, 0, i)),
                    whole(12 * HALF, DK),
                ),
                scratch_shapes=[
                    pltpu.VMEM((tokens + 16, 3 * SIDES * DK), F32),
                    pltpu.VMEM((tokens + 8, 3 * SIDES * DK), F32),
                ],
            ),
            compiler_params=PARAMS,
            name="sense",
            cost_estimate=pl.CostEstimate(flops=3000000000, transcendentals=0, bytes_accessed=10800000),
        )(place, inner, rim, conv_weight, columns, state, *before)

    conv_own, edge, tap_own = sense(True, kept)
    conv_other, edge, tap_other = sense(False, received, edge)

    tap_far = lax.ppermute(tap_other, "seq", pairs)

    def ordered(one, two):
        return jnp.where(core == 0, one, two), jnp.where(core == 0, two, one)

    back_one = [(i + 1, i) for i in range(count - 1)]
    edge = lax.ppermute(edge, "seq", back_one)

    def own_at(i, b):
        return jnp.clip(i - b[0] * half_blocks, 0, half_blocks - 1)

    def other_at(i, b):
        return jnp.clip(i - (1 - b[0]) * half_blocks, 0, half_blocks - 1)

    def readouts(inside):
        return pl.pallas_call(
            readout_kernel,
            out_shape=(shape((tokens, heads * DK), BF), shape((4 * heads, DK), F32)),
            grid_spec=pltpu.PrefetchScalarGridSpec(
                num_scalar_prefetch=1,
                grid=(blocks,),
                in_specs=[
                    pl.BlockSpec((1, 2, tokens, width), lambda i, b: (i, 0, 0, 0)),
                    pl.BlockSpec((1, tokens, 4 * SIDES), lambda i, b: (i, 0, 0)),
                    pl.BlockSpec((SIDES, 2 * DK, DK), lambda i, b: (own_at(i, b), 0, 0)),
                    pl.BlockSpec((SIDES, 2 * DK, DK), lambda i, b: (other_at(i, b), 0, 0)),
                    pl.BlockSpec((SIDES, EXTRA, DK), lambda i, b: (own_at(i, b), 4 * DK // EXTRA, 0)),
                    pl.BlockSpec((SIDES, EXTRA, DK), lambda i, b: (other_at(i, b), 4 * DK // EXTRA, 0)),
                ],
                out_specs=(
                    pl.BlockSpec((tokens, width), lambda i, b: (0, i)),
                    pl.BlockSpec((4 * SIDES, DK), lambda i, b: (i, 0)),
                ),
            ),
            compiler_params=PARAMS,
            name="readout",
            cost_estimate=pl.CostEstimate(flops=3000000000, transcendentals=0, bytes_accessed=10800000),
        )(place, inside, columns, kept, received, kept, received)

    def unrolled(rim):
        return pl.pallas_call(
            unroll_kernel,
            out_shape=shape((tokens, channels), BF),
            grid_spec=pltpu.PrefetchScalarGridSpec(
                num_scalar_prefetch=1,
                grid=(blocks,),
                in_specs=[
                    pl.BlockSpec((1, 3 * SIDES, tokens, DK), lambda i, b: (own_at(i, b), 0, 0, 0)),
                    pl.BlockSpec((1, 3 * SIDES, tokens, DK), lambda i, b: (other_at(i, b), 0, 0, 0)),
                    whole(4, channels),
                    pl.BlockSpec((1, 16, 3 * width), lambda i, b: (1, 0, own_at(i, b))),
                    pl.BlockSpec((1, 16, 3 * width), lambda i, b: (0, 0, other_at(i, b))),
                ],
                out_specs=whole(tokens, channels),
                scratch_shapes=[pltpu.VMEM((tokens + 8, 3 * SIDES * DK), F32)],
            ),
            compiler_params=PARAMS,
            name="unroll",
            cost_estimate=pl.CostEstimate(flops=4000000000, transcendentals=0, bytes_accessed=14400000),
        )(place, conv_own, conv_other, conv_weight, rim, rim)

    dp = lax.axis_size("dp")
    tap_rows = 12 * HALF
    sum_rows = tap_rows + 4 * heads
    spread_taps = pl.pallas_call(
        pack_kernel,
        out_shape=shape((CHIPS, tap_rows, DK), BF),
        compiler_params=SHARED,
        name="pack",
        cost_estimate=pl.CostEstimate(flops=800000000, transcendentals=0, bytes_accessed=2880000),
    )(tap_own, tap_far)

    spread_taps, inside = lax.optimization_barrier((spread_taps, inside))
    pieces = lax.all_to_all(spread_taps, "seq", 0, 0, axis_index_groups=groups)
    output, start_all = readouts(inside)
    pieces, output = lax.optimization_barrier((pieces, output))
    spread_sums = pl.pallas_call(
        fold_kernel,
        out_shape=shape((dp, sum_rows, DK), BF),
        compiler_params=SHARED,
        name="fold",
        cost_estimate=pl.CostEstimate(flops=800000000, transcendentals=0, bytes_accessed=2880000),
    )(pieces, start_all)
    spread_sums, edge = lax.optimization_barrier((spread_sums, edge))
    pieces = lax.all_to_all(spread_sums, "dp", 0, 0)
    grad = unrolled(edge)
    pieces, grad = lax.optimization_barrier((pieces, grad))
    total = pl.pallas_call(
        sum_kernel,
        out_shape=shape((sum_rows, DK), F32),
        compiler_params=SHARED,
        name="total",
        cost_estimate=pl.CostEstimate(flops=800000000, transcendentals=0, bytes_accessed=2880000),
    )(pieces)
    total_far = lax.ppermute(total, "seq", pairs)
    taps, start_all = pl.pallas_call(
        assemble_kernel,
        out_shape=(shape((4, channels), F32), shape((heads, 4, DK), F32)),
        grid_spec=pltpu.PrefetchScalarGridSpec(
            num_scalar_prefetch=1,
            grid=(1,),
            in_specs=[whole(sum_rows, DK)] * 2,
            out_specs=(whole(4, channels), whole(heads, 4, DK)),
        ),
        compiler_params=SHARED,
        name="assemble",
        cost_estimate=pl.CostEstimate(flops=1000000000, transcendentals=0, bytes_accessed=3600000),
    )(place, total, total_far)
    return (output[None], grad[None], taps, start_all)


def solution(mesh):
    in_specs = (
        P("dp", "seq", None),
        P(),
        P(),
        P("dp", None, "seq"),
        P("dp", None, "seq"),
        P("dp", None, "seq"),
        P("dp", "seq", None),
    )
    out_specs = (P("dp", "seq", None), P("dp", "seq", None), P(), P(None, "seq", None))
    return jax.shard_map(local, mesh=mesh, in_specs=in_specs, out_specs=out_specs, check_vma=False)
```

```python
import functools

import jax
import jax.numpy as jnp
from jax import lax
from jax.experimental import pallas as pl
from jax.experimental.pallas import tpu as pltpu
from jax.sharding import PartitionSpec as P

DK = 128
SIDES = 8
BF = jnp.bfloat16
F32 = jnp.float32
PARAMS = pltpu.CompilerParams(vmem_limit_bytes=32 * 1024 * 1024)
SHARED = pltpu.CompilerParams(vmem_limit_bytes=32 * 1024 * 1024)
CHIPS = 16
HALF = 8
EXTRA = 16
PIECE = 4 * 64 + EXTRA


def dot(a, b, contract):
    return lax.dot_general(a, b, ((contract[:1], contract[1:]), ((), ())), preferred_element_type=F32)


def to_column(row, eye):
    return jnp.sum(jnp.where(eye, row, 0.0), axis=1, keepdims=True)


def shifted(value, by, fill):
    tokens = value.shape[1]
    lane = lax.broadcasted_iota(jnp.int32, value.shape, 1)
    moved = pltpu.roll(value, by % tokens, axis=1)
    return jnp.where(lane >= by if by > 0 else lane < tokens + by, moved, fill)


def recurrence(factor, added, step):
    by = step
    while abs(by) < factor.shape[1]:
        added = added + factor * shifted(added, by, 0.0)
        factor = factor * shifted(factor, by, 1.0)
        by *= 2
    return added


def tables_kernel(gate_ref, column_ref, coef_ref, cum_ref):
    heads, tokens = gate_ref.shape[0] // 3, gate_ref.shape[1]
    rows = lax.broadcasted_iota(jnp.int32, (tokens, tokens), 0)
    lanes = lax.broadcasted_iota(jnp.int32, (tokens, tokens), 1)
    cum = lax.dot_general(
        gate_ref[0 : 2 * heads],
        (rows <= lanes).astype(F32),
        (((1,), (0,)), ((), ())),
        precision=lax.Precision.HIGHEST,
        preferred_element_type=F32,
    )
    cum_ref[...] = cum
    last = tokens - 1
    cum_forget, cum_moment = cum[:heads], cum[heads:]
    rate = gate_ref[2 * heads :]
    forget = jnp.exp(cum_forget)
    moment = jnp.exp(cum_moment)
    carry = recurrence(jnp.exp(gate_ref[0:heads]), moment, 1)
    lane = lax.broadcasted_iota(jnp.int32, (heads, tokens), 1)
    later = jnp.where(lane < last, pltpu.roll(jnp.exp(gate_ref[heads : 2 * heads]), last, axis=1), 0.0)
    memory = recurrence(later, jnp.exp(jnp.minimum(cum_forget[:, last:] - cum_forget, 0.0)), -1)
    memory = memory * rate
    tail = rate * jnp.exp(jnp.minimum(cum_moment[:, last:] - cum_moment, 0.0))
    for group in range(heads // SIDES):
        at = slice(group * SIDES, (group + 1) * SIDES)
        column_ref[group] = jnp.transpose(
            jnp.concatenate([memory[at], tail[at], forget[at], carry[at]], axis=0)
        )
    for which, value in enumerate((forget, carry, moment)):
        coef_ref[which * heads : (which + 1) * heads] = jnp.broadcast_to(value[:, last:], (heads, tokens))


def couple_kernel(gate_ref, cum_ref, coupling_ref):
    heads, tokens = gate_ref.shape[0] // 3, gate_ref.shape[1]
    rows = lax.broadcasted_iota(jnp.int32, (tokens, tokens), 0)
    lanes = lax.broadcasted_iota(jnp.int32, (tokens, tokens), 1)
    eye = rows == lanes
    causal = rows >= lanes
    for h in range(heads):
        maps = []
        for at in (h, heads + h):
            row = cum_ref[at : at + 1, :]
            decay = jnp.exp(jnp.minimum(to_column(row, eye) - row, 0.0))
            maps.append(jnp.where(causal, decay, 0.0).astype(BF))
        rated = dot(maps[0], maps[1], (1, 0)) * gate_ref[2 * heads + h : 2 * heads + h + 1, :]
        coupling_ref[h] = rated.astype(BF)


def extend(ext_ref, slot, halo, own):
    cols = slice(slot * DK, (slot + 1) * DK)
    ext_ref[0:8, cols] = halo.astype(F32)
    ext_ref[8 : 8 + own.shape[0], cols] = own.astype(F32)


def convolve(ext_ref, slot, weights, tokens):
    cols = slice(slot * DK, (slot + 1) * DK)
    total = weights[0:1] * ext_ref[5 : 5 + tokens, cols]
    for tap in range(1, 4):
        total = total + weights[tap : tap + 1] * ext_ref[5 + tap : 5 + tap + tokens, cols]
    return total


def element_kernel(
    mine, place_ref, rows_ref, u_ref, halo_ref, weight_ref, column_ref, element_ref, ext_ref
):
    tokens = rows_ref.shape[0]
    section = rows_ref.shape[1] // 3
    half = place_ref[0] if mine else 1 - place_ref[0]
    for side in range(HALF):
        made = []
        for part in range(3):
            at = pl.ds(pl.multiple_of(part * section + half * (HALF * DK) + side * DK, DK), DK)
            slot = side * 3 + part
            extend(ext_ref, slot, halo_ref[:, at], rows_ref[:, at])
            conv = convolve(ext_ref, slot, weight_ref[:, at], tokens)
            active = conv * (0.5 + 0.5 * jnp.tanh(0.5 * conv))
            if part < 2:
                active = active * lax.rsqrt(
                    jnp.sum(active * active, axis=1, keepdims=True) + 1e-06
                )
            made.append(active)
        query, key, value = made
        column = picker(column_ref, half, side)
        query = query.astype(BF).astype(F32)
        key = key.astype(BF).astype(F32)
        left = jnp.concatenate(
            [(key * column(0)).astype(BF), (key * column(1)).astype(BF)], axis=1
        )
        element_ref[side, 0 : 2 * DK] = dot(left, value.astype(BF), (0, 0)).astype(BF)
        left = jnp.concatenate(
            [(query * column(2)).astype(BF), (query * column(3)).astype(BF)], axis=1
        )
        upstream = u_ref[:, pl.ds(pl.multiple_of(half * (HALF * DK) + side * DK, DK), DK)]
        element_ref[side, 2 * DK : 4 * DK] = dot(left, upstream, (0, 0)).astype(BF)


def compose_kernel(place_ref, own_ref, other_ref, own_coef_ref, other_coef_ref, out_ref):
    core = place_ref[0]
    first_core = core == 0
    heads = own_coef_ref.shape[0] // 3
    for j in range(own_ref.shape[0]):
        head = core * HALF + pl.program_id(0) * own_ref.shape[0] + j

        def coef(which):
            mine = own_coef_ref[pl.ds(which * heads + head, 1), :]
            theirs = other_coef_ref[pl.ds(which * heads + head, 1), :]
            return jnp.where(first_core, mine, theirs), jnp.where(first_core, theirs, mine)

        def matrix(which):
            at = slice(which * DK, (which + 1) * DK)
            mine = own_ref[j, at].astype(F32)
            theirs = other_ref[j, at].astype(F32)
            return jnp.where(first_core, mine, theirs), jnp.where(first_core, theirs, mine)

        forget_a, forget_b = coef(0)
        carry_a, carry_b = coef(1)
        moment_a, moment_b = coef(2)
        memory_a, memory_b = matrix(0)
        state_a, state_b = matrix(1)
        recall_a, recall_b = matrix(2)
        direct_a, direct_b = matrix(3)
        joined = (
            forget_b * memory_a + carry_b * state_a + memory_b,
            moment_b * state_a + state_b,
            forget_a * recall_b + recall_a,
            carry_a * recall_b + moment_a * direct_b + direct_a,
        )
        scalars = []
        for value in (
            forget_a * forget_b,
            forget_b * carry_a + carry_b * moment_a,
            moment_a * moment_b,
        ):
            for term in range(3):
                kept = value.astype(BF).astype(F32)
                scalars.append(kept)
                value = value - kept
        scalars.append(jnp.zeros((EXTRA - len(scalars), DK), F32))
        tail = jnp.concatenate(scalars, axis=0).astype(BF)
        for half in range(2):
            for which, full in enumerate(joined):
                out_ref[2 * j + half, which * 64 : (which + 1) * 64] = full[
                    half * 64 : (half + 1) * 64
                ].astype(BF)
            out_ref[2 * j + half, 256:PIECE] = tail


def scan_kernel(place_ref, got_ref, start_ref, out_ref):
    count = got_ref.shape[0]

    def coefs(c):
        rows = got_ref[c, 256:PIECE].astype(F32)
        return tuple(
            (rows[3 * i : 3 * i + 1] + rows[3 * i + 1 : 3 * i + 2]) + rows[3 * i + 2 : 3 * i + 3]
            for i in range(3)
        )

    scalars = [coefs(c) for c in range(count)]
    memory = start_ref[pl.ds(pl.multiple_of(place_ref[2] * 64, 64), 64), :]
    state = jnp.zeros_like(memory)
    for c in range(count):
        out_ref[c, 0:64] = memory.astype(BF)
        out_ref[c, 64:128] = state.astype(BF)
        forget, carry, moment = scalars[c]
        memory = forget * memory + carry * state + got_ref[c, 0:64].astype(F32)
        state = moment * state + got_ref[c, 64:128].astype(F32)
    memory = jnp.zeros_like(state)
    state = jnp.zeros_like(state)
    for c in reversed(range(count)):
        out_ref[c, 128:192] = memory.astype(BF)
        out_ref[c, 192:256] = state.astype(BF)
        forget, carry, moment = scalars[c]
        state = carry * memory + moment * state + got_ref[c, 192:256].astype(F32)
        memory = forget * memory + got_ref[c, 128:192].astype(F32)
    for c in range(count):
        rows = memory[8 * (c % 8) : 8 * (c % 8) + 8]
        high = rows.astype(BF).astype(F32)
        out_ref[c, 256:PIECE] = jnp.concatenate([high, rows - high], axis=0).astype(BF)


def spread_kernel(
    place_ref, got_ref, own_ref, other_ref, own_coef_ref, other_coef_ref, keep_ref, send_ref
):
    core = place_ref[0]
    side = place_ref[1]
    first_core = core == 0
    heads = own_coef_ref.shape[0] // 3
    for j in range(own_ref.shape[0]):
        head = core * HALF + pl.program_id(0) * own_ref.shape[0] + j

        def coef(which):
            mine = own_coef_ref[pl.ds(which * heads + head, 1), :]
            theirs = other_coef_ref[pl.ds(which * heads + head, 1), :]
            return jnp.where(first_core, mine, theirs), jnp.where(first_core, theirs, mine)

        def local(which):
            at = slice(which * DK, (which + 1) * DK)
            mine = own_ref[j, at].astype(F32)
            theirs = other_ref[j, at].astype(F32)
            return jnp.where(first_core, mine, theirs), jnp.where(first_core, theirs, mine)

        def entering(which):
            at = slice(which * 64, (which + 1) * 64)
            return jnp.concatenate([got_ref[2 * j, at], got_ref[2 * j + 1, at]], axis=0).astype(F32)

        forget_a, forget_b = coef(0)
        carry_a, carry_b = coef(1)
        moment_a, moment_b = coef(2)
        memory, state = entering(0), entering(1)
        memory_end, state_end = entering(2), entering(3)
        one = (
            memory,
            state,
            forget_b * memory_end + local(2)[1],
            carry_b * memory_end + moment_b * state_end + local(3)[1],
        )
        two = (
            forget_a * memory + carry_a * state + local(0)[0],
            moment_a * state + local(1)[0],
            memory_end,
            state_end,
        )
        for which in range(4):
            at = slice(which * DK, (which + 1) * DK)
            keep_ref[j, at] = jnp.where(first_core, one[which], two[which]).astype(BF)
            send_ref[j, at] = jnp.where(first_core, two[which], one[which]).astype(BF)
        start = got_ref[2 * j + side, 256:PIECE]
        keep_ref[j, 4 * DK :] = start
        send_ref[j, 4 * DK :] = start


def inner_kernel(
    q_ref, k_ref, v_ref, u_ref, halo_ref, weight_ref, coupling_ref, out_ref, read_ref, ext_ref
):
    tokens, width = q_ref.shape
    section = halo_ref.shape[1] // 3
    block = pl.program_id(0)
    for side in range(width // DK):
        cols = slice(side * DK, (side + 1) * DK)
        made, slopes, units = [], [], []
        for part, ref in enumerate((q_ref, k_ref, v_ref)):
            at = pl.ds(pl.multiple_of(part * section + block * width + side * DK, DK), DK)
            slot = side * 3 + part
            extend(ext_ref, slot, halo_ref[:, at], ref[:, cols])
            conv = convolve(ext_ref, slot, weight_ref[:, at], tokens)
            gate = 0.5 + 0.5 * jnp.tanh(0.5 * conv)
            active = conv * gate
            slope = gate * (1.0 + conv * (1.0 - gate))
            slopes.append(slope)
            if part < 2:
                scale = lax.rsqrt(jnp.sum(active * active, axis=1, keepdims=True) + 1e-06)
                active = active * scale
                slope = slope * scale
                slopes[part] = slope
                units.append(active)
            active = active.astype(BF)
            made.append(active)
            out_ref[0, part, :, cols] = active
            out_ref[0, 4 + part, :, cols] = slope.astype(BF)
            out_ref[0, 10 + part, :, cols] = ref[:, cols]
        query, key, value = made
        upstream = u_ref[:, cols]
        out_ref[0, 3, :, cols] = upstream
        coupling = coupling_ref[side].astype(F32)
        scores = (dot(query, key, (1, 1)) * coupling).astype(BF)
        sense = (dot(upstream, value, (1, 1)) * coupling).astype(BF)
        grads = (
            dot(sense, key, (1, 0)),
            dot(sense, query, (0, 0)),
            dot(scores, upstream, (0, 0)),
        )
        for part, grad in enumerate(grads):
            if part < 2:
                unit = units[part]
                grad = grad - unit * jnp.sum(unit * grad, axis=1, keepdims=True)
            out_ref[0, 7 + part, :, cols] = (grad * slopes[part]).astype(BF)
        read_ref[0, 0, :, cols] = query
        read_ref[0, 1, :, cols] = dot(scores, value, (1, 0)).astype(BF)


def picker(column_ref, group, side):
    values = column_ref[group]
    return lambda which: values[:, which * SIDES + side : which * SIDES + side + 1]


def along_rows(left, pair):
    return dot(left, pair[:DK], (1, 0)), dot(left, pair[DK:], (1, 0))


def along_lanes(left, pair):
    both = dot(left, pair, (1, 1))
    return both[:, :DK], both[:, DK:]


def sense_kernel(
    mine, place_ref, in_ref, halo_ref, weight_ref, column_ref, state_ref, *refs
):
    conv_ref, rim_ref, tap_ref, start_ref, pad_ref, ext_ref = refs[-6:]
    tokens = in_ref.shape[2]
    width = in_ref.shape[3]
    section = halo_ref.shape[1] // 3
    block = place_ref[0] if mine else 1 - place_ref[0]
    if len(refs) > 6:
        rim_ref[0] = refs[0][1]
    else:
        rim_ref[0] = jnp.zeros(rim_ref.shape[1:], BF)

    pad_ref[0:8] = jnp.zeros((8, pad_ref.shape[1]), F32)
    pad_ref[8 + tokens :] = jnp.zeros((8, pad_ref.shape[1]), F32)

    for side in range(width // DK):
        cols = slice(side * DK, (side + 1) * DK)
        query, key, value, upstream = (in_ref[block, i, :, cols] for i in range(4))
        column = picker(column_ref, block, side)
        memory_col, tail_col, forget_col, carry_col = (column(i) for i in range(4))
        start = state_ref[side, 4 * DK :].astype(F32)
        start = start[0:8] + start[8:16]
        start_ref[4 * side : 4 * side + 4] = jnp.where(place_ref[0] == 0, start[0:4], start[4:8])
        forward, adjoint = state_ref[side, : 2 * DK], state_ref[side, 2 * DK : 4 * DK]
        grads = []
        a, b = along_lanes(upstream, forward)
        grads.append(forget_col * a + carry_col * b)
        a, b = along_lanes(value, adjoint)
        grads.append(memory_col * a + tail_col * b)
        a, b = along_rows(key, adjoint)
        grads.append(memory_col * a + tail_col * b)
        for part in range(3):
            grad = grads[part]
            if part < 2:
                unit = (query, key)[part].astype(F32)
                grad = grad - unit * jnp.sum(unit * grad, axis=1, keepdims=True)
            grad = grad * in_ref[block, 4 + part, :, cols].astype(F32)
            grad = grad + in_ref[block, 7 + part, :, cols].astype(F32)
            slot = side * 3 + part
            conv_ref[0, slot] = grad.astype(BF)
            there = slice(slot * DK, (slot + 1) * DK)
            pad_ref[8 : 8 + tokens, there] = grad
            at = pl.ds(pl.multiple_of(part * section + block * width + side * DK, DK), DK)
            extend(ext_ref, slot, halo_ref[:, at], in_ref[block, 10 + part, :, cols])
            rows = ext_ref[:, there]
            weights = weight_ref[:, at]
            rim = None
            for tap in range(4):
                moved = pad_ref[3 - tap : 3 - tap + 8 + tokens, there]
                slot_row = 12 * side + 4 * part + tap
                tap_ref[slot_row : slot_row + 1, :] = jnp.sum(moved * rows, axis=0, keepdims=True)
                lead = moved[0:8] * weights[tap : tap + 1]
                rim = lead if rim is None else rim + lead
            rim_ref[1, :, part * width + side * DK : part * width + (side + 1) * DK] = jnp.concatenate(
                [jnp.zeros_like(rim), rim], axis=0
            ).astype(BF)


def readout_kernel(
    place_ref, read_ref, column_ref, own_ref, other_ref, output_ref
):
    width = read_ref.shape[3]
    owned = (pl.program_id(0) // (pl.num_programs(0) // 2)) == place_ref[0]
    for side in range(width // DK):
        cols = slice(side * DK, (side + 1) * DK)
        column = picker(column_ref, 0, side)
        states = jnp.where(owned, own_ref[side], other_ref[side])
        from_memory, from_moment = along_rows(read_ref[0, 0, :, cols], states)
        readout = read_ref[0, 1, :, cols].astype(F32) + column(2) * from_memory + column(3) * from_moment
        output_ref[:, cols] = readout.astype(BF)


def unroll_kernel(
    place_ref, conv_own_ref, conv_other_ref, weight_ref, rim_own_ref, rim_other_ref, grad_ref, pad_ref
):
    tokens = conv_own_ref.shape[2]
    width = conv_own_ref.shape[1] // 3 * DK
    section = weight_ref.shape[1] // 3
    block = pl.program_id(0)
    owned = (block // (pl.num_programs(0) // 2)) == place_ref[0]

    @pl.when(block == 0)
    def _():
        pad_ref[tokens:] = jnp.zeros((8, pad_ref.shape[1]), F32)

    for side in range(width // DK):
        cols = slice(side * DK, (side + 1) * DK)
        for part in range(3):
            at = pl.ds(pl.multiple_of(part * section + block * width + side * DK, DK), DK)
            slot = side * 3 + part
            there = slice(slot * DK, (slot + 1) * DK)
            grad = jnp.where(owned, conv_own_ref[0, slot], conv_other_ref[0, slot]).astype(F32)
            weights = weight_ref[:, at]
            pad_ref[0:tokens, there] = grad
            total = grad * weights[3:4]
            for tap in range(3):
                total = total + pad_ref[3 - tap : 3 - tap + tokens, there] * weights[tap : tap + 1]
            near = slice(part * width + side * DK, part * width + (side + 1) * DK)
            rim = jnp.where(owned, rim_own_ref[0, :, near], rim_other_ref[0, :, near]).astype(F32)
            total = jnp.concatenate([total[: tokens - 16], total[tokens - 16 :] + rim], axis=0)
            grad_ref[:, at] = total.astype(BF)


def pack_kernel(own_ref, far_ref, out_ref):
    value = (own_ref[...] + far_ref[...]).astype(BF)
    for i in range(out_ref.shape[0]):
        out_ref[i] = value


def fold_kernel(place_ref, pieces_ref, own_ref, other_ref, out_ref):
    total = pieces_ref[0].astype(F32)
    for i in range(1, pieces_ref.shape[0]):
        total = total + pieces_ref[i].astype(F32)
    own, other = own_ref[...], other_ref[...]
    first_core = place_ref[0] == 0
    value = jnp.concatenate(
        [total, jnp.where(first_core, own, other), jnp.where(first_core, other, own)], axis=0
    ).astype(BF)
    for i in range(out_ref.shape[0]):
        out_ref[i] = value


def sum_kernel(pieces_ref, out_ref):
    total = pieces_ref[0].astype(F32)
    for i in range(1, pieces_ref.shape[0]):
        total = total + pieces_ref[i].astype(F32)
    out_ref[...] = total


def assemble_kernel(place_ref, own_ref, other_ref, out_ref, start_ref):
    section = out_ref.shape[1] // 3
    for h in range(section // DK):
        first = 12 * HALF + 4 * h
        start_ref[h] = own_ref[first : first + 4]
    for h in range(section // DK):
        for part in range(3):
            first = 12 * (h % HALF) + 4 * part
            rows = slice(first, first + 4)
            at = part * section + h * DK
            out_ref[:, at : at + DK] = jnp.where(
                place_ref[0] == h // HALF, own_ref[rows], other_ref[rows]
            )


RESIDENT = pl.BlockSpec(memory_space=pltpu.VMEM)


def whole(*shape):
    return pl.BlockSpec(shape, lambda *_: (0,) * len(shape))


def local(projected, conv_weight, initial_memory, log_forget, log_momentum, learn_rate, cotangent):
    rows = projected[0]
    upstream = cotangent[0]
    tokens, channels = rows.shape
    heads = initial_memory.shape[0]
    width = SIDES * DK
    blocks = heads * DK // width
    count = lax.axis_size("seq")
    mine = lax.axis_index("seq")
    core = mine % 2
    chip = mine // 2
    place = jnp.stack([core, chip // 8, core * (HALF * DK // 64) + chip]).astype(jnp.int32)
    gates = jnp.concatenate([log_forget[0], log_momentum[0], learn_rate[0]], axis=0)
    gates, place = lax.optimization_barrier((gates, place))
    pairs = [(i, i ^ 1) for i in range(count)]
    groups = [[2 * c + k for c in range(count // 2)] for k in range(2)]

    rim = lax.ppermute(rows[tokens - 8 :], "seq", [(i, i + 1) for i in range(count - 1)])
    shape = jax.ShapeDtypeStruct
    columns, coefs, cums = pl.pallas_call(
        tables_kernel,
        out_shape=(
            shape((heads // SIDES, tokens, 4 * SIDES), F32),
            shape((3 * heads, DK), F32),
            shape((2 * heads, tokens), F32),
        ),
        compiler_params=SHARED,
        name="tables",
        cost_estimate=pl.CostEstimate(flops=2000000000, transcendentals=0, bytes_accessed=7200000),
    )(gates)
    other_coefs = lax.ppermute(coefs, "seq", pairs)

    def elements(mine):
        return pl.pallas_call(
            functools.partial(element_kernel, mine),
            out_shape=shape((HALF, 4 * DK, DK), BF),
            grid_spec=pltpu.PrefetchScalarGridSpec(
                num_scalar_prefetch=1,
                grid=(1,),
                in_specs=[RESIDENT] * 5,
                out_specs=RESIDENT,
                scratch_shapes=[pltpu.VMEM((tokens + 8, 3 * HALF * DK), F32)],
            ),
            compiler_params=SHARED,
            name="elements",
            cost_estimate=pl.CostEstimate(flops=3400000000, transcendentals=0, bytes_accessed=12240000),
        )(place, rows, upstream, rim, conv_weight, columns)

    sent = elements(False)
    other = lax.ppermute(sent, "seq", pairs)
    own = elements(True)

    payload = pl.pallas_call(
        compose_kernel,
        out_shape=shape((CHIPS, PIECE, DK), BF),
        grid_spec=pltpu.PrefetchScalarGridSpec(
            num_scalar_prefetch=1,
            grid=(1,),
            in_specs=[RESIDENT] * 4,
            out_specs=RESIDENT,
        ),
        compiler_params=SHARED,
        name="compose",
        cost_estimate=pl.CostEstimate(flops=1200000000, transcendentals=0, bytes_accessed=4320000),
    )(place, own, other, coefs, other_coefs)
    payload, cums = lax.optimization_barrier((payload, cums))
    got = lax.all_to_all(payload, "seq", 0, 0, axis_index_groups=groups)

    coupling = pl.pallas_call(
        couple_kernel,
        out_shape=shape((heads, tokens, tokens), BF),
        compiler_params=SHARED,
        name="couple",
        cost_estimate=pl.CostEstimate(flops=3500000000, transcendentals=0, bytes_accessed=12600000),
    )(gates, cums)

    def block_at(part):
        return pl.BlockSpec((tokens, width), lambda i: (0, part * blocks + i))

    inner, inside = pl.pallas_call(
        inner_kernel,
        out_shape=(
            shape((blocks, 13, tokens, width), BF),
            shape((blocks, 2, tokens, width), BF),
        ),
        grid=(blocks,),
        in_specs=[
            block_at(0),
            block_at(1),
            block_at(2),
            block_at(0),
            whole(8, channels),
            whole(4, channels),
            pl.BlockSpec((SIDES, tokens, tokens), lambda i: (i, 0, 0)),
        ],
        out_specs=(
            pl.BlockSpec((1, 13, tokens, width), lambda i: (i, 0, 0, 0)),
            pl.BlockSpec((1, 2, tokens, width), lambda i: (i, 0, 0, 0)),
        ),
        scratch_shapes=[pltpu.VMEM((tokens + 8, 3 * SIDES * DK), F32)],
        compiler_params=PARAMS,
        name="inner",
        cost_estimate=pl.CostEstimate(flops=8000000000, transcendentals=0, bytes_accessed=28800000),
    )(rows, rows, rows, upstream, rim, conv_weight, coupling)

    got, inner, inside = lax.optimization_barrier((got, inner, inside))
    back = pl.pallas_call(
        scan_kernel,
        out_shape=shape((CHIPS, PIECE, DK), BF),
        grid_spec=pltpu.PrefetchScalarGridSpec(
            num_scalar_prefetch=1,
            grid=(1,),
            in_specs=[RESIDENT] * 2,
            out_specs=RESIDENT,
        ),
        compiler_params=SHARED,
        name="scan",
        cost_estimate=pl.CostEstimate(flops=400000000, transcendentals=0, bytes_accessed=1440000),
    )(place, got, initial_memory.reshape(heads * DK, DK))
    states = lax.all_to_all(back, "seq", 0, 0, axis_index_groups=groups)

    kept, passed = pl.pallas_call(
        spread_kernel,
        out_shape=(
            shape((HALF, 4 * DK + EXTRA, DK), BF),
            shape((HALF, 4 * DK + EXTRA, DK), BF),
        ),
        grid_spec=pltpu.PrefetchScalarGridSpec(
            num_scalar_prefetch=1,
            grid=(1,),
            in_specs=[RESIDENT] * 5,
            out_specs=(RESIDENT,) * 2,
        ),
        compiler_params=SHARED,
        name="spread",
        cost_estimate=pl.CostEstimate(flops=1300000000, transcendentals=0, bytes_accessed=4680000),
    )(place, states, own, other, coefs, other_coefs)
    received = lax.ppermute(passed, "seq", pairs)

    half_blocks = blocks // 2

    def sense(mine, state, *before):
        return pl.pallas_call(
            functools.partial(sense_kernel, mine),
            out_shape=(
                shape((half_blocks, 3 * SIDES, tokens, DK), BF),
                shape((2, 16, channels // 2), BF),
                shape((12 * HALF, DK), F32),
                shape((4 * HALF, DK), F32),
            ),
            grid_spec=pltpu.PrefetchScalarGridSpec(
                num_scalar_prefetch=1,
                grid=(1,),
                in_specs=[RESIDENT] * (5 + len(before)),
                out_specs=(RESIDENT,) * 4,
                scratch_shapes=[
                    pltpu.VMEM((tokens + 16, 3 * SIDES * DK), F32),
                    pltpu.VMEM((tokens + 8, 3 * SIDES * DK), F32),
                ],
            ),
            compiler_params=PARAMS,
            name="sense",
            cost_estimate=pl.CostEstimate(flops=3000000000, transcendentals=0, bytes_accessed=10800000),
        )(place, inner, rim, conv_weight, columns, state, *before)

    conv_own, edge, tap_own, start_own = sense(True, kept)
    conv_other, edge, tap_other, start_other = sense(False, received, edge)

    tap_far = lax.ppermute(tap_other, "seq", pairs)

    def ordered(one, two):
        return jnp.where(core == 0, one, two), jnp.where(core == 0, two, one)

    back_one = [(i + 1, i) for i in range(count - 1)]
    edge = lax.ppermute(edge, "seq", back_one)

    def own_at(i, b):
        return jnp.clip(i - b[0] * half_blocks, 0, half_blocks - 1)

    def other_at(i, b):
        return jnp.clip(i - (1 - b[0]) * half_blocks, 0, half_blocks - 1)

    def readouts(inside):
        return pl.pallas_call(
            readout_kernel,
            out_shape=shape((tokens, heads * DK), BF),
            grid_spec=pltpu.PrefetchScalarGridSpec(
                num_scalar_prefetch=1,
                grid=(blocks,),
                in_specs=[
                    pl.BlockSpec((1, 2, tokens, width), lambda i, b: (i, 0, 0, 0)),
                    pl.BlockSpec((1, tokens, 4 * SIDES), lambda i, b: (i, 0, 0)),
                    pl.BlockSpec((SIDES, 2 * DK, DK), lambda i, b: (own_at(i, b), 0, 0)),
                    pl.BlockSpec((SIDES, 2 * DK, DK), lambda i, b: (other_at(i, b), 0, 0)),
                ],
                out_specs=pl.BlockSpec((tokens, width), lambda i, b: (0, i)),
            ),
            compiler_params=PARAMS,
            name="readout",
            cost_estimate=pl.CostEstimate(flops=3000000000, transcendentals=0, bytes_accessed=10800000),
        )(place, inside, columns, kept, received)

    def unrolled(rim):
        return pl.pallas_call(
            unroll_kernel,
            out_shape=shape((tokens, channels), BF),
            grid_spec=pltpu.PrefetchScalarGridSpec(
                num_scalar_prefetch=1,
                grid=(blocks,),
                in_specs=[
                    pl.BlockSpec((1, 3 * SIDES, tokens, DK), lambda i, b: (own_at(i, b), 0, 0, 0)),
                    pl.BlockSpec((1, 3 * SIDES, tokens, DK), lambda i, b: (other_at(i, b), 0, 0, 0)),
                    whole(4, channels),
                    pl.BlockSpec((1, 16, 3 * width), lambda i, b: (1, 0, own_at(i, b))),
                    pl.BlockSpec((1, 16, 3 * width), lambda i, b: (0, 0, other_at(i, b))),
                ],
                out_specs=whole(tokens, channels),
                scratch_shapes=[pltpu.VMEM((tokens + 8, 3 * SIDES * DK), F32)],
            ),
            compiler_params=PARAMS,
            name="unroll",
            cost_estimate=pl.CostEstimate(flops=4000000000, transcendentals=0, bytes_accessed=14400000),
        )(place, conv_own, conv_other, conv_weight, rim, rim)

    dp = lax.axis_size("dp")
    tap_rows = 12 * HALF
    sum_rows = tap_rows + 4 * heads
    spread_taps = pl.pallas_call(
        pack_kernel,
        out_shape=shape((CHIPS, tap_rows, DK), BF),
        compiler_params=SHARED,
        name="pack",
        cost_estimate=pl.CostEstimate(flops=800000000, transcendentals=0, bytes_accessed=2880000),
    )(tap_own, tap_far)

    pieces = lax.all_to_all(spread_taps, "seq", 0, 0, axis_index_groups=groups)
    pieces, edge = lax.optimization_barrier((pieces, edge))
    spread_sums = pl.pallas_call(
        fold_kernel,
        out_shape=shape((dp, sum_rows, DK), BF),
        grid_spec=pltpu.PrefetchScalarGridSpec(
            num_scalar_prefetch=1,
            grid=(1,),
            in_specs=[RESIDENT] * 3,
            out_specs=RESIDENT,
        ),
        compiler_params=SHARED,
        name="fold",
        cost_estimate=pl.CostEstimate(flops=800000000, transcendentals=0, bytes_accessed=2880000),
    )(place, pieces, start_own, start_other)
    spread_sums, edge, inside = lax.optimization_barrier((spread_sums, edge, inside))
    pieces = lax.all_to_all(spread_sums, "dp", 0, 0)
    output = readouts(inside)
    grad = unrolled(edge)
    pieces, output, grad = lax.optimization_barrier((pieces, output, grad))
    total = pl.pallas_call(
        sum_kernel,
        out_shape=shape((sum_rows, DK), F32),
        compiler_params=SHARED,
        name="total",
        cost_estimate=pl.CostEstimate(flops=800000000, transcendentals=0, bytes_accessed=2880000),
    )(pieces)
    total_far = lax.ppermute(total, "seq", pairs)
    taps, start_all = pl.pallas_call(
        assemble_kernel,
        out_shape=(shape((4, channels), F32), shape((heads, 4, DK), F32)),
        grid_spec=pltpu.PrefetchScalarGridSpec(
            num_scalar_prefetch=1,
            grid=(1,),
            in_specs=[whole(sum_rows, DK)] * 2,
            out_specs=(whole(4, channels), whole(heads, 4, DK)),
        ),
        compiler_params=SHARED,
        name="assemble",
        cost_estimate=pl.CostEstimate(flops=1000000000, transcendentals=0, bytes_accessed=3600000),
    )(place, total, total_far)
    return (output[None], grad[None], taps, start_all)


def solution(mesh):
    in_specs = (
        P("dp", "seq", None),
        P(),
        P(),
        P("dp", None, "seq"),
        P("dp", None, "seq"),
        P("dp", None, "seq"),
        P("dp", "seq", None),
    )
    out_specs = (P("dp", "seq", None), P("dp", "seq", None), P(), P(None, "seq", None))
    return jax.shard_map(local, mesh=mesh, in_specs=in_specs, out_specs=out_specs, check_vma=False)
```

```python
import functools

import jax
import jax.numpy as jnp
from jax import lax
from jax.experimental import pallas as pl
from jax.experimental.pallas import tpu as pltpu
from jax.sharding import PartitionSpec as P

DK = 128
SIDES = 8
BF = jnp.bfloat16
F32 = jnp.float32
PARAMS = pltpu.CompilerParams(vmem_limit_bytes=32 * 1024 * 1024)
SHARED = pltpu.CompilerParams(vmem_limit_bytes=32 * 1024 * 1024)
CHIPS = 16
HALF = 8
EXTRA = 16
PIECE = 4 * 64 + EXTRA


def dot(a, b, contract):
    return lax.dot_general(a, b, ((contract[:1], contract[1:]), ((), ())), preferred_element_type=F32)


def here():
    mine = lax.axis_index("seq")
    core, chip = lax.rem(mine, 2), lax.div(mine, 2)
    return core, lax.div(chip, 8), core * (HALF * DK // 64) + chip


def to_column(row, eye):
    return jnp.sum(jnp.where(eye, row, 0.0), axis=1, keepdims=True)


def shifted(value, by, fill):
    tokens = value.shape[1]
    lane = lax.broadcasted_iota(jnp.int32, value.shape, 1)
    moved = pltpu.roll(value, by % tokens, axis=1)
    return jnp.where(lane >= by if by > 0 else lane < tokens + by, moved, fill)


def recurrence(factor, added, step):
    by = step
    while abs(by) < factor.shape[1]:
        added = added + factor * shifted(added, by, 0.0)
        factor = factor * shifted(factor, by, 1.0)
        by *= 2
    return added


def tables_kernel(gate_ref, column_ref, coef_ref, cum_ref):
    heads, tokens = gate_ref.shape[0] // 3, gate_ref.shape[1]
    rows = lax.broadcasted_iota(jnp.int32, (tokens, tokens), 0)
    lanes = lax.broadcasted_iota(jnp.int32, (tokens, tokens), 1)
    cum = lax.dot_general(
        gate_ref[0 : 2 * heads],
        (rows <= lanes).astype(F32),
        (((1,), (0,)), ((), ())),
        precision=lax.Precision.HIGHEST,
        preferred_element_type=F32,
    )
    cum_ref[...] = cum
    last = tokens - 1
    cum_forget, cum_moment = cum[:heads], cum[heads:]
    rate = gate_ref[2 * heads :]
    forget = jnp.exp(cum_forget)
    moment = jnp.exp(cum_moment)
    carry = recurrence(jnp.exp(gate_ref[0:heads]), moment, 1)
    lane = lax.broadcasted_iota(jnp.int32, (heads, tokens), 1)
    later = jnp.where(lane < last, pltpu.roll(jnp.exp(gate_ref[heads : 2 * heads]), last, axis=1), 0.0)
    memory = recurrence(later, jnp.exp(jnp.minimum(cum_forget[:, last:] - cum_forget, 0.0)), -1)
    memory = memory * rate
    tail = rate * jnp.exp(jnp.minimum(cum_moment[:, last:] - cum_moment, 0.0))
    for group in range(heads // SIDES):
        at = slice(group * SIDES, (group + 1) * SIDES)
        column_ref[group] = jnp.transpose(
            jnp.concatenate([memory[at], tail[at], forget[at], carry[at]], axis=0)
        )
    for which, value in enumerate((forget, carry, moment)):
        coef_ref[which * heads : (which + 1) * heads] = jnp.broadcast_to(value[:, last:], (heads, tokens))


def couple_kernel(gate_ref, cum_ref, coupling_ref):
    heads, tokens = gate_ref.shape[0] // 3, gate_ref.shape[1]
    rows = lax.broadcasted_iota(jnp.int32, (tokens, tokens), 0)
    lanes = lax.broadcasted_iota(jnp.int32, (tokens, tokens), 1)
    eye = rows == lanes
    causal = rows >= lanes
    for h in range(heads):
        maps = []
        for at in (h, heads + h):
            row = cum_ref[at : at + 1, :]
            decay = jnp.exp(jnp.minimum(to_column(row, eye) - row, 0.0))
            maps.append(jnp.where(causal, decay, 0.0).astype(BF))
        rated = dot(maps[0], maps[1], (1, 0)) * gate_ref[2 * heads + h : 2 * heads + h + 1, :]
        coupling_ref[h] = rated.astype(BF)


def extend(ext_ref, slot, halo, own):
    cols = slice(slot * DK, (slot + 1) * DK)
    ext_ref[0:8, cols] = halo.astype(F32)[8:16]
    ext_ref[8 : 8 + own.shape[0], cols] = own.astype(F32)


def convolve(ext_ref, slot, weights, tokens):
    cols = slice(slot * DK, (slot + 1) * DK)
    total = weights[0:1] * ext_ref[5 : 5 + tokens, cols]
    for tap in range(1, 4):
        total = total + weights[tap : tap + 1] * ext_ref[5 + tap : 5 + tap + tokens, cols]
    return total


def element_kernel(
    mine, rows_ref, u_ref, halo_ref, weight_ref, column_ref, element_ref, ext_ref
):
    tokens = rows_ref.shape[0]
    section = rows_ref.shape[1] // 3
    half = here()[0] if mine else 1 - here()[0]
    for side in range(HALF):
        made = []
        for part in range(3):
            at = pl.ds(pl.multiple_of(part * section + half * (HALF * DK) + side * DK, DK), DK)
            slot = side * 3 + part
            extend(ext_ref, slot, halo_ref[:, at], rows_ref[:, at])
            conv = convolve(ext_ref, slot, weight_ref[:, at], tokens)
            active = conv * (0.5 + 0.5 * jnp.tanh(0.5 * conv))
            if part < 2:
                active = active * lax.rsqrt(
                    jnp.sum(active * active, axis=1, keepdims=True) + 1e-06
                )
            made.append(active)
        query, key, value = made
        column = picker(column_ref, half, side)
        query = query.astype(BF).astype(F32)
        key = key.astype(BF).astype(F32)
        left = jnp.concatenate(
            [(key * column(0)).astype(BF), (key * column(1)).astype(BF)], axis=1
        )
        element_ref[side, 0 : 2 * DK] = dot(left, value.astype(BF), (0, 0)).astype(BF)
        left = jnp.concatenate(
            [(query * column(2)).astype(BF), (query * column(3)).astype(BF)], axis=1
        )
        upstream = u_ref[:, pl.ds(pl.multiple_of(half * (HALF * DK) + side * DK, DK), DK)]
        element_ref[side, 2 * DK : 4 * DK] = dot(left, upstream, (0, 0)).astype(BF)


def compose_kernel(own_ref, other_ref, own_coef_ref, other_coef_ref, out_ref):
    core = here()[0]
    first_core = core == 0
    heads = own_coef_ref.shape[0] // 3
    for j in range(own_ref.shape[0]):
        head = core * HALF + j

        def coef(which):
            mine = own_coef_ref[pl.ds(which * heads + head, 1), :]
            theirs = other_coef_ref[pl.ds(which * heads + head, 1), :]
            return jnp.where(first_core, mine, theirs), jnp.where(first_core, theirs, mine)

        def matrix(which):
            at = slice(which * DK, (which + 1) * DK)
            mine = own_ref[j, at].astype(F32)
            theirs = other_ref[j, at].astype(F32)
            return jnp.where(first_core, mine, theirs), jnp.where(first_core, theirs, mine)

        forget_a, forget_b = coef(0)
        carry_a, carry_b = coef(1)
        moment_a, moment_b = coef(2)
        memory_a, memory_b = matrix(0)
        state_a, state_b = matrix(1)
        recall_a, recall_b = matrix(2)
        direct_a, direct_b = matrix(3)
        joined = (
            forget_b * memory_a + carry_b * state_a + memory_b,
            moment_b * state_a + state_b,
            forget_a * recall_b + recall_a,
            carry_a * recall_b + moment_a * direct_b + direct_a,
        )
        scalars = []
        for value in (
            forget_a * forget_b,
            forget_b * carry_a + carry_b * moment_a,
            moment_a * moment_b,
        ):
            for term in range(3):
                kept = value.astype(BF).astype(F32)
                scalars.append(kept)
                value = value - kept
        scalars.append(jnp.zeros((EXTRA - len(scalars), DK), F32))
        tail = jnp.concatenate(scalars, axis=0).astype(BF)
        for half in range(2):
            for which, full in enumerate(joined):
                out_ref[2 * j + half, which * 64 : (which + 1) * 64] = full[
                    half * 64 : (half + 1) * 64
                ].astype(BF)
            out_ref[2 * j + half, 256:PIECE] = tail


def scan_kernel(got_ref, start_ref, out_ref):
    count = got_ref.shape[0]

    def coefs(c):
        rows = got_ref[c, 256:PIECE].astype(F32)
        return tuple(
            (rows[3 * i : 3 * i + 1] + rows[3 * i + 1 : 3 * i + 2]) + rows[3 * i + 2 : 3 * i + 3]
            for i in range(3)
        )

    scalars = [coefs(c) for c in range(count)]
    memory = start_ref[pl.ds(pl.multiple_of(here()[2] * 64, 64), 64), :]
    state = jnp.zeros_like(memory)
    for c in range(count):
        out_ref[c, 0:64] = memory.astype(BF)
        out_ref[c, 64:128] = state.astype(BF)
        forget, carry, moment = scalars[c]
        memory = forget * memory + carry * state + got_ref[c, 0:64].astype(F32)
        state = moment * state + got_ref[c, 64:128].astype(F32)
    memory = jnp.zeros_like(state)
    state = jnp.zeros_like(state)
    for c in reversed(range(count)):
        out_ref[c, 128:192] = memory.astype(BF)
        out_ref[c, 192:256] = state.astype(BF)
        forget, carry, moment = scalars[c]
        state = carry * memory + moment * state + got_ref[c, 192:256].astype(F32)
        memory = forget * memory + got_ref[c, 128:192].astype(F32)
    for c in range(count):
        rows = memory[8 * (c % 8) : 8 * (c % 8) + 8]
        high = rows.astype(BF).astype(F32)
        out_ref[c, 256:PIECE] = jnp.concatenate([high, rows - high], axis=0).astype(BF)


def spread_kernel(
    got_ref, own_ref, other_ref, own_coef_ref, other_coef_ref, keep_ref, send_ref
):
    core, side, _ = here()
    first_core = core == 0
    heads = own_coef_ref.shape[0] // 3
    for j in range(own_ref.shape[0]):
        head = core * HALF + j

        def coef(which):
            mine = own_coef_ref[pl.ds(which * heads + head, 1), :]
            theirs = other_coef_ref[pl.ds(which * heads + head, 1), :]
            return jnp.where(first_core, mine, theirs), jnp.where(first_core, theirs, mine)

        def local(which):
            at = slice(which * DK, (which + 1) * DK)
            mine = own_ref[j, at].astype(F32)
            theirs = other_ref[j, at].astype(F32)
            return jnp.where(first_core, mine, theirs), jnp.where(first_core, theirs, mine)

        def entering(which):
            at = slice(which * 64, (which + 1) * 64)
            return jnp.concatenate([got_ref[2 * j, at], got_ref[2 * j + 1, at]], axis=0).astype(F32)

        forget_a, forget_b = coef(0)
        carry_a, carry_b = coef(1)
        moment_a, moment_b = coef(2)
        memory, state = entering(0), entering(1)
        memory_end, state_end = entering(2), entering(3)
        one = (
            memory,
            state,
            forget_b * memory_end + local(2)[1],
            carry_b * memory_end + moment_b * state_end + local(3)[1],
        )
        two = (
            forget_a * memory + carry_a * state + local(0)[0],
            moment_a * state + local(1)[0],
            memory_end,
            state_end,
        )
        for which in range(4):
            at = slice(which * DK, (which + 1) * DK)
            keep_ref[j, at] = jnp.where(first_core, one[which], two[which]).astype(BF)
            send_ref[j, at] = jnp.where(first_core, two[which], one[which]).astype(BF)
        start = got_ref[2 * j + side, 256:PIECE]
        keep_ref[j, 4 * DK :] = start
        send_ref[j, 4 * DK :] = start


def inner_kernel(
    q_ref, k_ref, v_ref, u_ref, halo_ref, weight_ref, coupling_ref, out_ref, read_ref, ext_ref
):
    tokens, width = q_ref.shape
    section = halo_ref.shape[1] // 3
    block = pl.program_id(0)
    for side in range(width // DK):
        cols = slice(side * DK, (side + 1) * DK)
        made, slopes, units = [], [], []
        for part, ref in enumerate((q_ref, k_ref, v_ref)):
            at = pl.ds(pl.multiple_of(part * section + block * width + side * DK, DK), DK)
            slot = side * 3 + part
            extend(ext_ref, slot, halo_ref[:, at], ref[:, cols])
            conv = convolve(ext_ref, slot, weight_ref[:, at], tokens)
            gate = 0.5 + 0.5 * jnp.tanh(0.5 * conv)
            active = conv * gate
            slope = gate * (1.0 + conv * (1.0 - gate))
            slopes.append(slope)
            if part < 2:
                scale = lax.rsqrt(jnp.sum(active * active, axis=1, keepdims=True) + 1e-06)
                active = active * scale
                slope = slope * scale
                slopes[part] = slope
                units.append(active)
            active = active.astype(BF)
            made.append(active)
            out_ref[0, part, :, cols] = active
            out_ref[0, 4 + part, :, cols] = slope.astype(BF)
            out_ref[0, 10 + part, :, cols] = ref[:, cols]
        query, key, value = made
        upstream = u_ref[:, cols]
        out_ref[0, 3, :, cols] = upstream
        coupling = coupling_ref[side].astype(F32)
        scores = (dot(query, key, (1, 1)) * coupling).astype(BF)
        sense = (dot(upstream, value, (1, 1)) * coupling).astype(BF)
        grads = (
            dot(sense, key, (1, 0)),
            dot(sense, query, (0, 0)),
            dot(scores, upstream, (0, 0)),
        )
        for part, grad in enumerate(grads):
            if part < 2:
                unit = units[part]
                grad = grad - unit * jnp.sum(unit * grad, axis=1, keepdims=True)
            out_ref[0, 7 + part, :, cols] = (grad * slopes[part]).astype(BF)
        read_ref[0, 0, :, cols] = query
        read_ref[0, 1, :, cols] = dot(scores, value, (1, 0)).astype(BF)


def picker(column_ref, group, side):
    values = column_ref[group]
    return lambda which: values[:, which * SIDES + side : which * SIDES + side + 1]


def along_rows(left, pair):
    return dot(left, pair[:DK], (1, 0)), dot(left, pair[DK:], (1, 0))


def along_lanes(left, pair):
    both = dot(left, pair, (1, 1))
    return both[:, :DK], both[:, DK:]


def sense_kernel(
    mine, in_ref, halo_ref, weight_ref, column_ref, state_ref, *refs
):
    conv_ref, rim_ref, tap_ref, start_ref, pad_ref, ext_ref = refs[-6:]
    tokens = in_ref.shape[2]
    width = in_ref.shape[3]
    section = halo_ref.shape[1] // 3
    core = here()[0]
    block = core if mine else 1 - core
    if len(refs) > 6:
        rim_ref[0] = refs[0][1]
    else:
        rim_ref[0] = jnp.zeros(rim_ref.shape[1:], BF)

    pad_ref[0:8] = jnp.zeros((8, pad_ref.shape[1]), F32)
    pad_ref[8 + tokens :] = jnp.zeros((8, pad_ref.shape[1]), F32)

    for side in range(width // DK):
        cols = slice(side * DK, (side + 1) * DK)
        query, key, value, upstream = (in_ref[block, i, :, cols] for i in range(4))
        column = picker(column_ref, block, side)
        memory_col, tail_col, forget_col, carry_col = (column(i) for i in range(4))
        start = state_ref[side, 4 * DK :].astype(F32)
        start = start[0:8] + start[8:16]
        start_ref[4 * side : 4 * side + 4] = jnp.where(core == 0, start[0:4], start[4:8])
        forward, adjoint = state_ref[side, : 2 * DK], state_ref[side, 2 * DK : 4 * DK]
        grads = []
        a, b = along_lanes(upstream, forward)
        grads.append(forget_col * a + carry_col * b)
        a, b = along_lanes(value, adjoint)
        grads.append(memory_col * a + tail_col * b)
        a, b = along_rows(key, adjoint)
        grads.append(memory_col * a + tail_col * b)
        for part in range(3):
            grad = grads[part]
            if part < 2:
                unit = (query, key)[part].astype(F32)
                grad = grad - unit * jnp.sum(unit * grad, axis=1, keepdims=True)
            grad = grad * in_ref[block, 4 + part, :, cols].astype(F32)
            grad = grad + in_ref[block, 7 + part, :, cols].astype(F32)
            slot = side * 3 + part
            conv_ref[0, slot] = grad.astype(BF)
            there = slice(slot * DK, (slot + 1) * DK)
            pad_ref[8 : 8 + tokens, there] = grad
            at = pl.ds(pl.multiple_of(part * section + block * width + side * DK, DK), DK)
            extend(ext_ref, slot, halo_ref[:, at], in_ref[block, 10 + part, :, cols])
            rows = ext_ref[:, there]
            weights = weight_ref[:, at]
            rim = None
            for tap in range(4):
                moved = pad_ref[3 - tap : 3 - tap + 8 + tokens, there]
                slot_row = 12 * side + 4 * part + tap
                tap_ref[slot_row : slot_row + 1, :] = jnp.sum(moved * rows, axis=0, keepdims=True)
                lead = moved[0:8] * weights[tap : tap + 1]
                rim = lead if rim is None else rim + lead
            rim_ref[1, :, part * width + side * DK : part * width + (side + 1) * DK] = jnp.concatenate(
                [jnp.zeros_like(rim), rim], axis=0
            ).astype(BF)


def readout_kernel(
    place_ref, read_ref, column_ref, own_ref, other_ref, output_ref
):
    width = read_ref.shape[3]
    owned = (pl.program_id(0) // (pl.num_programs(0) // 2)) == place_ref[0]
    for side in range(width // DK):
        cols = slice(side * DK, (side + 1) * DK)
        column = picker(column_ref, 0, side)
        states = jnp.where(owned, own_ref[side], other_ref[side])
        from_memory, from_moment = along_rows(read_ref[0, 0, :, cols], states)
        readout = read_ref[0, 1, :, cols].astype(F32) + column(2) * from_memory + column(3) * from_moment
        output_ref[:, cols] = readout.astype(BF)


def unroll_kernel(
    place_ref, conv_own_ref, conv_other_ref, weight_ref, rim_own_ref, rim_other_ref, grad_ref, pad_ref
):
    tokens = conv_own_ref.shape[2]
    width = conv_own_ref.shape[1] // 3 * DK
    section = weight_ref.shape[1] // 3
    block = pl.program_id(0)
    owned = (block // (pl.num_programs(0) // 2)) == place_ref[0]

    @pl.when(block == 0)
    def _():
        pad_ref[tokens:] = jnp.zeros((8, pad_ref.shape[1]), F32)

    for side in range(width // DK):
        cols = slice(side * DK, (side + 1) * DK)
        for part in range(3):
            at = pl.ds(pl.multiple_of(part * section + block * width + side * DK, DK), DK)
            slot = side * 3 + part
            there = slice(slot * DK, (slot + 1) * DK)
            grad = jnp.where(owned, conv_own_ref[0, slot], conv_other_ref[0, slot]).astype(F32)
            weights = weight_ref[:, at]
            pad_ref[0:tokens, there] = grad
            total = grad * weights[3:4]
            for tap in range(3):
                total = total + pad_ref[3 - tap : 3 - tap + tokens, there] * weights[tap : tap + 1]
            near = slice(part * width + side * DK, part * width + (side + 1) * DK)
            rim = jnp.where(owned, rim_own_ref[0, :, near], rim_other_ref[0, :, near]).astype(F32)
            total = jnp.concatenate([total[: tokens - 16], total[tokens - 16 :] + rim], axis=0)
            grad_ref[:, at] = total.astype(BF)


def pack_kernel(own_ref, far_ref, out_ref):
    value = (own_ref[...] + far_ref[...]).astype(BF)
    for i in range(out_ref.shape[0]):
        out_ref[i] = value


def fold_kernel(pieces_ref, own_ref, other_ref, out_ref):
    total = pieces_ref[0].astype(F32)
    for i in range(1, pieces_ref.shape[0]):
        total = total + pieces_ref[i].astype(F32)
    own, other = own_ref[...], other_ref[...]
    first_core = here()[0] == 0
    value = jnp.concatenate(
        [total, jnp.where(first_core, own, other), jnp.where(first_core, other, own)], axis=0
    ).astype(BF)
    for i in range(out_ref.shape[0]):
        out_ref[i] = value


def sum_kernel(pieces_ref, out_ref):
    total = pieces_ref[0].astype(F32)
    for i in range(1, pieces_ref.shape[0]):
        total = total + pieces_ref[i].astype(F32)
    out_ref[...] = total


def assemble_kernel(own_ref, other_ref, out_ref, start_ref):
    section = out_ref.shape[1] // 3
    core = here()[0]
    for h in range(section // DK):
        first = 12 * HALF + 4 * h
        start_ref[h] = own_ref[first : first + 4]
    for h in range(section // DK):
        for part in range(3):
            first = 12 * (h % HALF) + 4 * part
            rows = slice(first, first + 4)
            at = part * section + h * DK
            out_ref[:, at : at + DK] = jnp.where(
                core == h // HALF, own_ref[rows], other_ref[rows]
            )


RESIDENT = pl.BlockSpec(memory_space=pltpu.VMEM)


def whole(*shape):
    return pl.BlockSpec(shape, lambda *_: (0,) * len(shape))


def local(projected, conv_weight, initial_memory, log_forget, log_momentum, learn_rate, cotangent):
    rows = projected[0]
    upstream = cotangent[0]
    tokens, channels = rows.shape
    heads = initial_memory.shape[0]
    width = SIDES * DK
    blocks = heads * DK // width
    count = lax.axis_size("seq")
    mine = lax.axis_index("seq")
    core = lax.rem(mine, 2)
    place = core.astype(jnp.int32).reshape(1)
    gates = jnp.concatenate([log_forget[0], log_momentum[0], learn_rate[0]], axis=0)
    gates, place = lax.optimization_barrier((gates, place))
    pairs = [(i, i ^ 1) for i in range(count)]
    groups = [[2 * c + k for c in range(count // 2)] for k in range(2)]

    rim = lax.ppermute(rows[tokens - 16 :], "seq", [(i, i + 1) for i in range(count - 1)])
    shape = jax.ShapeDtypeStruct
    columns, coefs, cums = pl.pallas_call(
        tables_kernel,
        out_shape=(
            shape((heads // SIDES, tokens, 4 * SIDES), F32),
            shape((3 * heads, DK), F32),
            shape((2 * heads, tokens), F32),
        ),
        compiler_params=SHARED,
        name="tables",
        cost_estimate=pl.CostEstimate(flops=2000000000, transcendentals=0, bytes_accessed=7200000),
    )(gates)
    other_coefs = lax.ppermute(coefs, "seq", pairs)

    def elements(mine):
        return pl.pallas_call(
            functools.partial(element_kernel, mine),
            out_shape=shape((HALF, 4 * DK, DK), BF),
            in_specs=[RESIDENT] * 5,
                out_specs=RESIDENT,
                scratch_shapes=[pltpu.VMEM((tokens + 8, 3 * HALF * DK), F32)],
            compiler_params=SHARED,
            name="elements",
            cost_estimate=pl.CostEstimate(flops=3400000000, transcendentals=0, bytes_accessed=12240000),
        )(rows, upstream, rim, conv_weight, columns)

    sent = elements(False)
    other = lax.ppermute(sent, "seq", pairs)
    own = elements(True)

    payload = pl.pallas_call(
        compose_kernel,
        out_shape=shape((CHIPS, PIECE, DK), BF),
        in_specs=[RESIDENT] * 4,
            out_specs=RESIDENT,
        compiler_params=SHARED,
        name="compose",
        cost_estimate=pl.CostEstimate(flops=1200000000, transcendentals=0, bytes_accessed=4320000),
    )(own, other, coefs, other_coefs)
    payload, cums = lax.optimization_barrier((payload, cums))
    got = lax.all_to_all(payload, "seq", 0, 0, axis_index_groups=groups)

    coupling = pl.pallas_call(
        couple_kernel,
        out_shape=shape((heads, tokens, tokens), BF),
        compiler_params=SHARED,
        name="couple",
        cost_estimate=pl.CostEstimate(flops=3500000000, transcendentals=0, bytes_accessed=12600000),
    )(gates, cums)

    def block_at(part):
        return pl.BlockSpec((tokens, width), lambda i: (0, part * blocks + i))

    inner, inside = pl.pallas_call(
        inner_kernel,
        out_shape=(
            shape((blocks, 13, tokens, width), BF),
            shape((blocks, 2, tokens, width), BF),
        ),
        grid=(blocks,),
        in_specs=[
            block_at(0),
            block_at(1),
            block_at(2),
            block_at(0),
            whole(16, channels),
            whole(4, channels),
            pl.BlockSpec((SIDES, tokens, tokens), lambda i: (i, 0, 0)),
        ],
        out_specs=(
            pl.BlockSpec((1, 13, tokens, width), lambda i: (i, 0, 0, 0)),
            pl.BlockSpec((1, 2, tokens, width), lambda i: (i, 0, 0, 0)),
        ),
        scratch_shapes=[pltpu.VMEM((tokens + 8, 3 * SIDES * DK), F32)],
        compiler_params=PARAMS,
        name="inner",
        cost_estimate=pl.CostEstimate(flops=8000000000, transcendentals=0, bytes_accessed=28800000),
    )(rows, rows, rows, upstream, rim, conv_weight, coupling)

    got, inner, inside = lax.optimization_barrier((got, inner, inside))
    back = pl.pallas_call(
        scan_kernel,
        out_shape=shape((CHIPS, PIECE, DK), BF),
        in_specs=[RESIDENT] * 2,
            out_specs=RESIDENT,
        compiler_params=SHARED,
        name="scan",
        cost_estimate=pl.CostEstimate(flops=400000000, transcendentals=0, bytes_accessed=1440000),
    )(got, initial_memory.reshape(heads * DK, DK))
    states = lax.all_to_all(back, "seq", 0, 0, axis_index_groups=groups)

    kept, passed = pl.pallas_call(
        spread_kernel,
        out_shape=(
            shape((HALF, 4 * DK + EXTRA, DK), BF),
            shape((HALF, 4 * DK + EXTRA, DK), BF),
        ),
        in_specs=[RESIDENT] * 5,
            out_specs=(RESIDENT,) * 2,
        compiler_params=SHARED,
        name="spread",
        cost_estimate=pl.CostEstimate(flops=1300000000, transcendentals=0, bytes_accessed=4680000),
    )(states, own, other, coefs, other_coefs)
    received = lax.ppermute(passed, "seq", pairs)

    half_blocks = blocks // 2

    def sense(mine, state, *before):
        return pl.pallas_call(
            functools.partial(sense_kernel, mine),
            out_shape=(
                shape((half_blocks, 3 * SIDES, tokens, DK), BF),
                shape((2, 16, channels // 2), BF),
                shape((12 * HALF, DK), F32),
                shape((4 * HALF, DK), F32),
            ),
            in_specs=[RESIDENT] * (5 + len(before)),
                out_specs=(RESIDENT,) * 4,
                scratch_shapes=[
                    pltpu.VMEM((tokens + 16, 3 * SIDES * DK), F32),
                    pltpu.VMEM((tokens + 8, 3 * SIDES * DK), F32),
                ],
            compiler_params=PARAMS,
            name="sense",
            cost_estimate=pl.CostEstimate(flops=3000000000, transcendentals=0, bytes_accessed=10800000),
        )(inner, rim, conv_weight, columns, state, *before)

    conv_own, edge, tap_own, start_own = sense(True, kept)
    conv_other, edge, tap_other, start_other = sense(False, received, edge)

    tap_far = lax.ppermute(tap_other, "seq", pairs)

    def ordered(one, two):
        return jnp.where(core == 0, one, two), jnp.where(core == 0, two, one)

    back_one = [(i + 1, i) for i in range(count - 1)]
    edge = lax.ppermute(edge, "seq", back_one)

    def own_at(i, b):
        return jnp.clip(i - b[0] * half_blocks, 0, half_blocks - 1)

    def other_at(i, b):
        return jnp.clip(i - (1 - b[0]) * half_blocks, 0, half_blocks - 1)

    def readouts(inside):
        return pl.pallas_call(
            readout_kernel,
            out_shape=shape((tokens, heads * DK), BF),
            grid_spec=pltpu.PrefetchScalarGridSpec(
                num_scalar_prefetch=1,
                grid=(blocks,),
                in_specs=[
                    pl.BlockSpec((1, 2, tokens, width), lambda i, b: (i, 0, 0, 0)),
                    pl.BlockSpec((1, tokens, 4 * SIDES), lambda i, b: (i, 0, 0)),
                    pl.BlockSpec((SIDES, 2 * DK, DK), lambda i, b: (own_at(i, b), 0, 0)),
                    pl.BlockSpec((SIDES, 2 * DK, DK), lambda i, b: (other_at(i, b), 0, 0)),
                ],
                out_specs=pl.BlockSpec((tokens, width), lambda i, b: (0, i)),
            ),
            compiler_params=PARAMS,
            name="readout",
            cost_estimate=pl.CostEstimate(flops=3000000000, transcendentals=0, bytes_accessed=10800000),
        )(place, inside, columns, kept, received)

    def unrolled(rim):
        return pl.pallas_call(
            unroll_kernel,
            out_shape=shape((tokens, channels), BF),
            grid_spec=pltpu.PrefetchScalarGridSpec(
                num_scalar_prefetch=1,
                grid=(blocks,),
                in_specs=[
                    pl.BlockSpec((1, 3 * SIDES, tokens, DK), lambda i, b: (own_at(i, b), 0, 0, 0)),
                    pl.BlockSpec((1, 3 * SIDES, tokens, DK), lambda i, b: (other_at(i, b), 0, 0, 0)),
                    whole(4, channels),
                    pl.BlockSpec((1, 16, 3 * width), lambda i, b: (1, 0, own_at(i, b))),
                    pl.BlockSpec((1, 16, 3 * width), lambda i, b: (0, 0, other_at(i, b))),
                ],
                out_specs=whole(tokens, channels),
                scratch_shapes=[pltpu.VMEM((tokens + 8, 3 * SIDES * DK), F32)],
            ),
            compiler_params=PARAMS,
            name="unroll",
            cost_estimate=pl.CostEstimate(flops=4000000000, transcendentals=0, bytes_accessed=14400000),
        )(place, conv_own, conv_other, conv_weight, rim, rim)

    dp = lax.axis_size("dp")
    tap_rows = 12 * HALF
    sum_rows = tap_rows + 4 * heads
    spread_taps = pl.pallas_call(
        pack_kernel,
        out_shape=shape((CHIPS, tap_rows, DK), BF),
        compiler_params=SHARED,
        name="pack",
        cost_estimate=pl.CostEstimate(flops=800000000, transcendentals=0, bytes_accessed=2880000),
    )(tap_own, tap_far)

    pieces = lax.all_to_all(spread_taps, "seq", 0, 0, axis_index_groups=groups)
    spread_sums = pl.pallas_call(
        fold_kernel,
        out_shape=shape((dp, sum_rows, DK), BF),
        in_specs=[RESIDENT] * 3,
            out_specs=RESIDENT,
        compiler_params=SHARED,
        name="fold",
        cost_estimate=pl.CostEstimate(flops=800000000, transcendentals=0, bytes_accessed=2880000),
    )(pieces, start_own, start_other)
    spread_sums, inside = lax.optimization_barrier((spread_sums, inside))
    pieces = lax.all_to_all(spread_sums, "dp", 0, 0)
    output = readouts(inside)
    edge, output = lax.optimization_barrier((edge, output))
    grad = unrolled(edge)
    pieces, output, grad = lax.optimization_barrier((pieces, output, grad))
    total = pl.pallas_call(
        sum_kernel,
        out_shape=shape((sum_rows, DK), F32),
        compiler_params=SHARED,
        name="total",
        cost_estimate=pl.CostEstimate(flops=800000000, transcendentals=0, bytes_accessed=2880000),
    )(pieces)
    total_far = lax.ppermute(total, "seq", pairs)
    taps, start_all = pl.pallas_call(
        assemble_kernel,
        out_shape=(shape((4, channels), F32), shape((heads, 4, DK), F32)),
        in_specs=[RESIDENT] * 2,
            out_specs=(RESIDENT,) * 2,
        compiler_params=SHARED,
        name="assemble",
        cost_estimate=pl.CostEstimate(flops=1000000000, transcendentals=0, bytes_accessed=3600000),
    )(total, total_far)
    return (output[None], grad[None], taps, start_all)


def solution(mesh):
    in_specs = (
        P("dp", "seq", None),
        P(),
        P(),
        P("dp", None, "seq"),
        P("dp", None, "seq"),
        P("dp", None, "seq"),
        P("dp", "seq", None),
    )
    out_specs = (P("dp", "seq", None), P("dp", "seq", None), P(), P(None, "seq", None))
    return jax.shard_map(local, mesh=mesh, in_specs=in_specs, out_specs=out_specs, check_vma=False)
```

```python
import functools

import jax
import jax.numpy as jnp
from jax import lax
from jax.experimental import pallas as pl
from jax.experimental.pallas import tpu as pltpu
from jax.sharding import PartitionSpec as P

DK = 128
SIDES = 8
BF = jnp.bfloat16
F32 = jnp.float32
PARAMS = pltpu.CompilerParams(vmem_limit_bytes=32 * 1024 * 1024)
SHARED = pltpu.CompilerParams(vmem_limit_bytes=32 * 1024 * 1024)
CHIPS = 16
HALF = 8
EXTRA = 16
PIECE = 4 * 64 + EXTRA


def dot(a, b, contract):
    return lax.dot_general(a, b, ((contract[:1], contract[1:]), ((), ())), preferred_element_type=F32)


def here():
    mine = lax.axis_index("seq")
    core, chip = lax.rem(mine, 2), lax.div(mine, 2)
    return core, lax.div(chip, 8), core * (HALF * DK // 64) + chip


def to_column(row, eye):
    return jnp.sum(jnp.where(eye, row, 0.0), axis=1, keepdims=True)


def shifted(value, by, fill):
    tokens = value.shape[1]
    lane = lax.broadcasted_iota(jnp.int32, value.shape, 1)
    moved = pltpu.roll(value, by % tokens, axis=1)
    return jnp.where(lane >= by if by > 0 else lane < tokens + by, moved, fill)


def recurrence(factor, added, step):
    by = step
    while abs(by) < factor.shape[1]:
        added = added + factor * shifted(added, by, 0.0)
        factor = factor * shifted(factor, by, 1.0)
        by *= 2
    return added


def tables_kernel(gate_ref, column_ref, coef_ref, cum_ref):
    heads, tokens = gate_ref.shape[0] // 3, gate_ref.shape[1]
    rows = lax.broadcasted_iota(jnp.int32, (tokens, tokens), 0)
    lanes = lax.broadcasted_iota(jnp.int32, (tokens, tokens), 1)
    cum = lax.dot_general(
        gate_ref[0 : 2 * heads],
        (rows <= lanes).astype(F32),
        (((1,), (0,)), ((), ())),
        precision=lax.Precision.HIGHEST,
        preferred_element_type=F32,
    )
    cum_ref[...] = cum
    last = tokens - 1
    cum_forget, cum_moment = cum[:heads], cum[heads:]
    rate = gate_ref[2 * heads :]
    forget = jnp.exp(cum_forget)
    moment = jnp.exp(cum_moment)
    carry = recurrence(jnp.exp(gate_ref[0:heads]), moment, 1)
    lane = lax.broadcasted_iota(jnp.int32, (heads, tokens), 1)
    later = jnp.where(lane < last, pltpu.roll(jnp.exp(gate_ref[heads : 2 * heads]), last, axis=1), 0.0)
    memory = recurrence(later, jnp.exp(jnp.minimum(cum_forget[:, last:] - cum_forget, 0.0)), -1)
    memory = memory * rate
    tail = rate * jnp.exp(jnp.minimum(cum_moment[:, last:] - cum_moment, 0.0))
    for group in range(heads // SIDES):
        at = slice(group * SIDES, (group + 1) * SIDES)
        column_ref[group] = jnp.transpose(
            jnp.concatenate([memory[at], tail[at], forget[at], carry[at]], axis=0)
        )
    for which, value in enumerate((forget, carry, moment)):
        coef_ref[which * heads : (which + 1) * heads] = jnp.broadcast_to(value[:, last:], (heads, tokens))


def couple_kernel(gate_ref, cum_ref, coupling_ref):
    heads, tokens = gate_ref.shape[0] // 3, gate_ref.shape[1]
    rows = lax.broadcasted_iota(jnp.int32, (tokens, tokens), 0)
    lanes = lax.broadcasted_iota(jnp.int32, (tokens, tokens), 1)
    eye = rows == lanes
    causal = rows >= lanes
    for h in range(heads):
        maps = []
        for at in (h, heads + h):
            row = cum_ref[at : at + 1, :]
            decay = jnp.exp(jnp.minimum(to_column(row, eye) - row, 0.0))
            maps.append(jnp.where(causal, decay, 0.0).astype(BF))
        rated = dot(maps[0], maps[1], (1, 0)) * gate_ref[2 * heads + h : 2 * heads + h + 1, :]
        coupling_ref[h] = rated.astype(BF)


def extend(ext_ref, slot, halo, own):
    cols = slice(slot * DK, (slot + 1) * DK)
    ext_ref[0:8, cols] = halo.astype(F32)[8:16]
    ext_ref[8 : 8 + own.shape[0], cols] = own.astype(F32)


def convolve(ext_ref, slot, weights, tokens):
    cols = slice(slot * DK, (slot + 1) * DK)
    total = weights[0:1] * ext_ref[5 : 5 + tokens, cols]
    for tap in range(1, 4):
        total = total + weights[tap : tap + 1] * ext_ref[5 + tap : 5 + tap + tokens, cols]
    return total


def element_kernel(
    mine, rows_ref, u_ref, halo_ref, weight_ref, column_ref, element_ref, ext_ref
):
    tokens = rows_ref.shape[0]
    section = rows_ref.shape[1] // 3
    half = here()[0] if mine else 1 - here()[0]
    for side in range(HALF):
        made = []
        for part in range(3):
            at = pl.ds(pl.multiple_of(part * section + half * (HALF * DK) + side * DK, DK), DK)
            slot = side * 3 + part
            extend(ext_ref, slot, halo_ref[:, at], rows_ref[:, at])
            conv = convolve(ext_ref, slot, weight_ref[:, at], tokens)
            active = conv * (0.5 + 0.5 * jnp.tanh(0.5 * conv))
            if part < 2:
                active = active * lax.rsqrt(
                    jnp.sum(active * active, axis=1, keepdims=True) + 1e-06
                )
            made.append(active)
        query, key, value = made
        column = picker(column_ref, half, side)
        value = value.astype(BF).astype(F32)
        right = jnp.concatenate([(value * column(0)).astype(BF), (value * column(1)).astype(BF)], axis=1)
        both = dot(key.astype(BF), right, (0, 0)).astype(BF)
        element_ref[side, 0:DK] = both[:, :DK]
        element_ref[side, DK : 2 * DK] = both[:, DK:]
        upstream = u_ref[:, pl.ds(pl.multiple_of(half * (HALF * DK) + side * DK, DK), DK)].astype(F32)
        right = jnp.concatenate(
            [(upstream * column(2)).astype(BF), (upstream * column(3)).astype(BF)], axis=1
        )
        both = dot(query.astype(BF), right, (0, 0)).astype(BF)
        element_ref[side, 2 * DK : 3 * DK] = both[:, :DK]
        element_ref[side, 3 * DK : 4 * DK] = both[:, DK:]


def compose_kernel(own_ref, other_ref, own_coef_ref, other_coef_ref, out_ref):
    core = here()[0]
    first_core = core == 0
    heads = own_coef_ref.shape[0] // 3
    for j in range(own_ref.shape[0]):
        head = core * HALF + j

        def coef(which):
            mine = own_coef_ref[pl.ds(which * heads + head, 1), :]
            theirs = other_coef_ref[pl.ds(which * heads + head, 1), :]
            return jnp.where(first_core, mine, theirs), jnp.where(first_core, theirs, mine)

        def matrix(which):
            at = slice(which * DK, (which + 1) * DK)
            mine = own_ref[j, at].astype(F32)
            theirs = other_ref[j, at].astype(F32)
            return jnp.where(first_core, mine, theirs), jnp.where(first_core, theirs, mine)

        forget_a, forget_b = coef(0)
        carry_a, carry_b = coef(1)
        moment_a, moment_b = coef(2)
        memory_a, memory_b = matrix(0)
        state_a, state_b = matrix(1)
        recall_a, recall_b = matrix(2)
        direct_a, direct_b = matrix(3)
        joined = (
            forget_b * memory_a + carry_b * state_a + memory_b,
            moment_b * state_a + state_b,
            forget_a * recall_b + recall_a,
            carry_a * recall_b + moment_a * direct_b + direct_a,
        )
        scalars = []
        for value in (
            forget_a * forget_b,
            forget_b * carry_a + carry_b * moment_a,
            moment_a * moment_b,
        ):
            for term in range(3):
                kept = value.astype(BF).astype(F32)
                scalars.append(kept)
                value = value - kept
        scalars.append(jnp.zeros((EXTRA - len(scalars), DK), F32))
        tail = jnp.concatenate(scalars, axis=0).astype(BF)
        for half in range(2):
            for which, full in enumerate(joined):
                out_ref[2 * j + half, which * 64 : (which + 1) * 64] = full[
                    half * 64 : (half + 1) * 64
                ].astype(BF)
            out_ref[2 * j + half, 256:PIECE] = tail


def scan_kernel(got_ref, start_ref, out_ref):
    count = got_ref.shape[0]

    def coefs(c):
        rows = got_ref[c, 256:PIECE].astype(F32)
        return tuple(
            (rows[3 * i : 3 * i + 1] + rows[3 * i + 1 : 3 * i + 2]) + rows[3 * i + 2 : 3 * i + 3]
            for i in range(3)
        )

    scalars = [coefs(c) for c in range(count)]
    memory = start_ref[pl.ds(pl.multiple_of(here()[2] * 64, 64), 64), :]
    state = jnp.zeros_like(memory)
    for c in range(count):
        out_ref[c, 0:64] = memory.astype(BF)
        out_ref[c, 64:128] = state.astype(BF)
        forget, carry, moment = scalars[c]
        memory = forget * memory + carry * state + got_ref[c, 0:64].astype(F32)
        state = moment * state + got_ref[c, 64:128].astype(F32)
    memory = jnp.zeros_like(state)
    state = jnp.zeros_like(state)
    for c in reversed(range(count)):
        out_ref[c, 128:192] = memory.astype(BF)
        out_ref[c, 192:256] = state.astype(BF)
        forget, carry, moment = scalars[c]
        state = carry * memory + moment * state + got_ref[c, 192:256].astype(F32)
        memory = forget * memory + got_ref[c, 128:192].astype(F32)
    for c in range(count):
        rows = memory[8 * (c % 8) : 8 * (c % 8) + 8]
        high = rows.astype(BF).astype(F32)
        out_ref[c, 256:PIECE] = jnp.concatenate([high, rows - high], axis=0).astype(BF)


def spread_kernel(
    got_ref, own_ref, other_ref, own_coef_ref, other_coef_ref, keep_ref, send_ref
):
    core, side, _ = here()
    first_core = core == 0
    heads = own_coef_ref.shape[0] // 3
    for j in range(own_ref.shape[0]):
        head = core * HALF + j

        def coef(which):
            mine = own_coef_ref[pl.ds(which * heads + head, 1), :]
            theirs = other_coef_ref[pl.ds(which * heads + head, 1), :]
            return jnp.where(first_core, mine, theirs), jnp.where(first_core, theirs, mine)

        def local(which):
            at = slice(which * DK, (which + 1) * DK)
            mine = own_ref[j, at].astype(F32)
            theirs = other_ref[j, at].astype(F32)
            return jnp.where(first_core, mine, theirs), jnp.where(first_core, theirs, mine)

        def entering(which):
            at = slice(which * 64, (which + 1) * 64)
            return jnp.concatenate([got_ref[2 * j, at], got_ref[2 * j + 1, at]], axis=0).astype(F32)

        forget_a, forget_b = coef(0)
        carry_a, carry_b = coef(1)
        moment_a, moment_b = coef(2)
        memory, state = entering(0), entering(1)
        memory_end, state_end = entering(2), entering(3)
        one = (
            memory,
            state,
            forget_b * memory_end + local(2)[1],
            carry_b * memory_end + moment_b * state_end + local(3)[1],
        )
        two = (
            forget_a * memory + carry_a * state + local(0)[0],
            moment_a * state + local(1)[0],
            memory_end,
            state_end,
        )
        for which in range(4):
            at = slice(which * DK, (which + 1) * DK)
            keep_ref[j, at] = jnp.where(first_core, one[which], two[which]).astype(BF)
            send_ref[j, at] = jnp.where(first_core, two[which], one[which]).astype(BF)
        start = got_ref[2 * j + side, 256:PIECE]
        keep_ref[j, 4 * DK :] = start
        send_ref[j, 4 * DK :] = start


def inner_kernel(
    q_ref, k_ref, v_ref, u_ref, halo_ref, weight_ref, coupling_ref, out_ref, read_ref, ext_ref
):
    tokens, width = q_ref.shape
    section = halo_ref.shape[1] // 3
    block = pl.program_id(0)
    for side in range(width // DK):
        cols = slice(side * DK, (side + 1) * DK)
        made, slopes, units = [], [], []
        for part, ref in enumerate((q_ref, k_ref, v_ref)):
            at = pl.ds(pl.multiple_of(part * section + block * width + side * DK, DK), DK)
            slot = side * 3 + part
            extend(ext_ref, slot, halo_ref[:, at], ref[:, cols])
            conv = convolve(ext_ref, slot, weight_ref[:, at], tokens)
            gate = 0.5 + 0.5 * jnp.tanh(0.5 * conv)
            active = conv * gate
            slope = gate * (1.0 + conv * (1.0 - gate))
            slopes.append(slope)
            if part < 2:
                scale = lax.rsqrt(jnp.sum(active * active, axis=1, keepdims=True) + 1e-06)
                active = active * scale
                slope = slope * scale
                slopes[part] = slope
                units.append(active)
            active = active.astype(BF)
            made.append(active)
            out_ref[0, part, :, cols] = active
            out_ref[0, 4 + part, :, cols] = slope.astype(BF)
            out_ref[0, 10 + part, :, cols] = ref[:, cols]
        query, key, value = made
        upstream = u_ref[:, cols]
        out_ref[0, 3, :, cols] = upstream
        coupling = coupling_ref[side].astype(F32)
        scores = (dot(query, key, (1, 1)) * coupling).astype(BF)
        sense = (dot(upstream, value, (1, 1)) * coupling).astype(BF)
        grads = (
            dot(sense, key, (1, 0)),
            dot(sense, query, (0, 0)),
            dot(scores, upstream, (0, 0)),
        )
        for part, grad in enumerate(grads):
            if part < 2:
                unit = units[part]
                grad = grad - unit * jnp.sum(unit * grad, axis=1, keepdims=True)
            out_ref[0, 7 + part, :, cols] = (grad * slopes[part]).astype(BF)
        read_ref[0, 0, :, cols] = query
        read_ref[0, 1, :, cols] = dot(scores, value, (1, 0)).astype(BF)


def picker(column_ref, group, side):
    values = column_ref[group]
    return lambda which: values[:, which * SIDES + side : which * SIDES + side + 1]


def along_rows(left, pair):
    return dot(left, pair[:DK], (1, 0)), dot(left, pair[DK:], (1, 0))


def along_lanes(left, pair):
    both = dot(left, pair, (1, 1))
    return both[:, :DK], both[:, DK:]


def sense_kernel(
    mine, in_ref, halo_ref, weight_ref, column_ref, state_ref, *refs
):
    conv_ref, rim_ref, tap_ref, start_ref, pad_ref, ext_ref = refs[-6:]
    tokens = in_ref.shape[2]
    width = in_ref.shape[3]
    section = halo_ref.shape[1] // 3
    core = here()[0]
    block = core if mine else 1 - core
    if len(refs) > 6:
        rim_ref[0] = refs[0][1]
    else:
        rim_ref[0] = jnp.zeros(rim_ref.shape[1:], BF)

    pad_ref[0:8] = jnp.zeros((8, pad_ref.shape[1]), F32)
    pad_ref[8 + tokens :] = jnp.zeros((8, pad_ref.shape[1]), F32)

    for side in range(width // DK):
        cols = slice(side * DK, (side + 1) * DK)
        query, key, value, upstream = (in_ref[block, i, :, cols] for i in range(4))
        column = picker(column_ref, block, side)
        memory_col, tail_col, forget_col, carry_col = (column(i) for i in range(4))
        start = state_ref[side, 4 * DK :].astype(F32)
        start = start[0:8] + start[8:16]
        start_ref[4 * side : 4 * side + 4] = jnp.where(core == 0, start[0:4], start[4:8])
        forward, adjoint = state_ref[side, : 2 * DK], state_ref[side, 2 * DK : 4 * DK]
        grads = []
        a, b = along_lanes(upstream, forward)
        grads.append(forget_col * a + carry_col * b)
        a, b = along_lanes(value, adjoint)
        grads.append(memory_col * a + tail_col * b)
        a, b = along_rows(key, adjoint)
        grads.append(memory_col * a + tail_col * b)
        rims = []
        for part in range(3):
            grad = grads[part]
            if part < 2:
                unit = (query, key)[part].astype(F32)
                grad = grad - unit * jnp.sum(unit * grad, axis=1, keepdims=True)
            grad = grad * in_ref[block, 4 + part, :, cols].astype(F32)
            grad = grad + in_ref[block, 7 + part, :, cols].astype(F32)
            slot = side * 3 + part
            conv_ref[0, slot] = grad.astype(BF)
            there = slice(slot * DK, (slot + 1) * DK)
            pad_ref[8 : 8 + tokens, there] = grad
            at = pl.ds(pl.multiple_of(part * section + block * width + side * DK, DK), DK)
            extend(ext_ref, slot, halo_ref[:, at], in_ref[block, 10 + part, :, cols])
            rows = ext_ref[:, there]
            weights = weight_ref[:, at]
            rim = None
            for tap in range(4):
                moved = pad_ref[3 - tap : 3 - tap + 8 + tokens, there]
                slot_row = 12 * side + 4 * part + tap
                tap_ref[slot_row : slot_row + 1, :] = jnp.sum(moved * rows, axis=0, keepdims=True)
                lead = moved[0:8] * weights[tap : tap + 1]
                rim = lead if rim is None else rim + lead
            rims.append(rim[5:8])
        rims.append(jnp.zeros((7, DK), F32))
        rim_ref[1, :, cols] = jnp.concatenate(rims, axis=0).astype(BF)


def readout_kernel(
    place_ref, read_ref, column_ref, own_ref, other_ref, output_ref
):
    width = read_ref.shape[3]
    owned = (pl.program_id(0) // (pl.num_programs(0) // 2)) == place_ref[0]
    for side in range(width // DK):
        cols = slice(side * DK, (side + 1) * DK)
        column = picker(column_ref, 0, side)
        states = jnp.where(owned, own_ref[side], other_ref[side])
        from_memory, from_moment = along_rows(read_ref[0, 0, :, cols], states)
        readout = read_ref[0, 1, :, cols].astype(F32) + column(2) * from_memory + column(3) * from_moment
        output_ref[:, cols] = readout.astype(BF)


def unroll_kernel(
    place_ref, conv_own_ref, conv_other_ref, weight_ref, rim_own_ref, rim_other_ref, grad_ref, pad_ref
):
    tokens = conv_own_ref.shape[2]
    width = conv_own_ref.shape[1] // 3 * DK
    section = weight_ref.shape[1] // 3
    block = pl.program_id(0)
    owned = (block // (pl.num_programs(0) // 2)) == place_ref[0]

    @pl.when(block == 0)
    def _():
        pad_ref[tokens:] = jnp.zeros((8, pad_ref.shape[1]), F32)

    for side in range(width // DK):
        cols = slice(side * DK, (side + 1) * DK)
        rims = jnp.where(owned, rim_own_ref[0, :, cols], rim_other_ref[0, :, cols]).astype(F32)
        for part in range(3):
            at = pl.ds(pl.multiple_of(part * section + block * width + side * DK, DK), DK)
            slot = side * 3 + part
            there = slice(slot * DK, (slot + 1) * DK)
            grad = jnp.where(owned, conv_own_ref[0, slot], conv_other_ref[0, slot]).astype(F32)
            weights = weight_ref[:, at]
            pad_ref[0:tokens, there] = grad
            total = grad * weights[3:4]
            for tap in range(3):
                total = total + pad_ref[3 - tap : 3 - tap + tokens, there] * weights[tap : tap + 1]
            rim = rims[3 * part : 3 * part + 3]
            total = jnp.concatenate([total[: tokens - 3], total[tokens - 3 :] + rim], axis=0)
            grad_ref[:, at] = total.astype(BF)


def pack_kernel(own_ref, far_ref, out_ref):
    value = (own_ref[...] + far_ref[...]).astype(BF)
    for i in range(out_ref.shape[0]):
        out_ref[i] = value


def fold_kernel(pieces_ref, own_ref, other_ref, out_ref):
    total = pieces_ref[0].astype(F32)
    for i in range(1, pieces_ref.shape[0]):
        total = total + pieces_ref[i].astype(F32)
    own, other = own_ref[...], other_ref[...]
    first_core = here()[0] == 0
    value = jnp.concatenate(
        [total, jnp.where(first_core, own, other), jnp.where(first_core, other, own)], axis=0
    ).astype(BF)
    for i in range(out_ref.shape[0]):
        out_ref[i] = value


def sum_kernel(pieces_ref, out_ref):
    total = pieces_ref[0].astype(F32)
    for i in range(1, pieces_ref.shape[0]):
        total = total + pieces_ref[i].astype(F32)
    out_ref[...] = total


def assemble_kernel(own_ref, other_ref, out_ref, start_ref):
    section = out_ref.shape[1] // 3
    core = here()[0]
    for h in range(section // DK):
        first = 12 * HALF + 4 * h
        start_ref[h] = own_ref[first : first + 4]
    for h in range(section // DK):
        for part in range(3):
            first = 12 * (h % HALF) + 4 * part
            rows = slice(first, first + 4)
            at = part * section + h * DK
            out_ref[:, at : at + DK] = jnp.where(
                core == h // HALF, own_ref[rows], other_ref[rows]
            )


RESIDENT = pl.BlockSpec(memory_space=pltpu.VMEM)


def whole(*shape):
    return pl.BlockSpec(shape, lambda *_: (0,) * len(shape))


def local(projected, conv_weight, initial_memory, log_forget, log_momentum, learn_rate, cotangent):
    rows = projected[0]
    upstream = cotangent[0]
    tokens, channels = rows.shape
    heads = initial_memory.shape[0]
    width = SIDES * DK
    blocks = heads * DK // width
    count = lax.axis_size("seq")
    mine = lax.axis_index("seq")
    core = lax.rem(mine, 2)
    place = core.astype(jnp.int32).reshape(1)
    gates = jnp.concatenate([log_forget[0], log_momentum[0], learn_rate[0]], axis=0)
    gates, place = lax.optimization_barrier((gates, place))
    pairs = [(i, i ^ 1) for i in range(count)]
    groups = [[2 * c + k for c in range(count // 2)] for k in range(2)]

    rim = lax.ppermute(rows[tokens - 16 :], "seq", [(i, i + 1) for i in range(count - 1)])
    shape = jax.ShapeDtypeStruct
    columns, coefs, cums = pl.pallas_call(
        tables_kernel,
        out_shape=(
            shape((heads // SIDES, tokens, 4 * SIDES), F32),
            shape((3 * heads, DK), F32),
            shape((2 * heads, tokens), F32),
        ),
        compiler_params=SHARED,
        name="tables",
        cost_estimate=pl.CostEstimate(flops=2000000000, transcendentals=0, bytes_accessed=7200000),
    )(gates)
    other_coefs = lax.ppermute(coefs, "seq", pairs)

    def elements(mine):
        return pl.pallas_call(
            functools.partial(element_kernel, mine),
            out_shape=shape((HALF, 4 * DK, DK), BF),
            in_specs=[RESIDENT] * 5,
                out_specs=RESIDENT,
                scratch_shapes=[pltpu.VMEM((tokens + 8, 3 * HALF * DK), F32)],
            compiler_params=SHARED,
            name="elements",
            cost_estimate=pl.CostEstimate(flops=3400000000, transcendentals=0, bytes_accessed=12240000),
        )(rows, upstream, rim, conv_weight, columns)

    sent = elements(False)
    other = lax.ppermute(sent, "seq", pairs)
    own = elements(True)

    payload = pl.pallas_call(
        compose_kernel,
        out_shape=shape((CHIPS, PIECE, DK), BF),
        in_specs=[RESIDENT] * 4,
            out_specs=RESIDENT,
        compiler_params=SHARED,
        name="compose",
        cost_estimate=pl.CostEstimate(flops=1200000000, transcendentals=0, bytes_accessed=4320000),
    )(own, other, coefs, other_coefs)
    payload, cums = lax.optimization_barrier((payload, cums))
    got = lax.all_to_all(payload, "seq", 0, 0, axis_index_groups=groups)

    coupling = pl.pallas_call(
        couple_kernel,
        out_shape=shape((heads, tokens, tokens), BF),
        compiler_params=SHARED,
        name="couple",
        cost_estimate=pl.CostEstimate(flops=3500000000, transcendentals=0, bytes_accessed=12600000),
    )(gates, cums)

    def block_at(part):
        return pl.BlockSpec((tokens, width), lambda i: (0, part * blocks + i))

    inner, inside = pl.pallas_call(
        inner_kernel,
        out_shape=(
            shape((blocks, 13, tokens, width), BF),
            shape((blocks, 2, tokens, width), BF),
        ),
        grid=(blocks,),
        in_specs=[
            block_at(0),
            block_at(1),
            block_at(2),
            block_at(0),
            whole(16, channels),
            whole(4, channels),
            pl.BlockSpec((SIDES, tokens, tokens), lambda i: (i, 0, 0)),
        ],
        out_specs=(
            pl.BlockSpec((1, 13, tokens, width), lambda i: (i, 0, 0, 0)),
            pl.BlockSpec((1, 2, tokens, width), lambda i: (i, 0, 0, 0)),
        ),
        scratch_shapes=[pltpu.VMEM((tokens + 8, 3 * SIDES * DK), F32)],
        compiler_params=PARAMS,
        name="inner",
        cost_estimate=pl.CostEstimate(flops=8000000000, transcendentals=0, bytes_accessed=28800000),
    )(rows, rows, rows, upstream, rim, conv_weight, coupling)

    got, inner, inside = lax.optimization_barrier((got, inner, inside))
    back = pl.pallas_call(
        scan_kernel,
        out_shape=shape((CHIPS, PIECE, DK), BF),
        in_specs=[RESIDENT] * 2,
            out_specs=RESIDENT,
        compiler_params=SHARED,
        name="scan",
        cost_estimate=pl.CostEstimate(flops=400000000, transcendentals=0, bytes_accessed=1440000),
    )(got, initial_memory.reshape(heads * DK, DK))
    states = lax.all_to_all(back, "seq", 0, 0, axis_index_groups=groups)

    kept, passed = pl.pallas_call(
        spread_kernel,
        out_shape=(
            shape((HALF, 4 * DK + EXTRA, DK), BF),
            shape((HALF, 4 * DK + EXTRA, DK), BF),
        ),
        in_specs=[RESIDENT] * 5,
            out_specs=(RESIDENT,) * 2,
        compiler_params=SHARED,
        name="spread",
        cost_estimate=pl.CostEstimate(flops=1300000000, transcendentals=0, bytes_accessed=4680000),
    )(states, own, other, coefs, other_coefs)
    received = lax.ppermute(passed, "seq", pairs)

    half_blocks = blocks // 2

    def sense(mine, state, *before):
        return pl.pallas_call(
            functools.partial(sense_kernel, mine),
            out_shape=(
                shape((half_blocks, 3 * SIDES, tokens, DK), BF),
                shape((2, 16, HALF * DK), BF),
                shape((12 * HALF, DK), F32),
                shape((4 * HALF, DK), F32),
            ),
            in_specs=[RESIDENT] * (5 + len(before)),
                out_specs=(RESIDENT,) * 4,
                scratch_shapes=[
                    pltpu.VMEM((tokens + 16, 3 * SIDES * DK), F32),
                    pltpu.VMEM((tokens + 8, 3 * SIDES * DK), F32),
                ],
            compiler_params=PARAMS,
            name="sense",
            cost_estimate=pl.CostEstimate(flops=3000000000, transcendentals=0, bytes_accessed=10800000),
        )(inner, rim, conv_weight, columns, state, *before)

    conv_own, edge, tap_own, start_own = sense(True, kept)
    conv_other, edge, tap_other, start_other = sense(False, received, edge)

    tap_far = lax.ppermute(tap_other, "seq", pairs)

    def ordered(one, two):
        return jnp.where(core == 0, one, two), jnp.where(core == 0, two, one)

    back_one = [(i + 1, i) for i in range(count - 1)]
    edge = lax.ppermute(edge, "seq", back_one)

    def own_at(i, b):
        return jnp.clip(i - b[0] * half_blocks, 0, half_blocks - 1)

    def other_at(i, b):
        return jnp.clip(i - (1 - b[0]) * half_blocks, 0, half_blocks - 1)

    def readouts(inside):
        return pl.pallas_call(
            readout_kernel,
            out_shape=shape((tokens, heads * DK), BF),
            grid_spec=pltpu.PrefetchScalarGridSpec(
                num_scalar_prefetch=1,
                grid=(blocks,),
                in_specs=[
                    pl.BlockSpec((1, 2, tokens, width), lambda i, b: (i, 0, 0, 0)),
                    pl.BlockSpec((1, tokens, 4 * SIDES), lambda i, b: (i, 0, 0)),
                    pl.BlockSpec((SIDES, 2 * DK, DK), lambda i, b: (own_at(i, b), 0, 0)),
                    pl.BlockSpec((SIDES, 2 * DK, DK), lambda i, b: (other_at(i, b), 0, 0)),
                ],
                out_specs=pl.BlockSpec((tokens, width), lambda i, b: (0, i)),
            ),
            compiler_params=PARAMS,
            name="readout",
            cost_estimate=pl.CostEstimate(flops=3000000000, transcendentals=0, bytes_accessed=10800000),
        )(place, inside, columns, kept, received)

    def unrolled(rim):
        return pl.pallas_call(
            unroll_kernel,
            out_shape=shape((tokens, channels), BF),
            grid_spec=pltpu.PrefetchScalarGridSpec(
                num_scalar_prefetch=1,
                grid=(blocks,),
                in_specs=[
                    pl.BlockSpec((1, 3 * SIDES, tokens, DK), lambda i, b: (own_at(i, b), 0, 0, 0)),
                    pl.BlockSpec((1, 3 * SIDES, tokens, DK), lambda i, b: (other_at(i, b), 0, 0, 0)),
                    whole(4, channels),
                    pl.BlockSpec((1, 16, width), lambda i, b: (1, 0, own_at(i, b))),
                    pl.BlockSpec((1, 16, width), lambda i, b: (0, 0, other_at(i, b))),
                ],
                out_specs=whole(tokens, channels),
                scratch_shapes=[pltpu.VMEM((tokens + 8, 3 * SIDES * DK), F32)],
            ),
            compiler_params=PARAMS,
            name="unroll",
            cost_estimate=pl.CostEstimate(flops=4000000000, transcendentals=0, bytes_accessed=14400000),
        )(place, conv_own, conv_other, conv_weight, rim, rim)

    dp = lax.axis_size("dp")
    tap_rows = 12 * HALF
    sum_rows = tap_rows + 4 * heads
    spread_taps = pl.pallas_call(
        pack_kernel,
        out_shape=shape((CHIPS, tap_rows, DK), BF),
        compiler_params=SHARED,
        name="pack",
        cost_estimate=pl.CostEstimate(flops=800000000, transcendentals=0, bytes_accessed=2880000),
    )(tap_own, tap_far)

    pieces = lax.all_to_all(spread_taps, "seq", 0, 0, axis_index_groups=groups)
    spread_sums = pl.pallas_call(
        fold_kernel,
        out_shape=shape((dp, sum_rows, DK), BF),
        in_specs=[RESIDENT] * 3,
            out_specs=RESIDENT,
        compiler_params=SHARED,
        name="fold",
        cost_estimate=pl.CostEstimate(flops=800000000, transcendentals=0, bytes_accessed=2880000),
    )(pieces, start_own, start_other)
    spread_sums, inside = lax.optimization_barrier((spread_sums, inside))
    pieces = lax.all_to_all(spread_sums, "dp", 0, 0)
    output = readouts(inside)
    edge, output = lax.optimization_barrier((edge, output))
    grad = unrolled(edge)
    pieces, output, grad = lax.optimization_barrier((pieces, output, grad))
    total = pl.pallas_call(
        sum_kernel,
        out_shape=shape((sum_rows, DK), F32),
        compiler_params=SHARED,
        name="total",
        cost_estimate=pl.CostEstimate(flops=800000000, transcendentals=0, bytes_accessed=2880000),
    )(pieces)
    total_far = lax.ppermute(total, "seq", pairs)
    taps, start_all = pl.pallas_call(
        assemble_kernel,
        out_shape=(shape((4, channels), F32), shape((heads, 4, DK), F32)),
        in_specs=[RESIDENT] * 2,
            out_specs=(RESIDENT,) * 2,
        compiler_params=SHARED,
        name="assemble",
        cost_estimate=pl.CostEstimate(flops=1000000000, transcendentals=0, bytes_accessed=3600000),
    )(total, total_far)
    return (output[None], grad[None], taps, start_all)


def solution(mesh):
    in_specs = (
        P("dp", "seq", None),
        P(),
        P(),
        P("dp", None, "seq"),
        P("dp", None, "seq"),
        P("dp", None, "seq"),
        P("dp", "seq", None),
    )
    out_specs = (P("dp", "seq", None), P("dp", "seq", None), P(), P(None, "seq", None))
    return jax.shard_map(local, mesh=mesh, in_specs=in_specs, out_specs=out_specs, check_vma=False)
```

```python
import functools

import jax
import jax.numpy as jnp
from jax import lax
from jax.experimental import pallas as pl
from jax.experimental.pallas import tpu as pltpu
from jax.sharding import PartitionSpec as P

DK = 128
SIDES = 8
BF = jnp.bfloat16
F32 = jnp.float32
PARAMS = pltpu.CompilerParams(vmem_limit_bytes=32 * 1024 * 1024)
SHARED = pltpu.CompilerParams(vmem_limit_bytes=32 * 1024 * 1024)
CHIPS = 16
HALF = 8
EXTRA = 16
PIECE = 4 * 64 + EXTRA


def dot(a, b, contract):
    return lax.dot_general(a, b, ((contract[:1], contract[1:]), ((), ())), preferred_element_type=F32)


def here():
    mine = lax.axis_index("seq")
    core, chip = lax.rem(mine, 2), lax.div(mine, 2)
    return core, lax.div(chip, 8), core * (HALF * DK // 64) + chip


def to_column(row, eye):
    return jnp.sum(jnp.where(eye, row, 0.0), axis=1, keepdims=True)


def shifted(value, by, fill):
    tokens = value.shape[1]
    lane = lax.broadcasted_iota(jnp.int32, value.shape, 1)
    moved = pltpu.roll(value, by % tokens, axis=1)
    return jnp.where(lane >= by if by > 0 else lane < tokens + by, moved, fill)


def recurrence(factor, added, step):
    by = step
    while abs(by) < factor.shape[1]:
        added = added + factor * shifted(added, by, 0.0)
        factor = factor * shifted(factor, by, 1.0)
        by *= 2
    return added


def tables_kernel(gate_ref, column_ref, coef_ref, cum_ref):
    heads, tokens = gate_ref.shape[0] // 3, gate_ref.shape[1]
    rows = lax.broadcasted_iota(jnp.int32, (tokens, tokens), 0)
    lanes = lax.broadcasted_iota(jnp.int32, (tokens, tokens), 1)
    cum = lax.dot_general(
        gate_ref[0 : 2 * heads],
        (rows <= lanes).astype(F32),
        (((1,), (0,)), ((), ())),
        precision=lax.Precision.HIGHEST,
        preferred_element_type=F32,
    )
    cum_ref[...] = cum
    last = tokens - 1
    cum_forget, cum_moment = cum[:heads], cum[heads:]
    rate = gate_ref[2 * heads :]
    forget = jnp.exp(cum_forget)
    moment = jnp.exp(cum_moment)
    carry = recurrence(jnp.exp(gate_ref[0:heads]), moment, 1)
    lane = lax.broadcasted_iota(jnp.int32, (heads, tokens), 1)
    later = jnp.where(lane < last, pltpu.roll(jnp.exp(gate_ref[heads : 2 * heads]), last, axis=1), 0.0)
    memory = recurrence(later, jnp.exp(jnp.minimum(cum_forget[:, last:] - cum_forget, 0.0)), -1)
    memory = memory * rate
    tail = rate * jnp.exp(jnp.minimum(cum_moment[:, last:] - cum_moment, 0.0))
    for group in range(heads // SIDES):
        at = slice(group * SIDES, (group + 1) * SIDES)
        column_ref[group] = jnp.transpose(
            jnp.concatenate([memory[at], tail[at], forget[at], carry[at]], axis=0)
        )
    for which, value in enumerate((forget, carry, moment)):
        coef_ref[which * heads : (which + 1) * heads] = jnp.broadcast_to(value[:, last:], (heads, tokens))


def couple_kernel(gate_ref, cum_ref, coupling_ref):
    heads, tokens = gate_ref.shape[0] // 3, gate_ref.shape[1]
    rows = lax.broadcasted_iota(jnp.int32, (tokens, tokens), 0)
    lanes = lax.broadcasted_iota(jnp.int32, (tokens, tokens), 1)
    eye = rows == lanes
    causal = rows >= lanes
    for h in range(heads):
        maps = []
        for at in (h, heads + h):
            row = cum_ref[at : at + 1, :]
            decay = jnp.exp(jnp.minimum(to_column(row, eye) - row, 0.0))
            maps.append(jnp.where(causal, decay, 0.0).astype(BF))
        rated = dot(maps[0], maps[1], (1, 0)) * gate_ref[2 * heads + h : 2 * heads + h + 1, :]
        coupling_ref[h] = rated


def extend(ext_ref, slot, halo, own):
    cols = slice(slot * DK, (slot + 1) * DK)
    ext_ref[0:8, cols] = halo.astype(F32)[8:16]
    ext_ref[8 : 8 + own.shape[0], cols] = own.astype(F32)


def convolve(ext_ref, slot, weights, tokens):
    cols = slice(slot * DK, (slot + 1) * DK)
    total = weights[0:1] * ext_ref[5 : 5 + tokens, cols]
    for tap in range(1, 4):
        total = total + weights[tap : tap + 1] * ext_ref[5 + tap : 5 + tap + tokens, cols]
    return total


def element_kernel(
    mine, rows_ref, u_ref, halo_ref, weight_ref, column_ref, element_ref, ext_ref
):
    tokens = rows_ref.shape[0]
    section = rows_ref.shape[1] // 3
    half = here()[0] if mine else 1 - here()[0]
    for side in range(HALF):
        made = []
        for part in range(3):
            at = pl.ds(pl.multiple_of(part * section + half * (HALF * DK) + side * DK, DK), DK)
            slot = side * 3 + part
            extend(ext_ref, slot, halo_ref[:, at], rows_ref[:, at])
            conv = convolve(ext_ref, slot, weight_ref[:, at], tokens)
            active = conv * (0.5 + 0.5 * jnp.tanh(0.5 * conv))
            if part < 2:
                active = active * lax.rsqrt(
                    jnp.sum(active * active, axis=1, keepdims=True) + 1e-06
                )
            made.append(active)
        query, key, value = made
        column = picker(column_ref, half, side)
        value = value.astype(BF).astype(F32)
        right = jnp.concatenate([(value * column(0)).astype(BF), (value * column(1)).astype(BF)], axis=1)
        both = dot(key.astype(BF), right, (0, 0)).astype(BF)
        element_ref[side, 0:DK] = both[:, :DK]
        element_ref[side, DK : 2 * DK] = both[:, DK:]
        upstream = u_ref[:, pl.ds(pl.multiple_of(half * (HALF * DK) + side * DK, DK), DK)].astype(F32)
        right = jnp.concatenate(
            [(upstream * column(2)).astype(BF), (upstream * column(3)).astype(BF)], axis=1
        )
        both = dot(query.astype(BF), right, (0, 0)).astype(BF)
        element_ref[side, 2 * DK : 3 * DK] = both[:, :DK]
        element_ref[side, 3 * DK : 4 * DK] = both[:, DK:]


def compose_kernel(own_ref, other_ref, own_coef_ref, other_coef_ref, out_ref):
    core = here()[0]
    first_core = core == 0
    heads = own_coef_ref.shape[0] // 3
    for j in range(own_ref.shape[0]):
        head = core * HALF + j

        def coef(which):
            mine = own_coef_ref[pl.ds(which * heads + head, 1), :]
            theirs = other_coef_ref[pl.ds(which * heads + head, 1), :]
            return jnp.where(first_core, mine, theirs), jnp.where(first_core, theirs, mine)

        def matrix(which):
            at = slice(which * DK, (which + 1) * DK)
            mine = own_ref[j, at].astype(F32)
            theirs = other_ref[j, at].astype(F32)
            return jnp.where(first_core, mine, theirs), jnp.where(first_core, theirs, mine)

        forget_a, forget_b = coef(0)
        carry_a, carry_b = coef(1)
        moment_a, moment_b = coef(2)
        memory_a, memory_b = matrix(0)
        state_a, state_b = matrix(1)
        recall_a, recall_b = matrix(2)
        direct_a, direct_b = matrix(3)
        joined = (
            forget_b * memory_a + carry_b * state_a + memory_b,
            moment_b * state_a + state_b,
            forget_a * recall_b + recall_a,
            carry_a * recall_b + moment_a * direct_b + direct_a,
        )
        scalars = []
        for value in (
            forget_a * forget_b,
            forget_b * carry_a + carry_b * moment_a,
            moment_a * moment_b,
        ):
            for term in range(3):
                kept = value.astype(BF).astype(F32)
                scalars.append(kept)
                value = value - kept
        scalars.append(jnp.zeros((EXTRA - len(scalars), DK), F32))
        tail = jnp.concatenate(scalars, axis=0).astype(BF)
        for half in range(2):
            for which, full in enumerate(joined):
                out_ref[2 * j + half, which * 64 : (which + 1) * 64] = full[
                    half * 64 : (half + 1) * 64
                ].astype(BF)
            out_ref[2 * j + half, 256:PIECE] = tail


def scan_kernel(got_ref, start_ref, out_ref):
    count = got_ref.shape[0]

    def coefs(c):
        rows = got_ref[c, 256:PIECE].astype(F32)
        return tuple(
            (rows[3 * i : 3 * i + 1] + rows[3 * i + 1 : 3 * i + 2]) + rows[3 * i + 2 : 3 * i + 3]
            for i in range(3)
        )

    scalars = [coefs(c) for c in range(count)]
    memory = start_ref[pl.ds(pl.multiple_of(here()[2] * 64, 64), 64), :]
    state = jnp.zeros_like(memory)
    for c in range(count):
        out_ref[c, 0:64] = memory.astype(BF)
        out_ref[c, 64:128] = state.astype(BF)
        forget, carry, moment = scalars[c]
        memory = forget * memory + carry * state + got_ref[c, 0:64].astype(F32)
        state = moment * state + got_ref[c, 64:128].astype(F32)
    memory = jnp.zeros_like(state)
    state = jnp.zeros_like(state)
    for c in reversed(range(count)):
        out_ref[c, 128:192] = memory.astype(BF)
        out_ref[c, 192:256] = state.astype(BF)
        forget, carry, moment = scalars[c]
        state = carry * memory + moment * state + got_ref[c, 192:256].astype(F32)
        memory = forget * memory + got_ref[c, 128:192].astype(F32)
    for c in range(count):
        rows = memory[8 * (c % 8) : 8 * (c % 8) + 8]
        high = rows.astype(BF).astype(F32)
        out_ref[c, 256:PIECE] = jnp.concatenate([high, rows - high], axis=0).astype(BF)


def spread_kernel(
    got_ref, own_ref, other_ref, own_coef_ref, other_coef_ref, keep_ref, send_ref
):
    core, side, _ = here()
    first_core = core == 0
    heads = own_coef_ref.shape[0] // 3
    for j in range(own_ref.shape[0]):
        head = core * HALF + j

        def coef(which):
            mine = own_coef_ref[pl.ds(which * heads + head, 1), :]
            theirs = other_coef_ref[pl.ds(which * heads + head, 1), :]
            return jnp.where(first_core, mine, theirs), jnp.where(first_core, theirs, mine)

        def local(which):
            at = slice(which * DK, (which + 1) * DK)
            mine = own_ref[j, at].astype(F32)
            theirs = other_ref[j, at].astype(F32)
            return jnp.where(first_core, mine, theirs), jnp.where(first_core, theirs, mine)

        def entering(which):
            at = slice(which * 64, (which + 1) * 64)
            return jnp.concatenate([got_ref[2 * j, at], got_ref[2 * j + 1, at]], axis=0).astype(F32)

        forget_a, forget_b = coef(0)
        carry_a, carry_b = coef(1)
        moment_a, moment_b = coef(2)
        memory, state = entering(0), entering(1)
        memory_end, state_end = entering(2), entering(3)
        one = (
            memory,
            state,
            forget_b * memory_end + local(2)[1],
            carry_b * memory_end + moment_b * state_end + local(3)[1],
        )
        two = (
            forget_a * memory + carry_a * state + local(0)[0],
            moment_a * state + local(1)[0],
            memory_end,
            state_end,
        )
        for which in range(4):
            at = slice(which * DK, (which + 1) * DK)
            keep_ref[j, at] = jnp.where(first_core, one[which], two[which]).astype(BF)
            send_ref[j, at] = jnp.where(first_core, two[which], one[which]).astype(BF)
        start = got_ref[2 * j + side, 256:PIECE]
        keep_ref[j, 4 * DK :] = start
        send_ref[j, 4 * DK :] = start


def inner_kernel(
    q_ref, k_ref, v_ref, u_ref, halo_ref, weight_ref, coupling_ref, out_ref, read_ref, ext_ref
):
    tokens, width = q_ref.shape
    section = halo_ref.shape[1] // 3
    block = pl.program_id(0)
    for side in range(width // DK):
        cols = slice(side * DK, (side + 1) * DK)
        made, slopes, units = [], [], []
        for part, ref in enumerate((q_ref, k_ref, v_ref)):
            at = pl.ds(pl.multiple_of(part * section + block * width + side * DK, DK), DK)
            slot = side * 3 + part
            extend(ext_ref, slot, halo_ref[:, at], ref[:, cols])
            conv = convolve(ext_ref, slot, weight_ref[:, at], tokens)
            gate = 0.5 + 0.5 * jnp.tanh(0.5 * conv)
            active = conv * gate
            slope = gate * (1.0 + conv * (1.0 - gate))
            slopes.append(slope)
            if part < 2:
                scale = lax.rsqrt(jnp.sum(active * active, axis=1, keepdims=True) + 1e-06)
                active = active * scale
                slope = slope * scale
                slopes[part] = slope
                units.append(active)
            active = active.astype(BF)
            made.append(active)
            out_ref[0, part, :, cols] = active
            out_ref[0, 4 + part, :, cols] = slope.astype(BF)
            out_ref[0, 10 + part, :, cols] = ref[:, cols]
        query, key, value = made
        upstream = u_ref[:, cols]
        out_ref[0, 3, :, cols] = upstream
        coupling = coupling_ref[side]
        scores = (dot(query, key, (1, 1)) * coupling).astype(BF)
        sense = (dot(upstream, value, (1, 1)) * coupling).astype(BF)
        grads = (
            dot(sense, key, (1, 0)),
            dot(sense, query, (0, 0)),
            dot(scores, upstream, (0, 0)),
        )
        for part, grad in enumerate(grads):
            if part < 2:
                unit = units[part]
                grad = grad - unit * jnp.sum(unit * grad, axis=1, keepdims=True)
            out_ref[0, 7 + part, :, cols] = (grad * slopes[part]).astype(BF)
        read_ref[0, 0, :, cols] = query
        read_ref[0, 1, :, cols] = dot(scores, value, (1, 0)).astype(BF)


def picker(column_ref, group, side):
    values = column_ref[group]
    return lambda which: values[:, which * SIDES + side : which * SIDES + side + 1]


def along_rows(left, pair):
    return dot(left, pair[:DK], (1, 0)), dot(left, pair[DK:], (1, 0))


def along_lanes(left, pair):
    both = dot(left, pair, (1, 1))
    return both[:, :DK], both[:, DK:]


def sense_kernel(
    mine, in_ref, halo_ref, weight_ref, column_ref, state_ref, *refs
):
    conv_ref, rim_ref, tap_ref, start_ref, pad_ref, ext_ref = refs[-6:]
    tokens = in_ref.shape[2]
    width = in_ref.shape[3]
    section = halo_ref.shape[1] // 3
    core = here()[0]
    block = core if mine else 1 - core
    if len(refs) > 6:
        rim_ref[0] = refs[0][1]
    else:
        rim_ref[0] = jnp.zeros(rim_ref.shape[1:], BF)

    pad_ref[0:8] = jnp.zeros((8, pad_ref.shape[1]), F32)
    pad_ref[8 + tokens :] = jnp.zeros((8, pad_ref.shape[1]), F32)

    for side in range(width // DK):
        cols = slice(side * DK, (side + 1) * DK)
        query, key, value, upstream = (in_ref[block, i, :, cols] for i in range(4))
        column = picker(column_ref, block, side)
        memory_col, tail_col, forget_col, carry_col = (column(i) for i in range(4))
        start = state_ref[side, 4 * DK :].astype(F32)
        start = start[0:8] + start[8:16]
        start_ref[4 * side : 4 * side + 4] = jnp.where(core == 0, start[0:4], start[4:8])
        forward, adjoint = state_ref[side, : 2 * DK], state_ref[side, 2 * DK : 4 * DK]
        grads = []
        a, b = along_lanes(upstream, forward)
        grads.append(forget_col * a + carry_col * b)
        a, b = along_lanes(value, adjoint)
        grads.append(memory_col * a + tail_col * b)
        a, b = along_rows(key, adjoint)
        grads.append(memory_col * a + tail_col * b)
        rims = []
        for part in range(3):
            grad = grads[part]
            if part < 2:
                unit = (query, key)[part].astype(F32)
                grad = grad - unit * jnp.sum(unit * grad, axis=1, keepdims=True)
            grad = grad * in_ref[block, 4 + part, :, cols].astype(F32)
            grad = grad + in_ref[block, 7 + part, :, cols].astype(F32)
            slot = side * 3 + part
            conv_ref[0, slot] = grad.astype(BF)
            there = slice(slot * DK, (slot + 1) * DK)
            pad_ref[8 : 8 + tokens, there] = grad
            at = pl.ds(pl.multiple_of(part * section + block * width + side * DK, DK), DK)
            extend(ext_ref, slot, halo_ref[:, at], in_ref[block, 10 + part, :, cols])
            rows = ext_ref[:, there]
            weights = weight_ref[:, at]
            rim = None
            for tap in range(4):
                moved = pad_ref[3 - tap : 3 - tap + 8 + tokens, there]
                slot_row = 12 * side + 4 * part + tap
                tap_ref[slot_row : slot_row + 1, :] = jnp.sum(moved * rows, axis=0, keepdims=True)
                lead = moved[0:8] * weights[tap : tap + 1]
                rim = lead if rim is None else rim + lead
            rims.append(rim[5:8])
        rims.append(jnp.zeros((7, DK), F32))
        rim_ref[1, :, cols] = jnp.concatenate(rims, axis=0).astype(BF)


def readout_kernel(
    place_ref, read_ref, column_ref, own_ref, other_ref, output_ref
):
    width = read_ref.shape[3]
    owned = (pl.program_id(0) // (pl.num_programs(0) // 2)) == place_ref[0]
    for side in range(width // DK):
        cols = slice(side * DK, (side + 1) * DK)
        column = picker(column_ref, 0, side)
        states = jnp.where(owned, own_ref[side], other_ref[side])
        from_memory, from_moment = along_rows(read_ref[0, 0, :, cols], states)
        readout = read_ref[0, 1, :, cols].astype(F32) + column(2) * from_memory + column(3) * from_moment
        output_ref[:, cols] = readout.astype(BF)


def unroll_kernel(
    place_ref, conv_own_ref, conv_other_ref, weight_ref, rim_own_ref, rim_other_ref, grad_ref, pad_ref
):
    tokens = conv_own_ref.shape[2]
    width = conv_own_ref.shape[1] // 3 * DK
    section = weight_ref.shape[1] // 3
    block = pl.program_id(0)
    owned = (block // (pl.num_programs(0) // 2)) == place_ref[0]

    @pl.when(block == 0)
    def _():
        pad_ref[tokens:] = jnp.zeros((8, pad_ref.shape[1]), F32)

    for side in range(width // DK):
        cols = slice(side * DK, (side + 1) * DK)
        rims = jnp.where(owned, rim_own_ref[0, :, cols], rim_other_ref[0, :, cols]).astype(F32)
        for part in range(3):
            at = pl.ds(pl.multiple_of(part * section + block * width + side * DK, DK), DK)
            slot = side * 3 + part
            there = slice(slot * DK, (slot + 1) * DK)
            grad = jnp.where(owned, conv_own_ref[0, slot], conv_other_ref[0, slot]).astype(F32)
            weights = weight_ref[:, at]
            pad_ref[0:tokens, there] = grad
            total = grad * weights[3:4]
            for tap in range(3):
                total = total + pad_ref[3 - tap : 3 - tap + tokens, there] * weights[tap : tap + 1]
            rim = rims[3 * part : 3 * part + 3]
            total = jnp.concatenate([total[: tokens - 3], total[tokens - 3 :] + rim], axis=0)
            grad_ref[:, at] = total.astype(BF)


def pack_kernel(own_ref, far_ref, out_ref):
    value = (own_ref[...] + far_ref[...]).astype(BF)
    for i in range(out_ref.shape[0]):
        out_ref[i] = value


def fold_kernel(pieces_ref, own_ref, other_ref, out_ref):
    total = pieces_ref[0].astype(F32)
    for i in range(1, pieces_ref.shape[0]):
        total = total + pieces_ref[i].astype(F32)
    own, other = own_ref[...], other_ref[...]
    first_core = here()[0] == 0
    value = jnp.concatenate(
        [total, jnp.where(first_core, own, other), jnp.where(first_core, other, own)], axis=0
    ).astype(BF)
    for i in range(out_ref.shape[0]):
        out_ref[i] = value


def sum_kernel(pieces_ref, out_ref):
    total = pieces_ref[0].astype(F32)
    for i in range(1, pieces_ref.shape[0]):
        total = total + pieces_ref[i].astype(F32)
    out_ref[...] = total


def assemble_kernel(own_ref, other_ref, out_ref, start_ref):
    section = out_ref.shape[1] // 3
    core = here()[0]
    for h in range(section // DK):
        first = 12 * HALF + 4 * h
        start_ref[h] = own_ref[first : first + 4]
    for h in range(section // DK):
        for part in range(3):
            first = 12 * (h % HALF) + 4 * part
            rows = slice(first, first + 4)
            at = part * section + h * DK
            out_ref[:, at : at + DK] = jnp.where(
                core == h // HALF, own_ref[rows], other_ref[rows]
            )


RESIDENT = pl.BlockSpec(memory_space=pltpu.VMEM)


def whole(*shape):
    return pl.BlockSpec(shape, lambda *_: (0,) * len(shape))


def local(projected, conv_weight, initial_memory, log_forget, log_momentum, learn_rate, cotangent):
    rows = projected[0]
    upstream = cotangent[0]
    tokens, channels = rows.shape
    heads = initial_memory.shape[0]
    width = SIDES * DK
    blocks = heads * DK // width
    count = lax.axis_size("seq")
    mine = lax.axis_index("seq")
    core = lax.rem(mine, 2)
    place = core.astype(jnp.int32).reshape(1)
    gates = jnp.concatenate([log_forget[0], log_momentum[0], learn_rate[0]], axis=0)
    gates, place = lax.optimization_barrier((gates, place))
    pairs = [(i, i ^ 1) for i in range(count)]
    groups = [[2 * c + k for c in range(count // 2)] for k in range(2)]

    rim = lax.ppermute(rows[tokens - 16 :], "seq", [(i, i + 1) for i in range(count - 1)])
    shape = jax.ShapeDtypeStruct
    columns, coefs, cums = pl.pallas_call(
        tables_kernel,
        out_shape=(
            shape((heads // SIDES, tokens, 4 * SIDES), F32),
            shape((3 * heads, DK), F32),
            shape((2 * heads, tokens), F32),
        ),
        compiler_params=SHARED,
        name="tables",
        cost_estimate=pl.CostEstimate(flops=2000000000, transcendentals=0, bytes_accessed=7200000),
    )(gates)
    other_coefs = lax.ppermute(coefs, "seq", pairs)

    def elements(mine):
        return pl.pallas_call(
            functools.partial(element_kernel, mine),
            out_shape=shape((HALF, 4 * DK, DK), BF),
            in_specs=[RESIDENT] * 5,
                out_specs=RESIDENT,
                scratch_shapes=[pltpu.VMEM((tokens + 8, 3 * HALF * DK), F32)],
            compiler_params=SHARED,
            name="elements",
            cost_estimate=pl.CostEstimate(flops=3400000000, transcendentals=0, bytes_accessed=12240000),
        )(rows, upstream, rim, conv_weight, columns)

    sent = elements(False)
    other = lax.ppermute(sent, "seq", pairs)
    own = elements(True)

    payload = pl.pallas_call(
        compose_kernel,
        out_shape=shape((CHIPS, PIECE, DK), BF),
        in_specs=[RESIDENT] * 4,
            out_specs=RESIDENT,
        compiler_params=SHARED,
        name="compose",
        cost_estimate=pl.CostEstimate(flops=1200000000, transcendentals=0, bytes_accessed=4320000),
    )(own, other, coefs, other_coefs)
    payload, cums = lax.optimization_barrier((payload, cums))
    got = lax.all_to_all(payload, "seq", 0, 0, axis_index_groups=groups)

    coupling = pl.pallas_call(
        couple_kernel,
        out_shape=shape((heads, tokens, tokens), F32),
        compiler_params=SHARED,
        name="couple",
        cost_estimate=pl.CostEstimate(flops=3500000000, transcendentals=0, bytes_accessed=12600000),
    )(gates, cums)

    def block_at(part):
        return pl.BlockSpec((tokens, width), lambda i: (0, part * blocks + i))

    inner, inside = pl.pallas_call(
        inner_kernel,
        out_shape=(
            shape((blocks, 13, tokens, width), BF),
            shape((blocks, 2, tokens, width), BF),
        ),
        grid=(blocks,),
        in_specs=[
            block_at(0),
            block_at(1),
            block_at(2),
            block_at(0),
            whole(16, channels),
            whole(4, channels),
            pl.BlockSpec((SIDES, tokens, tokens), lambda i: (i, 0, 0)),
        ],
        out_specs=(
            pl.BlockSpec((1, 13, tokens, width), lambda i: (i, 0, 0, 0)),
            pl.BlockSpec((1, 2, tokens, width), lambda i: (i, 0, 0, 0)),
        ),
        scratch_shapes=[pltpu.VMEM((tokens + 8, 3 * SIDES * DK), F32)],
        compiler_params=PARAMS,
        name="inner",
        cost_estimate=pl.CostEstimate(flops=8000000000, transcendentals=0, bytes_accessed=28800000),
    )(rows, rows, rows, upstream, rim, conv_weight, coupling)

    got, inner, inside = lax.optimization_barrier((got, inner, inside))
    back = pl.pallas_call(
        scan_kernel,
        out_shape=shape((CHIPS, PIECE, DK), BF),
        in_specs=[RESIDENT] * 2,
            out_specs=RESIDENT,
        compiler_params=SHARED,
        name="scan",
        cost_estimate=pl.CostEstimate(flops=400000000, transcendentals=0, bytes_accessed=1440000),
    )(got, initial_memory.reshape(heads * DK, DK))
    states = lax.all_to_all(back, "seq", 0, 0, axis_index_groups=groups)

    kept, passed = pl.pallas_call(
        spread_kernel,
        out_shape=(
            shape((HALF, 4 * DK + EXTRA, DK), BF),
            shape((HALF, 4 * DK + EXTRA, DK), BF),
        ),
        in_specs=[RESIDENT] * 5,
            out_specs=(RESIDENT,) * 2,
        compiler_params=SHARED,
        name="spread",
        cost_estimate=pl.CostEstimate(flops=1300000000, transcendentals=0, bytes_accessed=4680000),
    )(states, own, other, coefs, other_coefs)
    received = lax.ppermute(passed, "seq", pairs)

    half_blocks = blocks // 2

    def sense(mine, state, *before):
        return pl.pallas_call(
            functools.partial(sense_kernel, mine),
            out_shape=(
                shape((half_blocks, 3 * SIDES, tokens, DK), BF),
                shape((2, 16, HALF * DK), BF),
                shape((12 * HALF, DK), F32),
                shape((4 * HALF, DK), F32),
            ),
            in_specs=[RESIDENT] * (5 + len(before)),
                out_specs=(RESIDENT,) * 4,
                scratch_shapes=[
                    pltpu.VMEM((tokens + 16, 3 * SIDES * DK), F32),
                    pltpu.VMEM((tokens + 8, 3 * SIDES * DK), F32),
                ],
            compiler_params=PARAMS,
            name="sense",
            cost_estimate=pl.CostEstimate(flops=3000000000, transcendentals=0, bytes_accessed=10800000),
        )(inner, rim, conv_weight, columns, state, *before)

    conv_own, edge, tap_own, start_own = sense(True, kept)
    conv_other, edge, tap_other, start_other = sense(False, received, edge)

    tap_far = lax.ppermute(tap_other, "seq", pairs)

    def ordered(one, two):
        return jnp.where(core == 0, one, two), jnp.where(core == 0, two, one)

    back_one = [(i + 1, i) for i in range(count - 1)]
    edge = lax.ppermute(edge, "seq", back_one)

    def own_at(i, b):
        return jnp.clip(i - b[0] * half_blocks, 0, half_blocks - 1)

    def other_at(i, b):
        return jnp.clip(i - (1 - b[0]) * half_blocks, 0, half_blocks - 1)

    def readouts(inside):
        return pl.pallas_call(
            readout_kernel,
            out_shape=shape((tokens, heads * DK), BF),
            grid_spec=pltpu.PrefetchScalarGridSpec(
                num_scalar_prefetch=1,
                grid=(blocks,),
                in_specs=[
                    pl.BlockSpec((1, 2, tokens, width), lambda i, b: (i, 0, 0, 0)),
                    pl.BlockSpec((1, tokens, 4 * SIDES), lambda i, b: (i, 0, 0)),
                    pl.BlockSpec((SIDES, 2 * DK, DK), lambda i, b: (own_at(i, b), 0, 0)),
                    pl.BlockSpec((SIDES, 2 * DK, DK), lambda i, b: (other_at(i, b), 0, 0)),
                ],
                out_specs=pl.BlockSpec((tokens, width), lambda i, b: (0, i)),
            ),
            compiler_params=PARAMS,
            name="readout",
            cost_estimate=pl.CostEstimate(flops=3000000000, transcendentals=0, bytes_accessed=10800000),
        )(place, inside, columns, kept, received)

    def unrolled(rim):
        return pl.pallas_call(
            unroll_kernel,
            out_shape=shape((tokens, channels), BF),
            grid_spec=pltpu.PrefetchScalarGridSpec(
                num_scalar_prefetch=1,
                grid=(blocks,),
                in_specs=[
                    pl.BlockSpec((1, 3 * SIDES, tokens, DK), lambda i, b: (own_at(i, b), 0, 0, 0)),
                    pl.BlockSpec((1, 3 * SIDES, tokens, DK), lambda i, b: (other_at(i, b), 0, 0, 0)),
                    whole(4, channels),
                    pl.BlockSpec((1, 16, width), lambda i, b: (1, 0, own_at(i, b))),
                    pl.BlockSpec((1, 16, width), lambda i, b: (0, 0, other_at(i, b))),
                ],
                out_specs=whole(tokens, channels),
                scratch_shapes=[pltpu.VMEM((tokens + 8, 3 * SIDES * DK), F32)],
            ),
            compiler_params=PARAMS,
            name="unroll",
            cost_estimate=pl.CostEstimate(flops=4000000000, transcendentals=0, bytes_accessed=14400000),
        )(place, conv_own, conv_other, conv_weight, rim, rim)

    dp = lax.axis_size("dp")
    tap_rows = 12 * HALF
    sum_rows = tap_rows + 4 * heads
    spread_taps = pl.pallas_call(
        pack_kernel,
        out_shape=shape((CHIPS, tap_rows, DK), BF),
        compiler_params=SHARED,
        name="pack",
        cost_estimate=pl.CostEstimate(flops=800000000, transcendentals=0, bytes_accessed=2880000),
    )(tap_own, tap_far)

    pieces = lax.all_to_all(spread_taps, "seq", 0, 0, axis_index_groups=groups)
    spread_sums = pl.pallas_call(
        fold_kernel,
        out_shape=shape((dp, sum_rows, DK), BF),
        in_specs=[RESIDENT] * 3,
            out_specs=RESIDENT,
        compiler_params=SHARED,
        name="fold",
        cost_estimate=pl.CostEstimate(flops=800000000, transcendentals=0, bytes_accessed=2880000),
    )(pieces, start_own, start_other)
    spread_sums, inside = lax.optimization_barrier((spread_sums, inside))
    pieces = lax.all_to_all(spread_sums, "dp", 0, 0)
    output = readouts(inside)
    edge, output = lax.optimization_barrier((edge, output))
    grad = unrolled(edge)
    pieces, output, grad = lax.optimization_barrier((pieces, output, grad))
    total = pl.pallas_call(
        sum_kernel,
        out_shape=shape((sum_rows, DK), F32),
        compiler_params=SHARED,
        name="total",
        cost_estimate=pl.CostEstimate(flops=800000000, transcendentals=0, bytes_accessed=2880000),
    )(pieces)
    total_far = lax.ppermute(total, "seq", pairs)
    taps, start_all = pl.pallas_call(
        assemble_kernel,
        out_shape=(shape((4, channels), F32), shape((heads, 4, DK), F32)),
        in_specs=[RESIDENT] * 2,
            out_specs=(RESIDENT,) * 2,
        compiler_params=SHARED,
        name="assemble",
        cost_estimate=pl.CostEstimate(flops=1000000000, transcendentals=0, bytes_accessed=3600000),
    )(total, total_far)
    return (output[None], grad[None], taps, start_all)


def solution(mesh):
    in_specs = (
        P("dp", "seq", None),
        P(),
        P(),
        P("dp", None, "seq"),
        P("dp", None, "seq"),
        P("dp", None, "seq"),
        P("dp", "seq", None),
    )
    out_specs = (P("dp", "seq", None), P("dp", "seq", None), P(), P(None, "seq", None))
    return jax.shard_map(local, mesh=mesh, in_specs=in_specs, out_specs=out_specs, check_vma=False)
```
